128 devices in a mesh: wide: 32 (over z, y, core), narrow: 4 (over x).
Axes of the slice: x: 4, y: 4, z: 4, core: 2. Of those that a mesh axis runs over, the one named last changes fastest.
Arguments:
- encoder_input: bfloat16 [32, 1024, 768], P('wide', 'narrow'), may hold values from -6 to 6
- seg_ids: int32 [32, 1024], P('wide'), may hold values from 0 to 6, as said below
- vis_slot: int32 [32, 1024], P('wide'), may hold values from 0 to 156, as said below
- restore_order: int32 [32, 4, 1568], P('wide', 'narrow'), may hold values from 0 to 1567, each once within a row
- enc_norm1_gain: bfloat16 [768], replicated, may hold values from 0.25 to 1.75
- enc_norm1_shift: bfloat16 [768], replicated, may hold values from -3 to 3
- enc_qkv_weight: bfloat16 [768, 2304], P('narrow'), may hold values from -0.21875 to 0.21875
- enc_qv_bias: bfloat16 [1536], replicated, may hold values from -3 to 3
- enc_proj_weight: bfloat16 [768, 768], P('narrow'), may hold values from -1.5 to 1.5
- enc_proj_bias: bfloat16 [768], replicated, may hold values from -3 to 3
- enc_norm2_gain: bfloat16 [768], replicated, may hold values from 0.25 to 1.75
- enc_norm2_shift: bfloat16 [768], replicated, may hold values from -3 to 3
- enc_fc1_weight: bfloat16 [768, 3072], P('narrow'), may hold values from -0.21875 to 0.21875
- enc_fc1_bias: bfloat16 [3072], replicated, may hold values from -3 to 3
- enc_fc2_weight: bfloat16 [3072, 768], P('narrow'), may hold values from -0.109375 to 0.109375
- enc_fc2_bias: bfloat16 [768], replicated, may hold values from -3 to 3
- to_dec_weight: bfloat16 [768, 384], replicated, may hold values from -0.21875 to 0.21875
- mask_token: bfloat16 [384], replicated, may hold values from -4 to 4
- dec_norm1_gain: bfloat16 [384], replicated, may hold values from 0.25 to 1.75
- dec_norm1_shift: bfloat16 [384], replicated, may hold values from -3 to 3
- dec_qkv_weight: bfloat16 [384, 1152], replicated, may hold values from -0.3125 to 0.3125
- dec_qv_bias: bfloat16 [768], replicated, may hold values from -3 to 3
- dec_proj_weight: bfloat16 [384, 384], replicated, may hold values from -6 to 6
- dec_proj_bias: bfloat16 [384], replicated, may hold values from -3 to 3
- dec_norm2_gain: bfloat16 [384], replicated, may hold values from 0.25 to 1.75
- dec_norm2_shift: bfloat16 [384], replicated, may hold values from -3 to 3
- dec_fc1_weight: bfloat16 [384, 1536], replicated, may hold values from -0.3125 to 0.3125
- dec_fc1_bias: bfloat16 [1536], replicated, may hold values from -3 to 3
- dec_fc2_weight: bfloat16 [1536, 384], replicated, may hold values from -0.15625 to 0.15625
- dec_fc2_bias: bfloat16 [384], replicated, may hold values from -3 to 3
- out_grad: bfloat16 [32, 4, 1568, 384], P('wide', 'narrow'), may hold values from -6 to 6
Outputs:
- dec_output: bfloat16 [32, 4, 1568, 384], P('wide', 'narrow')
- enc_input_grad: float32 [32, 1024, 768], P('wide', 'narrow')
- grad_enc_norm1_gain: float32 [768], replicated
- grad_enc_norm1_shift: float32 [768], replicated
- grad_enc_qkv_weight: float32 [768, 2304], replicated
- grad_enc_qv_bias: float32 [1536], replicated
- grad_enc_proj_weight: float32 [768, 768], replicated
- grad_enc_proj_bias: float32 [768], replicated
- grad_enc_norm2_gain: float32 [768], replicated
- grad_enc_norm2_shift: float32 [768], replicated
- grad_enc_fc1_weight: float32 [768, 3072], replicated
- grad_enc_fc1_bias: float32 [3072], replicated
- grad_enc_fc2_weight: float32 [3072, 768], replicated
- grad_enc_fc2_bias: float32 [768], replicated
- grad_to_dec_weight: float32 [768, 384], replicated
- grad_mask_token: float32 [384], replicated
- grad_dec_norm1_gain: float32 [384], replicated
- grad_dec_norm1_shift: float32 [384], replicated
- grad_dec_qkv_weight: float32 [384, 1152], replicated
- grad_dec_qv_bias: float32 [768], replicated
- grad_dec_proj_weight: float32 [384, 384], replicated
- grad_dec_proj_bias: float32 [384], replicated
- grad_dec_norm2_gain: float32 [384], replicated
- grad_dec_norm2_shift: float32 [384], replicated
- grad_dec_fc1_weight: float32 [384, 1536], replicated
- decoder_first_bias_grad: float32 [1536], replicated
- grad_dec_fc2_weight: float32 [1536, 384], replicated
- grad_dec_fc2_bias: float32 [384], replicated
The draws below stay inside these ranges and needn't reach their ends.
Inputs may be any that keep to these rules, and one draw needn't show every extreme that they name: `seg_ids`: in each row every clip 0 to 5 has exactly 157 positions and the remaining positions carry 6 (padding); each index of narrow (positions k * 256 to (k + 1) * 256 - 1 of a row) holds between 1 and 64 tokens of every clip 0 to 3, and in every row some index holds exactly 64 of one of them. `vis_slot`: within a row, the positions of one clip carry the slots 0 to 156, each once; padding positions carry 0. `restore_order`: each clip's row holds every number of 0 to 1567 once.
All inputs are finite; a program needn't handle non-finite values.
Results may differ from the reference program's by a relative error of at most 0.018.
Values may be sent and summed in bfloat16 or wider, within the bound.
No kernel may reach another device: no remote copies, remote signals or barrier semaphores. Data moves between devices by JAX's collectives and lax.ppermute only.
A program may use at most 384 MiB of HBM per device.

```python
import jax
import jax.numpy as jnp
from jax import lax

ENCODER_WIDTH = 768
HEADS = 12
HEAD_DIM = 64
FF = 3072
DD = 384
DHEADS = 6
DFF = 1536
VIS = 157
FULL = 1568
PACK = 6
ROW_LENGTH = 1024
CAP = 64
DCLIPS = 4
TOK_DEV = 256
PACKED_ROWS = 32


def packing(key):
    base = VIS // DCLIPS
    extra = VIS % DCLIPS
    shift_key, near_key, far_key, kept_key, spare_key, order_key = jax.random.split(key, 6)
    device = jnp.arange(DCLIPS)[None, :, None]
    clip = jnp.arange(PACK)[None, None, :]
    shift = jax.random.randint(shift_key, (PACKED_ROWS, 1, 1), 0, DCLIPS)
    counts = base + ((device - clip - shift) % DCLIPS < extra).astype(jnp.int32)
    first = jax.random.randint(near_key, (PACKED_ROWS, 1, 1), 0, DCLIPS)
    second = (first + jax.random.randint(far_key, (PACKED_ROWS, 1, 1), 1, DCLIPS)) % DCLIPS
    full_clip = jax.random.randint(kept_key, (PACKED_ROWS, 1, 1), 0, DCLIPS)
    spare_clip = jax.random.randint(spare_key, (PACKED_ROWS, 1, 1), DCLIPS, PACK)
    at_one = jnp.logical_and(device == first, clip == full_clip)
    move = CAP - jnp.sum(jnp.where(at_one, counts, 0), axis=(1, 2), keepdims=True)
    pattern = at_one.astype(jnp.int32) - jnp.logical_and(device == first, clip == spare_clip).astype(jnp.int32) - jnp.logical_and(device == second, clip == full_clip).astype(jnp.int32) + jnp.logical_and(device == second, clip == spare_clip).astype(jnp.int32)
    counts = counts + move * pattern
    padding = TOK_DEV - jnp.sum(counts, axis=-1, keepdims=True)
    every = jnp.concatenate([counts, padding], axis=-1)
    bounds = jnp.cumsum(every, axis=-1)
    position = jnp.arange(TOK_DEV)
    labels = jnp.sum((bounds[:, :, None, :] <= position[None, None, :, None]).astype(jnp.int32), axis=-1)
    orders = jax.vmap(lambda member: jax.random.permutation(member, TOK_DEV))(jax.random.split(order_key, PACKED_ROWS * DCLIPS)).reshape(PACKED_ROWS, DCLIPS, TOK_DEV)
    permuted_rows = jnp.take_along_axis(labels, orders, axis=-1)
    return permuted_rows.reshape(PACKED_ROWS, ROW_LENGTH).astype(jnp.int32)


def draw_seg_ids(key, part):
    segments = packing(key)
    return segments


def draw_vis_slot(key, part):
    segments = packing(key)
    key = jax.random.fold_in(key, 7)
    clip_index = jnp.arange(PACK + 1)
    member_of = (segments[:, :, None] == clip_index[None, None, :]).astype(jnp.int32)
    before = jnp.cumsum(member_of, axis=1) - member_of
    ranks = jnp.sum(before * member_of, axis=-1)
    slot_perms = jax.vmap(lambda member: jax.random.permutation(member, VIS))(jax.random.split(key, PACKED_ROWS * PACK)).reshape(PACKED_ROWS, PACK * VIS)
    index = jnp.minimum(segments, PACK - 1) * VIS + jnp.minimum(ranks, VIS - 1)
    picked = jnp.take_along_axis(slot_perms, index, axis=1)
    return jnp.where(segments < PACK, picked, 0).astype(jnp.int32)


def block_scale(stream_key, extent, shards, least, largest):
    def one(dim, shards_of):
        heights = jax.random.uniform(jax.random.fold_in(jax.random.fold_in(stream_key, 6), dim), (shards_of,), jnp.float32, least / len(shards), largest / len(shards))
        return jnp.repeat(jnp.exp(heights), extent[dim] // shards_of).reshape((-1,) + (1,) * (len(extent) - dim - 1))

    loudness = one(*shards[0])
    for cut in shards[1:]:
        loudness = loudness * one(*cut)
    return loudness


def noise(rng, dims, deviation, reach, cuts=(), dtype=jnp.bfloat16):
    loudness = block_scale(rng, dims, cuts, -0.22, 0.18) if cuts else 1.0
    entries = jax.random.normal(rng, dims, jnp.float32) * deviation * loudness
    return jnp.minimum(jnp.maximum(entries, -reach), reach).astype(dtype)


def setup_inputs(seed: int = 0) -> dict:
    arg_keys = jax.random.split(jax.random.key(seed), 32)
    return {
        "encoder_input": noise(arg_keys[0], (PACKED_ROWS, ROW_LENGTH, ENCODER_WIDTH), 1.0, 6.0, ((0, 32), (1, 4))),
        "seg_ids": draw_seg_ids(jax.random.fold_in(arg_keys[31], 71), 0),
        "vis_slot": draw_vis_slot(jax.random.fold_in(arg_keys[31], 71), 0),
        "restore_order": jax.vmap(lambda own: jax.random.permutation(own, FULL))(jax.random.split(arg_keys[3], PACKED_ROWS * DCLIPS)).reshape((PACKED_ROWS, DCLIPS, FULL)).astype(jnp.int32),
        "enc_norm1_gain": jnp.clip(1.0 + 0.15 * jax.random.normal(arg_keys[4], (ENCODER_WIDTH,), jnp.float32), 0.25, 1.75).astype(jnp.bfloat16),
        "enc_norm1_shift": noise(arg_keys[5], (ENCODER_WIDTH,), 0.5, 3.0),
        "enc_qkv_weight": noise(arg_keys[6], (ENCODER_WIDTH, 3 * ENCODER_WIDTH), ENCODER_WIDTH ** -0.5, 0.21875, ((0, 4),)),
        "enc_qv_bias": noise(arg_keys[7], (2 * ENCODER_WIDTH,), 0.5, 3.0),
        "enc_proj_weight": noise(arg_keys[8], (ENCODER_WIDTH, ENCODER_WIDTH), (HEAD_DIM // 4) ** -0.5, 1.5, ((0, 4),)),
        "enc_proj_bias": noise(arg_keys[9], (ENCODER_WIDTH,), 0.5, 3.0),
        "enc_norm2_gain": jnp.clip(1.0 + 0.15 * jax.random.normal(arg_keys[10], (ENCODER_WIDTH,), jnp.float32), 0.25, 1.75).astype(jnp.bfloat16),
        "enc_norm2_shift": noise(arg_keys[11], (ENCODER_WIDTH,), 0.5, 3.0),
        "enc_fc1_weight": noise(arg_keys[12], (ENCODER_WIDTH, FF), ENCODER_WIDTH ** -0.5, 0.21875, ((0, 4),)),
        "enc_fc1_bias": noise(arg_keys[13], (FF,), 0.5, 3.0),
        "enc_fc2_weight": noise(arg_keys[14], (FF, ENCODER_WIDTH), FF ** -0.5, 0.109375, ((0, 4),)),
        "enc_fc2_bias": noise(arg_keys[15], (ENCODER_WIDTH,), 0.5, 3.0),
        "to_dec_weight": noise(arg_keys[16], (ENCODER_WIDTH, DD), ENCODER_WIDTH ** -0.5, 0.21875),
        "mask_token": noise(arg_keys[17], (DD,), 1.0, 4.0),
        "dec_norm1_gain": jnp.clip(1.0 + 0.15 * jax.random.normal(arg_keys[18], (DD,), jnp.float32), 0.25, 1.75).astype(jnp.bfloat16),
        "dec_norm1_shift": noise(arg_keys[19], (DD,), 0.5, 3.0),
        "dec_qkv_weight": noise(arg_keys[20], (DD, 3 * DD), DD ** -0.5, 0.3125),
        "dec_qv_bias": noise(arg_keys[21], (2 * DD,), 0.5, 3.0),
        "dec_proj_weight": noise(arg_keys[22], (DD, DD), 1 ** -0.5, 6.0),
        "dec_proj_bias": noise(arg_keys[23], (DD,), 0.5, 3.0),
        "dec_norm2_gain": jnp.clip(1.0 + 0.15 * jax.random.normal(arg_keys[24], (DD,), jnp.float32), 0.25, 1.75).astype(jnp.bfloat16),
        "dec_norm2_shift": noise(arg_keys[25], (DD,), 0.5, 3.0),
        "dec_fc1_weight": noise(arg_keys[26], (DD, DFF), DD ** -0.5, 0.3125),
        "dec_fc1_bias": noise(arg_keys[27], (DFF,), 0.5, 3.0),
        "dec_fc2_weight": noise(arg_keys[28], (DFF, DD), DFF ** -0.5, 0.15625),
        "dec_fc2_bias": noise(arg_keys[29], (DD,), 0.5, 3.0),
        "out_grad": noise(arg_keys[30], (PACKED_ROWS, DCLIPS, FULL, DD), 1.0, 6.0, ((0, 32), (1, 4))),
    }


HIGH = lax.Precision.HIGHEST
NORM_EPS = 1e-06

@jax.custom_vjp
def low(v):
    return lax.optimization_barrier(v.astype(jnp.bfloat16)).astype(jnp.float32)

@jax.custom_vjp
def low_back(v):
    return v

def low_keep(v):
    return (low(v), None)

def low_pass(kept, grad):
    return (grad,)

def back_keep(v):
    return (v, None)

def back_low(kept, grad):
    return (low(grad),)
low.defvjp(low_keep, low_pass)
low_back.defvjp(back_keep, back_low)

def layer_norm(values, gain_vec, offset_vec):
    average = lax.optimization_barrier(jnp.mean(values, axis=-1, keepdims=True))
    centred = values - average
    variance = lax.optimization_barrier(jnp.mean(centred * centred, axis=-1, keepdims=True))
    return centred * lax.rsqrt(variance + NORM_EPS) * gain_vec + offset_vec

def dense(inputs, weight):
    return jnp.einsum('...k,kn->...n', inputs, weight, precision=HIGH)

def sincos_table(count_pos, count_col):
    position = jnp.arange(count_pos).astype(jnp.float32)[:, None]
    column = jnp.arange(count_col)
    exponent = (2 * (column // 2)).astype(jnp.float32) / count_col
    angles = position / jnp.power(10000.0, exponent)[None, :]
    return jnp.where(column[None, :] % 2 == 0, jnp.sin(angles), jnp.cos(angles))

def softmax_rows(scores):
    row_peak = lax.optimization_barrier(jnp.max(scores, axis=-1, keepdims=True))
    exp_scores = jnp.exp(scores - row_peak)
    return exp_scores / lax.optimization_barrier(jnp.sum(exp_scores, axis=-1, keepdims=True))

def attention(queries, key_rows, value_rows, allowed, head_count):
    head_dim = queries.shape[-1] // head_count
    query_heads = queries.reshape(queries.shape[0], head_count, head_dim)
    key_heads = key_rows.reshape(key_rows.shape[0], head_count, head_dim)
    value_heads = value_rows.reshape(value_rows.shape[0], head_count, head_dim)
    scores = low_back(jnp.einsum('qhe,khe->hqk', query_heads, key_heads, precision=HIGH))
    if allowed is not None:
        scores = jnp.where(allowed[None], scores, -1e+30)
    probs_low = low(softmax_rows(scores))
    attended = jnp.einsum('hqk,khe->qhe', probs_low, value_heads, precision=HIGH)
    return attended.reshape(queries.shape[0], head_count * head_dim)

def block(hidden, params, head_count, attend):
    norm1_gain, norm1_shift, qkv_weight, qv_bias, proj_weight, proj_bias, norm2_gain, norm2_shift, fc1_weight, fc1_bias, fc2_weight, fc2_bias = params
    width_all = hidden.shape[-1]
    q_scale = (width_all // head_count) ** (-0.5)
    normed_one = low(layer_norm(hidden, norm1_gain, norm1_shift))
    packed = dense(normed_one, qkv_weight)
    queries = low(low_back((packed[..., :width_all] + qv_bias[:width_all]) * q_scale))
    key_rows = low(low_back(packed[..., width_all:2 * width_all]))
    value_rows = low(low_back(packed[..., 2 * width_all:] + qv_bias[width_all:]))
    attended = low(low_back(attend(queries, key_rows, value_rows)))
    after_attn = hidden + low_back(dense(attended, proj_weight) + proj_bias)
    normed_two = low(layer_norm(after_attn, norm2_gain, norm2_shift))
    pre_act = low_back(dense(normed_two, fc1_weight) + fc1_bias)
    activated = low(jax.nn.gelu(pre_act, approximate=False))
    return after_attn + low_back(dense(activated, fc2_weight) + fc2_bias)

def row_forward(params, enc_row, seg_row, slot_row, restore_row):
    enc_params = params[0:12]
    to_dec = params[12]
    mask_vec = params[13]
    dec_params = params[14:26]
    allowed = seg_row[:, None] == seg_row[None, :]

    def enc_attend(queries, key_rows, value_rows):
        return attention(queries, key_rows, value_rows, allowed, HEADS)
    enc_out = block(enc_row, enc_params, HEADS, enc_attend)
    reduced = low(low_back(dense(low(enc_out), to_dec)))
    clip_ids = jnp.arange(DCLIPS).astype(jnp.int32)
    matches = jnp.logical_and(seg_row[None, None, :] == clip_ids[:, None, None], slot_row[None, None, :] == restore_row[:, :, None])
    placed = jnp.einsum('cfl,ld->cfd', matches.astype(jnp.float32), reduced, precision=HIGH)
    is_mask = (restore_row >= VIS)[:, :, None]
    grid = placed + jnp.where(is_mask, mask_vec, 0.0) + sincos_table(FULL, DD)[None]

    def per_clip(triple):
        return attention(triple[0], triple[1], triple[2], None, DHEADS)

    def dec_attend(queries, key_rows, value_rows):
        return lax.map(jax.checkpoint(per_clip), (queries, key_rows, value_rows))
    return block(grid, dec_params, DHEADS, dec_attend)

def reference(encoder_input, seg_ids, vis_slot, restore_order, enc_norm1_gain, enc_norm1_shift, enc_qkv_weight, enc_qv_bias, enc_proj_weight, enc_proj_bias, enc_norm2_gain, enc_norm2_shift, enc_fc1_weight, enc_fc1_bias, enc_fc2_weight, enc_fc2_bias, to_dec_weight, mask_token, dec_norm1_gain, dec_norm1_shift, dec_qkv_weight, dec_qv_bias, dec_proj_weight, dec_proj_bias, dec_norm2_gain, dec_norm2_shift, dec_fc1_weight, dec_fc1_bias, dec_fc2_weight, dec_fc2_bias, out_grad):
    weights = tuple((member.astype(jnp.float32) for member in (enc_norm1_gain, enc_norm1_shift, enc_qkv_weight, enc_qv_bias, enc_proj_weight, enc_proj_bias, enc_norm2_gain, enc_norm2_shift, enc_fc1_weight, enc_fc1_bias, enc_fc2_weight, enc_fc2_bias, to_dec_weight, mask_token, dec_norm1_gain, dec_norm1_shift, dec_qkv_weight, dec_qv_bias, dec_proj_weight, dec_proj_bias, dec_norm2_gain, dec_norm2_shift, dec_fc1_weight, dec_fc1_bias, dec_fc2_weight, dec_fc2_bias)))

    def forward(params, enc_values):

        def one_row(row_inputs):
            return row_forward(params, *row_inputs)
        return lax.map(jax.checkpoint(one_row), (enc_values, seg_ids, vis_slot, restore_order))
    outputs, pullback = jax.vjp(forward, weights, encoder_input.astype(jnp.float32))
    weight_grads, input_grad = pullback(out_grad.astype(jnp.float32))
    g_enc_a, g_enc_b, g_enc_c, g_enc_d, g_enc_e, g_enc_f, g_enc_g, g_enc_h, g_enc_i, g_enc_j, g_enc_k, g_enc_l, g_to_dec, g_mask_tok, g_dec_a, g_dec_b, g_dec_c, g_dec_d, g_dec_e, g_dec_f, g_dec_g, g_dec_h, g_dec_i, g_dec_j, g_dec_k, g_dec_l = weight_grads
    return (outputs.astype(jnp.bfloat16), input_grad, g_enc_a, g_enc_b, g_enc_c, g_enc_d, g_enc_e, g_enc_f, g_enc_g, g_enc_h, g_enc_i, g_enc_j, g_enc_k, g_enc_l, g_to_dec, g_mask_tok, g_dec_a, g_dec_b, g_dec_c, g_dec_d, g_dec_e, g_dec_f, g_dec_g, g_dec_h, g_dec_i, g_dec_j, g_dec_k, g_dec_l)
```

```python
import functools

import jax
import jax.numpy as jnp
import numpy as np
from jax import lax
from jax.experimental import pallas as pl
from jax.experimental.pallas import tpu as pltpu
from jax.sharding import Mesh
from jax.sharding import PartitionSpec as P

HEADS = 12
DD = 384
DHEADS = 6
VIS = 157
FULL = 1568
CAP = 64
NORM_EPS = 1e-06
NEG_LARGE = -1e30
ALL = ("z", "y", "core", "x")
WIDE = ("z", "y", "core")
F32 = jnp.float32
BF16 = jnp.bfloat16


def shift(value, axis, step):
    return lax.ppermute(value, axis, [(i, (i + step) % 4) for i in range(4)])


def swap(value):
    return lax.ppermute(value, "core", [(0, 1), (1, 0)])


def spread(piece, axis):
    across = shift(piece, axis, 2)
    return [piece, shift(piece, axis, 1), across, shift(piece, axis, 3)]


def exchange(pieces, axis, sign=1):
    far = shift(pieces[2], axis, 2)
    return [pieces[0], shift(pieces[1], axis, sign), far, shift(pieces[3], axis, -sign)]


def reduce_phase(current, axis):
    rows = current.shape[0] // 4
    index = lax.axis_index(axis)
    got = []
    for step in (2, 1, 3):
        piece = lax.dynamic_slice_in_dim(current, ((index + step) % 4) * rows, rows, 0)
        got.append(shift(piece.astype(BF16), axis, step).astype(F32))
    own = lax.dynamic_slice_in_dim(current, index * rows, rows, 0).astype(F32)
    return own + (got[0] + got[1] + got[2])


def sum_vector(vector):
    vector = vector + swap(vector)
    for axis in ("x", "y", "z"):
        parts = spread(vector, axis)
        vector = (parts[0] + parts[1]) + (parts[2] + parts[3])
    return vector


def tail_kernel(place, *refs):
    ins, out = refs[:8], refs[8]
    half, step = pl.program_id(0), pl.program_id(1)
    rows = ins[0].shape[0]
    mid, low = rows // 4, rows // 16
    for h in range(2):
        for k in range(4):

            @pl.when(jnp.logical_and(half == h, step == k))
            def _():
                for a in range(4):
                    for b in range(4):
                        to = ((place[1] + 4 - a) % 4) * mid + ((place[2] + 4 - b) % 4) * low
                        at = a * mid + b * low
                        out[pl.ds(pl.multiple_of(to, 8), low), :] = ins[h * 4 + k][
                            at : at + low, :
                        ].astype(F32)


def tail_sum(own_half, other_half):
    current = own_half + swap(other_half).astype(F32)
    current = reduce_phase(current, "y")
    current = reduce_phase(current, "z")
    parts = spread(current.astype(BF16), "z")
    parts = spread(jnp.concatenate(parts, 0), "y")
    mine = spread(jnp.concatenate(parts, 0), "x")
    theirs = [swap(part) for part in mine]
    rows, cols = mine[0].shape
    place = jnp.stack([lax.axis_index(a) for a in ("x", "y", "z", "core")]).astype(jnp.int32)
    whole = pl.BlockSpec((rows, cols), lambda h, k, s: (0, 0))
    return pl.pallas_call(
        tail_kernel,
        grid_spec=pltpu.PrefetchScalarGridSpec(
            num_scalar_prefetch=1,
            grid=(2, 4),
            in_specs=[whole] * 8,
            out_specs=pl.BlockSpec(
                (rows, cols), lambda h, k, s: (((s[0] + 4 - k) % 4) * 2 + (s[3] + h) % 2, 0)
            ),
        ),
        out_shape=jax.ShapeDtypeStruct((8 * rows, cols), F32),
        compiler_params=pltpu.CompilerParams(vmem_limit_bytes=40 << 20),
    )(place, *mine, *theirs)


def dot_nt(left, right):
    return lax.dot_general(left, right, (((1,), (1,)), ((), ())), preferred_element_type=F32)


def dot_nn(left, right):
    return lax.dot_general(left, right, (((1,), (0,)), ((), ())), preferred_element_type=F32)


def low_lanes(rows):
    return lax.broadcasted_iota(jnp.int32, (rows, 128), 1) < 64


def two_heads(ref, at, count):
    pair = ref[pl.ds(at, count), :]
    low, zero = low_lanes(count), jnp.zeros_like(pair)
    return jnp.concatenate([jnp.where(low, pair, zero), jnp.where(low, zero, pair)], axis=0)


def mask_scores(scores, seg_q, seg_k, at, count):
    if seg_q is None:
        return scores
    mine = seg_q[pl.ds(at, count), :]
    allowed = jnp.concatenate([mine, mine], axis=0) == seg_k[...]
    return jnp.where(allowed, scores, NEG_LARGE)


def forward_kernel(*refs, block, masked):
    if masked:
        seg_q, seg_k, q_ref, k_ref, v_ref, out_ref, lse_ref = refs
    else:
        seg_q = seg_k = None
        q_ref, k_ref, v_ref, out_ref, lse_ref = refs
    count = q_ref.shape[0] // block
    low = low_lanes(block)

    def scores_of(i):
        scores = dot_nt(two_heads(q_ref, i * block, block), k_ref[...])
        return mask_scores(scores, seg_q, seg_k, i * block, block)

    scores = scores_of(0)
    for i in range(count):
        later = scores_of(i + 1) if i + 1 < count else None
        peak = jnp.max(scores, axis=1, keepdims=True)
        probs = jnp.exp(scores - peak)
        total = jnp.sum(probs, axis=1, keepdims=True)
        out = dot_nn(probs.astype(BF16), v_ref[...]) * (1.0 / total)
        rows = pl.ds(i * block, block)
        out_ref[rows, :] = jnp.where(low, out[:block], out[block:]).astype(BF16)
        lse = peak + jnp.log(total)
        lse_ref[0, rows, :] = jnp.concatenate([lse[:block], lse[block:]], axis=1)
        scores = later


def backward_kernel(*refs, block, masked):
    if masked:
        seg_q, seg_k = refs[:2]
        refs = refs[2:]
    else:
        seg_q = seg_k = None
    q_ref, k_ref, v_ref, out_ref, grad_ref, lse_ref, res_ref, k_sum, v_sum = refs
    length = q_ref.shape[0]
    count = length // block
    low = low_lanes(block)
    pair = pl.program_id(0)
    width = res_ref.shape[1] // 3
    at_q = pl.multiple_of(pair * 128, 128)
    at_k = pl.multiple_of(width + pair * 128, 128)
    at_v = pl.multiple_of(2 * width + pair * 128, 128)

    def front(i):
        queries = two_heads(q_ref, i * block, block)
        grads = two_heads(grad_ref, i * block, block)
        scores = mask_scores(dot_nt(queries, k_ref[...]), seg_q, seg_k, i * block, block)
        return queries, grads, scores, dot_nt(grads, v_ref[...])

    current = front(0)
    for i in range(count):
        later = front(i + 1) if i + 1 < count else None
        queries, grads, scores, probs_grad = current
        rows = pl.ds(i * block, block)
        lse = lse_ref[0, rows, :]
        lse = jnp.concatenate([lse[:, 0:1], lse[:, 1:2]], axis=0)
        inner = grad_ref[rows, :].astype(F32) * out_ref[rows, :].astype(F32)
        zero = jnp.zeros_like(inner)
        inner = jnp.concatenate(
            [
                jnp.sum(jnp.where(low, inner, zero), axis=1, keepdims=True),
                jnp.sum(jnp.where(low, zero, inner), axis=1, keepdims=True),
            ],
            axis=0,
        )
        probs = jnp.exp(scores - lse)
        score_grad = (probs * (probs_grad - inner)).astype(BF16)
        q_grad = dot_nn(score_grad, k_ref[...])
        q_grad = jnp.where(low, q_grad[:block], q_grad[block:]).astype(BF16).astype(F32)
        res_ref[rows, pl.ds(at_q, 128)] = (q_grad * 0.125).astype(BF16)
        v_part = dot_nn(grads.T, probs.astype(BF16))
        k_part = dot_nn(queries.T, score_grad)
        if i == 0:
            k_sum[...] = k_part
            v_sum[...] = v_part
        else:
            k_sum[...] += k_part
            v_sum[...] += v_part
        current = later
    res_ref[:, pl.ds(at_k, 128)] = k_sum[...].T.astype(BF16)
    res_ref[:, pl.ds(at_v, 128)] = v_sum[...].T.astype(BF16)


def attention_specs(length, width, masked):
    pairs = width // 128
    column = lambda first: pl.BlockSpec((length, 128), lambda p: (0, first + p))
    segs = [
        pl.BlockSpec((length, 1), lambda p: (0, 0)),
        pl.BlockSpec((1, length), lambda p: (0, 0)),
    ]
    qkv = [column(0), column(pairs), column(2 * pairs)]
    stat = pl.BlockSpec((1, length, 2), lambda p: (p, 0, 0))
    return pairs, column, (segs if masked else []) + qkv, stat


def attend(qkv, segs, block):
    length, width = qkv.shape[0], qkv.shape[1] // 3
    masked = len(segs) > 0
    pairs, column, ins, stat = attention_specs(length, width, masked)
    work = 2 * pairs * length * length
    return pl.pallas_call(
        functools.partial(forward_kernel, block=block, masked=masked),
        grid=(pairs,),
        in_specs=ins,
        out_specs=[column(0), stat],
        out_shape=[
            jax.ShapeDtypeStruct((length, width), BF16),
            jax.ShapeDtypeStruct((pairs, length, 2), F32),
        ],
        compiler_params=pltpu.CompilerParams(vmem_limit_bytes=56 << 20),
        cost_estimate=pl.CostEstimate(
            flops=work * 64 * 16, bytes_accessed=length * width * 8, transcendentals=work
        ),
    )(*segs, qkv, qkv, qkv)


def attend_back(qkv, out, grad, lse, segs, block):
    length, width = qkv.shape[0], qkv.shape[1] // 3
    masked = len(segs) > 0
    pairs, column, ins, stat = attention_specs(length, width, masked)
    work = 2 * pairs * length * length
    return pl.pallas_call(
        functools.partial(backward_kernel, block=block, masked=masked),
        grid=(pairs,),
        in_specs=ins + [column(0), column(0), stat],
        out_specs=pl.BlockSpec((length, 3 * width), lambda p: (0, 0)),
        out_shape=jax.ShapeDtypeStruct((length, 3 * width), BF16),
        scratch_shapes=[pltpu.VMEM((128, length), F32)] * 2,
        compiler_params=pltpu.CompilerParams(vmem_limit_bytes=56 << 20),
        cost_estimate=pl.CostEstimate(
            flops=work * 64 * 40, bytes_accessed=length * width * 16, transcendentals=work
        ),
    )(*segs, qkv, qkv, qkv, out, grad, lse)


def sincos_table(count_pos, count_col):
    position = np.arange(count_pos).astype(np.float32)[:, None]
    column = np.arange(count_col)
    exponent = (2 * (column // 2)).astype(np.float32) / np.float32(count_col)
    angles = position / np.power(np.float32(10000.0), exponent)[None, :]
    table = np.where(column[None, :] % 2 == 0, np.sin(angles), np.cos(angles))
    return table.astype(np.float32)


def norm_parts(values):
    average = jnp.mean(values, axis=-1, keepdims=True)
    centred = values - average
    variance = jnp.mean(centred * centred, axis=-1, keepdims=True)
    inv_std = lax.rsqrt(variance + NORM_EPS)
    return centred * inv_std, inv_std


def norm_back(gradient, normed, inv_std, gain):
    scaled = gradient * gain
    return inv_std * (
        scaled
        - jnp.mean(scaled, axis=-1, keepdims=True)
        - normed * jnp.mean(scaled * normed, axis=-1, keepdims=True)
    )


def mm(left, right):
    return jnp.einsum("sk,kn->sn", left, right, preferred_element_type=F32)


def mm_back(left, right):
    return jnp.einsum("sn,kn->sk", left, right, preferred_element_type=F32)


def mm_grad(left, right):
    return jnp.einsum("sk,sn->kn", left, right, preferred_element_type=F32)


def exact_gelu(values):
    return jax.nn.gelu(values, approximate=False)


def feed_forward(x1, gain, offset, fc1, fc1_bias, fc2, fc2_bias):
    normed, inv_std = norm_parts(x1)
    low = (normed * gain + offset).astype(BF16)
    pre = mm(low, fc1) + fc1_bias
    act = exact_gelu(pre).astype(BF16)
    result = x1 + (mm(act, fc2) + fc2_bias)
    return result, (normed, inv_std, low, pre, act)


def feed_back(gy, kept, gain, fc1, fc2):
    normed, inv_std, low, pre, act = kept
    gz = gy.astype(BF16)
    fc2_grad = mm_grad(act, gz).astype(BF16)
    fc2_bias_grad = jnp.sum(gz.astype(F32), axis=0)
    gpre = jax.vjp(exact_gelu, pre)[1](mm_back(gz, fc2))[0].astype(BF16)
    fc1_grad = mm_grad(low, gpre).astype(BF16)
    fc1_bias_grad = jnp.sum(gpre.astype(F32), axis=0)
    back = mm_back(gpre, fc1)
    gain_grad = jnp.sum(back * normed, axis=0)
    shift_grad = jnp.sum(back, axis=0)
    gx1 = gy + norm_back(back, normed, inv_std, gain)
    return gx1, fc1_grad, fc2_grad, (gain_grad, shift_grad, fc1_bias_grad, fc2_bias_grad)


def body(
    encoder_input,
    seg_ids,
    vis_slot,
    restore_order,
    enc_norm1_gain,
    enc_norm1_shift,
    enc_qkv_weight,
    enc_qv_bias,
    enc_proj_weight,
    enc_proj_bias,
    enc_norm2_gain,
    enc_norm2_shift,
    enc_fc1_weight,
    enc_fc1_bias,
    enc_fc2_weight,
    enc_fc2_bias,
    to_dec_weight,
    mask_token,
    dec_norm1_gain,
    dec_norm1_shift,
    dec_qkv_weight,
    dec_qv_bias,
    dec_proj_weight,
    dec_proj_bias,
    dec_norm2_gain,
    dec_norm2_shift,
    dec_fc1_weight,
    dec_fc1_bias,
    dec_fc2_weight,
    dec_fc2_bias,
    out_grad,
):
    x_at = lax.axis_index("x")
    core = lax.axis_index("core")
    tokens, width = encoder_input.shape[1:]
    hw = width // 4
    wide = lambda vector: vector.astype(F32)

    own_input = encoder_input[0]
    row_input = jnp.concatenate(spread(own_input, "x"), axis=0)

    by_group = enc_qkv_weight.reshape(hw, 3, 4, hw)
    group = lambda step: lax.dynamic_index_in_dim(
        by_group, (x_at + step) % 4, 2, keepdims=False
    ).reshape(hw, 3 * hw)
    got = exchange([group(k) for k in range(4)], "x")
    qkv_mine = jnp.zeros((4, hw, 3 * hw), BF16)
    for k in range(4):
        qkv_mine = lax.dynamic_update_index_in_dim(qkv_mine, got[k], (x_at - k) % 4, 0)
    qkv_pad = jnp.pad(qkv_mine.reshape(width, 3, hw), ((0, 0), (0, 0), (0, 64)))
    qkv_pad = qkv_pad.reshape(width, 768)
    bias_mine = lax.dynamic_index_in_dim(
        wide(enc_qv_bias).reshape(2, 4, hw), x_at, 1, keepdims=False
    )
    bias_mine = jnp.pad(bias_mine, ((0, 0), (0, 64)))
    bias_mine = jnp.concatenate([bias_mine[0], jnp.zeros((256,), F32), bias_mine[1]])
    scale_mine = jnp.concatenate([jnp.full((256,), 0.125, F32), jnp.ones((512,), F32)])

    half = lambda weight: lax.dynamic_slice_in_dim(
        weight, core * (weight.shape[0] // 2), weight.shape[0] // 2, 0
    )
    gather = lambda weight: lax.all_gather(half(weight), ("x", "core"), axis=0, tiled=True)
    proj_whole = gather(enc_proj_weight)
    fc1_whole = gather(enc_fc1_weight)
    fc2_whole = gather(enc_fc2_weight)

    row_seg = seg_ids[0].reshape(4, tokens)
    row_slot = vis_slot[0].reshape(4, tokens)
    position = jnp.arange(tokens)
    earlier = position[None, :] < position[:, None]
    same_clip = row_seg[:, :, None] == row_seg[:, None, :]
    ranks = jnp.sum(jnp.logical_and(same_clip, earlier), axis=-1)
    turn = (x_at - jnp.arange(4)) % 4
    seg_turned = jnp.take(row_seg, turn, axis=0)
    segs = (seg_turned.reshape(4 * tokens, 1), seg_turned.reshape(1, 4 * tokens))
    own_seg = lax.dynamic_index_in_dim(row_seg, x_at, 0, keepdims=False)
    own_rank = lax.dynamic_index_in_dim(ranks, x_at, 0, keepdims=False)
    cap_index = jnp.arange(CAP)
    clip_to = (x_at + jnp.arange(4)) % 4
    send_map = jnp.logical_and(
        own_seg[None, None, :] == clip_to[:, None, None],
        own_rank[None, None, :] == cap_index[None, :, None],
    ).astype(BF16)
    chosen = jnp.logical_and(
        seg_turned[:, None, :] == x_at,
        jnp.take(ranks, turn, axis=0)[:, None, :] == cap_index[None, :, None],
    )
    slot_turned = jnp.take(row_slot, turn, axis=0)
    slot_vis = jnp.sum(jnp.where(chosen, slot_turned[:, None, :] + 1, 0), axis=-1) - 1
    restore_row = restore_order[0, 0]
    place_map = (restore_row[:, None] == slot_vis.reshape(1, 4 * CAP)).astype(BF16)
    is_mask = (restore_row >= VIS)[:, None]

    normed_one, inv_one = norm_parts(wide(row_input))
    first_in = (normed_one * wide(enc_norm1_gain) + wide(enc_norm1_shift)).astype(BF16)
    qkv = ((mm(first_in, qkv_pad) + bias_mine) * scale_mine).astype(BF16)
    att_mine, enc_lse = attend(qkv, segs, 128)
    blocks = att_mine.reshape(4, tokens, 256)
    got = exchange([blocks[(4 - k) % 4, :, :hw] for k in range(4)], "x")
    attended = jnp.zeros((4, tokens, hw), BF16)
    for k in range(4):
        attended = lax.dynamic_update_index_in_dim(attended, got[k], (x_at - k) % 4, 0)
    attended = jnp.moveaxis(attended, 0, 1).reshape(tokens, width)
    enc_x1 = wide(own_input) + (mm(attended, proj_whole) + wide(enc_proj_bias))
    enc_out, enc_kept = feed_forward(
        enc_x1,
        wide(enc_norm2_gain),
        wide(enc_norm2_shift),
        fc1_whole,
        wide(enc_fc1_bias),
        fc2_whole,
        wide(enc_fc2_bias),
    )
    enc_low = enc_out.astype(BF16)
    reduced = mm(enc_low, to_dec_weight).astype(BF16)

    send_rows = jnp.einsum("ast,td->asd", send_map, reduced, preferred_element_type=F32)
    send_rows = send_rows.astype(BF16)
    received = jnp.concatenate(exchange([send_rows[k] for k in range(4)], "x"), axis=0)
    grid = (
        mm(place_map, received)
        + jnp.where(is_mask, wide(mask_token), 0.0)
        + jnp.asarray(sincos_table(FULL, DD))
    )

    dec_normed, dec_inv = norm_parts(grid)
    dec_in = (dec_normed * wide(dec_norm1_gain) + wide(dec_norm1_shift)).astype(BF16)
    dec_bias = wide(dec_qv_bias)
    dec_bias = jnp.concatenate([dec_bias[:DD], jnp.zeros((DD,), F32), dec_bias[DD:]])
    dec_scale = jnp.concatenate([jnp.full((DD,), 0.125, F32), jnp.ones((2 * DD,), F32)])
    dec_qkv = ((mm(dec_in, dec_qkv_weight) + dec_bias) * dec_scale).astype(BF16)
    dec_att, dec_lse = attend(dec_qkv, (), 224)
    dec_x1 = grid + (mm(dec_att, dec_proj_weight) + wide(dec_proj_bias))
    dec_out, dec_kept = feed_forward(
        dec_x1,
        wide(dec_norm2_gain),
        wide(dec_norm2_shift),
        dec_fc1_weight,
        wide(dec_fc1_bias),
        dec_fc2_weight,
        wide(dec_fc2_bias),
    )

    dec_gx1, dec_fc1_grad, dec_fc2_grad, dec_small = feed_back(
        wide(out_grad[0, 0]), dec_kept, wide(dec_norm2_gain), dec_fc1_weight, dec_fc2_weight
    )
    dec_go = dec_gx1.astype(BF16)
    dec_proj_grad = mm_grad(dec_att, dec_go).astype(BF16)
    dec_proj_bias_grad = jnp.sum(wide(dec_go), axis=0)
    dec_gatt = mm_back(dec_go, dec_proj_weight).astype(BF16)
    dec_gqkv = attend_back(dec_qkv, dec_att, dec_gatt, dec_lse, (), 112)
    dec_qkv_grad = mm_grad(dec_in, dec_gqkv).astype(BF16)
    dec_gqkv_sum = jnp.sum(wide(dec_gqkv), axis=0)
    dec_qv_grad = jnp.concatenate([dec_gqkv_sum[:DD], dec_gqkv_sum[2 * DD :]])
    back = mm_back(dec_gqkv, dec_qkv_weight)
    dec_norm1_gain_grad = jnp.sum(back * dec_normed, axis=0)
    dec_norm1_shift_grad = jnp.sum(back, axis=0)
    grid_grad = dec_gx1 + norm_back(back, dec_normed, dec_inv, wide(dec_norm1_gain))
    mask_grad = jnp.sum(jnp.where(is_mask, grid_grad, 0.0), axis=0)

    slot_grads = mm_grad(place_map, grid_grad.astype(BF16)).astype(BF16).reshape(4, CAP, DD)
    returned = exchange([slot_grads[k] for k in range(4)], "x", -1)
    reduced_grad = jnp.einsum(
        "ast,asd->td", send_map, jnp.stack(returned), preferred_element_type=F32
    ).astype(BF16)
    to_dec_grad = mm_grad(enc_low, reduced_grad).astype(BF16)
    enc_gy = mm_back(reduced_grad, to_dec_weight)

    enc_gx1, enc_fc1_grad, enc_fc2_grad, enc_small = feed_back(
        enc_gy, enc_kept, wide(enc_norm2_gain), fc1_whole, fc2_whole
    )
    enc_go = enc_gx1.astype(BF16)
    enc_proj_grad = mm_grad(attended, enc_go).astype(BF16)
    enc_proj_bias_grad = jnp.sum(wide(enc_go), axis=0)
    enc_gatt = mm_back(enc_go, proj_whole).astype(BF16).reshape(tokens, 4, hw)
    got = exchange(
        [
            lax.dynamic_index_in_dim(enc_gatt, (x_at + k) % 4, 1, keepdims=False)
            for k in range(4)
        ],
        "x",
    )
    gatt_mine = jnp.pad(jnp.concatenate(got, axis=0), ((0, 0), (0, 64)))
    gqkv = attend_back(qkv, att_mine, gatt_mine, enc_lse, segs, 128)
    own_cols = jnp.concatenate(
        [gqkv[:, k * 256 : k * 256 + hw] for k in range(3)], axis=1
    )
    qkv_grad_half = lambda which: mm_grad(
        lax.dynamic_slice_in_dim(first_in, which * (width // 2), width // 2, 1), own_cols
    )
    tail = tail_sum(qkv_grad_half(core), qkv_grad_half(1 - core).astype(BF16))
    tail = tail.reshape(4, width, 3, hw).transpose(1, 2, 0, 3).reshape(width, 3 * width)
    gqkv_sum = jnp.sum(wide(own_cols), axis=0).reshape(3, hw)
    qv_grad = lax.dynamic_update_index_in_dim(
        jnp.zeros((2, 4, hw), F32), jnp.stack([gqkv_sum[0], gqkv_sum[2]]), x_at, 1
    ).reshape(2 * width)
    part = mm_back(gqkv, qkv_pad)
    norm1_gain_grad = jnp.sum(part * normed_one, axis=0)
    norm1_shift_grad = jnp.sum(part, axis=0)
    part_low = part.astype(BF16).reshape(4, tokens, width)
    others = exchange([part_low[k] for k in range(4)], "x", -1)
    back = part[:tokens] + (wide(others[1]) + wide(others[2]) + wide(others[3]))
    input_grad = enc_gx1 + norm_back(
        back, normed_one[:tokens], inv_one[:tokens], wide(enc_norm1_gain)
    )

    dec_fc1_grad, dec_fc2_grad, dec_proj_grad = lax.psum(
        (dec_fc1_grad, dec_fc2_grad, dec_proj_grad), ALL
    )
    enc_fc1_grad, enc_fc2_grad, enc_proj_grad, to_dec_grad, dec_qkv_grad = lax.psum(
        (enc_fc1_grad, enc_fc2_grad, enc_proj_grad, to_dec_grad, dec_qkv_grad), ALL
    )
    vectors = [
        norm1_gain_grad,
        norm1_shift_grad,
        qv_grad,
        enc_proj_bias_grad,
        *enc_small,
        mask_grad,
        dec_norm1_gain_grad,
        dec_norm1_shift_grad,
        dec_qv_grad,
        dec_proj_bias_grad,
        *dec_small,
    ]
    summed = sum_vector(jnp.concatenate(vectors).reshape(-1, 128)).reshape(-1)
    cuts = np.cumsum([v.shape[0] for v in vectors])[:-1]
    v = jnp.split(summed, [int(c) for c in cuts])
    return (
        dec_out.astype(BF16)[None, None],
        input_grad[None],
        v[0],
        v[1],
        tail,
        v[2],
        wide(enc_proj_grad),
        v[3],
        v[4],
        v[5],
        wide(enc_fc1_grad),
        v[6],
        wide(enc_fc2_grad),
        v[7],
        wide(to_dec_grad),
        v[8],
        v[9],
        v[10],
        wide(dec_qkv_grad),
        v[11],
        wide(dec_proj_grad),
        v[12],
        v[13],
        v[14],
        wide(dec_fc1_grad),
        v[15],
        wide(dec_fc2_grad),
        v[16],
    )


def solution(mesh):
    fine = Mesh(mesh.devices.reshape(4, 4, 2, 4), ALL)
    row, shared, split = P(WIDE, None), P(), P("x", None)
    return jax.shard_map(
        body,
        mesh=fine,
        in_specs=(
            P(WIDE, "x", None),
            row,
            row,
            P(WIDE, "x", None),
            shared,
            shared,
            split,
            shared,
            split,
            shared,
            shared,
            shared,
            split,
            shared,
            split,
        )
        + (shared,) * 15
        + (P(WIDE, "x", None, None),),
        out_specs=(P(WIDE, "x", None, None), P(WIDE, "x", None)) + (shared,) * 26,
        check_vma=False,
    )
```

```python
import functools

import jax
import jax.numpy as jnp
import numpy as np
from jax import lax
from jax.experimental import pallas as pl
from jax.experimental.pallas import tpu as pltpu
from jax.sharding import Mesh
from jax.sharding import PartitionSpec as P

HEADS = 12
DD = 384
DHEADS = 6
VIS = 157
FULL = 1568
CAP = 64
NORM_EPS = 1e-06
NEG_LARGE = -1e30
ALL = ("z", "y", "core", "x")
WIDE = ("z", "y", "core")
F32 = jnp.float32
BF16 = jnp.bfloat16


def shift(value, axis, step):
    return lax.ppermute(value, axis, [(i, (i + step) % 4) for i in range(4)])


def swap(value):
    return lax.ppermute(value, "core", [(0, 1), (1, 0)])


def spread(piece, axis):
    across = shift(piece, axis, 2)
    return [piece, shift(piece, axis, 1), across, shift(piece, axis, 3)]


def exchange(pieces, axis, sign=1):
    far = shift(pieces[2], axis, 2)
    return [pieces[0], shift(pieces[1], axis, sign), far, shift(pieces[3], axis, -sign)]


def reduce_phase(current, axis):
    rows = current.shape[0] // 4
    index = lax.axis_index(axis)
    got = []
    for step in (2, 1, 3):
        piece = lax.dynamic_slice_in_dim(current, ((index + step) % 4) * rows, rows, 0)
        got.append(shift(piece.astype(BF16), axis, step).astype(F32))
    own = lax.dynamic_slice_in_dim(current, index * rows, rows, 0).astype(F32)
    return own + (got[0] + got[1] + got[2])


def sum_vector(vector):
    vector = vector + swap(vector)
    for axis in ("x", "y", "z"):
        parts = spread(vector, axis)
        vector = (parts[0] + parts[1]) + (parts[2] + parts[3])
    return vector


def pick(values, index):
    low = jnp.where(index == 0, values[0], values[1])
    high = jnp.where(index == 2, values[2], values[3])
    return jnp.where(index < 2, low, high)


def place_of(axes):
    return jnp.stack([lax.axis_index(a) for a in axes]).astype(jnp.int32)


def tail_kernel(place, *refs):
    ins, out, extra = refs[:8], refs[8], refs[9]
    half = pl.program_id(0)
    low = out.shape[0] // 4
    for b in range(4):
        rows = pl.ds(b * low, low)
        parts = [jnp.where(half == 0, ins[k][rows, :], ins[4 + k][rows, :]) for k in range(4)]
        parts = [pick(parts, (place[0] + 4 - g) % 4).astype(F32) for g in range(4)]
        to = pl.multiple_of(((place[2] + 4 - b) % 4) * low, 8)
        for c in range(3):
            out[pl.ds(to, low), c * 768 : (c + 1) * 768] = jnp.concatenate(
                [part[:, c * 192 : (c + 1) * 192] for part in parts], axis=1
            )
        extra[pl.ds(to, low), :] = jnp.concatenate([part[:, 576:] for part in parts], axis=1)


def tail_sum(own_half, other_half):
    current = own_half.astype(F32) + swap(other_half).astype(F32)
    current = reduce_phase(current, "y")
    current = reduce_phase(current, "z")
    parts = spread(current.astype(BF16), "z")
    parts = spread(jnp.concatenate(parts, 0), "y")
    mine = spread(jnp.concatenate(parts, 0), "x")
    theirs = [swap(part) for part in mine]
    rows, cols = mine[0].shape
    piece = pl.BlockSpec((rows // 4, cols), lambda h, a, s: (a, 0))
    return pl.pallas_call(
        tail_kernel,
        grid_spec=pltpu.PrefetchScalarGridSpec(
            num_scalar_prefetch=1,
            grid=(2, 4),
            in_specs=[piece] * 8,
            out_specs=[
                pl.BlockSpec(
                    (rows // 4, 4 * count),
                    lambda h, a, s: (((s[3] + h) % 2) * 4 + (s[1] + 4 - a) % 4, 0),
                )
                for count in (576, 64)
            ],
        ),
        out_shape=[jax.ShapeDtypeStruct((2 * rows, 4 * count), F32) for count in (576, 64)],
        compiler_params=pltpu.CompilerParams(vmem_limit_bytes=40 << 20),
    )(place_of(("x", "y", "z", "core")), *mine, *theirs)


def dot_nt(left, right):
    return lax.dot_general(left, right, (((1,), (1,)), ((), ())), preferred_element_type=F32)


def dot_nn(left, right):
    return lax.dot_general(left, right, (((1,), (0,)), ((), ())), preferred_element_type=F32)


def low_lanes(rows):
    return lax.broadcasted_iota(jnp.int32, (rows, 128), 1) < 64


def two_heads(ref, at, count):
    pair = ref[pl.ds(at, count), :]
    low, zero = low_lanes(count), jnp.zeros_like(pair)
    return jnp.concatenate([jnp.where(low, pair, zero), jnp.where(low, zero, pair)], axis=0)


def mask_scores(scores, seg_q, seg_k, at, count):
    if seg_q is None:
        return scores
    mine = seg_q[pl.ds(at, count), :]
    allowed = jnp.concatenate([mine, mine], axis=0) == seg_k[...]
    return jnp.where(allowed, scores, NEG_LARGE)


def forward_kernel(*refs, block, masked):
    if masked:
        seg_q, seg_k, q_ref, k_ref, v_ref, out_ref, lse_ref = refs
    else:
        seg_q = seg_k = None
        q_ref, k_ref, v_ref, out_ref, lse_ref = refs
    count = q_ref.shape[0] // block
    low = low_lanes(block)

    def scores_of(i):
        scores = dot_nt(two_heads(q_ref, i * block, block), k_ref[...])
        return mask_scores(scores, seg_q, seg_k, i * block, block)

    scores = scores_of(0)
    for i in range(count):
        later = scores_of(i + 1) if i + 1 < count else None
        peak = jnp.max(scores, axis=1, keepdims=True)
        probs = jnp.exp(scores - peak)
        total = jnp.sum(probs, axis=1, keepdims=True)
        out = dot_nn(probs.astype(BF16), v_ref[...]) * (1.0 / total)
        rows = pl.ds(i * block, block)
        out_ref[rows, :] = jnp.where(low, out[:block], out[block:]).astype(BF16)
        lse = peak + jnp.log(total)
        lse_ref[0, rows, :] = jnp.concatenate([lse[:block], lse[block:]], axis=1)
        scores = later


def backward_kernel(*refs, block, masked, first):
    if masked:
        seg_q, seg_k = refs[:2]
        refs = refs[2:]
    else:
        seg_q = seg_k = None
    q_ref, k_ref, v_ref, out_ref, grad_ref, lse_ref = refs[:6]
    res_ref, k_sum, v_sum = refs[6 + first :]
    length = q_ref.shape[0]
    count = length // block
    low = low_lanes(block)
    pair = pl.program_id(0)
    width = res_ref.shape[1] // 3
    at_q = pl.multiple_of(pair * 128, 128)
    at_k = pl.multiple_of(width + pair * 128, 128)
    at_v = pl.multiple_of(2 * width + pair * 128, 128)

    def front(i):
        queries = two_heads(q_ref, i * block, block)
        grads = two_heads(grad_ref, i * block, block)
        scores = mask_scores(dot_nt(queries, k_ref[...]), seg_q, seg_k, i * block, block)
        return queries, grads, scores, dot_nt(grads, v_ref[...])

    current = front(0)
    for i in range(count):
        later = front(i + 1) if i + 1 < count else None
        queries, grads, scores, probs_grad = current
        rows = pl.ds(i * block, block)
        lse = lse_ref[0, rows, :]
        lse = jnp.concatenate([lse[:, 0:1], lse[:, 1:2]], axis=0)
        inner = grad_ref[rows, :].astype(F32) * out_ref[rows, :].astype(F32)
        zero = jnp.zeros_like(inner)
        inner = jnp.concatenate(
            [
                jnp.sum(jnp.where(low, inner, zero), axis=1, keepdims=True),
                jnp.sum(jnp.where(low, zero, inner), axis=1, keepdims=True),
            ],
            axis=0,
        )
        probs = jnp.exp(scores - lse)
        score_grad = (probs * (probs_grad - inner)).astype(BF16)
        q_grad = dot_nn(score_grad, k_ref[...])
        q_grad = jnp.where(low, q_grad[:block], q_grad[block:]).astype(BF16).astype(F32)
        res_ref[rows, pl.ds(at_q, 128)] = (q_grad * 0.125).astype(BF16)
        v_part = dot_nn(grads.T, probs.astype(BF16))
        k_part = dot_nn(queries.T, score_grad)
        if i == 0:
            k_sum[...] = k_part
            v_sum[...] = v_part
        else:
            k_sum[...] += k_part
            v_sum[...] += v_part
        current = later
    res_ref[:, pl.ds(at_k, 128)] = k_sum[...].T.astype(BF16)
    res_ref[:, pl.ds(at_v, 128)] = v_sum[...].T.astype(BF16)


def attention_specs(length, width, masked):
    pairs = width // 128
    column = lambda first: pl.BlockSpec((length, 128), lambda p: (0, first + p))
    segs = [
        pl.BlockSpec((length, 1), lambda p: (0, 0)),
        pl.BlockSpec((1, length), lambda p: (0, 0)),
    ]
    qkv = [column(0), column(pairs), column(2 * pairs)]
    stat = pl.BlockSpec((1, length, 2), lambda p: (p, 0, 0))
    return pairs, column, (segs if masked else []) + qkv, stat


def attend(qkv, segs, block):
    length, width = qkv.shape[0], qkv.shape[1] // 3
    masked = len(segs) > 0
    pairs, column, ins, stat = attention_specs(length, width, masked)
    work = 2 * pairs * length * length
    return pl.pallas_call(
        functools.partial(forward_kernel, block=block, masked=masked),
        grid=(pairs,),
        in_specs=ins,
        out_specs=[column(0), stat],
        out_shape=[
            jax.ShapeDtypeStruct((length, width), BF16),
            jax.ShapeDtypeStruct((pairs, length, 2), F32),
        ],
        compiler_params=pltpu.CompilerParams(vmem_limit_bytes=56 << 20),
        cost_estimate=pl.CostEstimate(
            flops=work * 64 * 16, bytes_accessed=length * width * 8, transcendentals=work
        ),
    )(*segs, qkv, qkv, qkv)


def attend_back(qkv, out, grad, lse, segs, block, first=()):
    length, width = qkv.shape[0], qkv.shape[1] // 3
    masked = len(segs) > 0
    pairs, column, ins, stat = attention_specs(length, width, masked)
    work = 2 * pairs * length * length
    return pl.pallas_call(
        functools.partial(backward_kernel, block=block, masked=masked, first=len(first)),
        grid=(pairs,),
        in_specs=ins
        + [column(0), column(0), stat]
        + [pl.BlockSpec(memory_space=pl.ANY)] * len(first),
        out_specs=pl.BlockSpec((length, 3 * width), lambda p: (0, 0)),
        out_shape=jax.ShapeDtypeStruct((length, 3 * width), BF16),
        scratch_shapes=[pltpu.VMEM((128, length), F32)] * 2,
        compiler_params=pltpu.CompilerParams(vmem_limit_bytes=56 << 20),
        cost_estimate=pl.CostEstimate(
            flops=work * 64 * 40, bytes_accessed=length * width * 16, transcendentals=work
        ),
    )(*segs, qkv, qkv, qkv, out, grad, lse, *first)


def sincos_table(count_pos, count_col):
    position = np.arange(count_pos).astype(np.float32)[:, None]
    column = np.arange(count_col)
    exponent = (2 * (column // 2)).astype(np.float32) / np.float32(count_col)
    angles = position / np.power(np.float32(10000.0), exponent)[None, :]
    table = np.where(column[None, :] % 2 == 0, np.sin(angles), np.cos(angles))
    return table.astype(np.float32)


VMEM_ALL = pltpu.CompilerParams(vmem_limit_bytes=56 << 20)


def shape(rows, cols, dtype):
    return jax.ShapeDtypeStruct((rows, cols), dtype)


def cost(flops, moved, special=0):
    return pl.CostEstimate(flops=flops, bytes_accessed=moved, transcendentals=special)


def norm_parts(values):
    average = jnp.mean(values, axis=-1, keepdims=True)
    centred = values - average
    variance = jnp.mean(centred * centred, axis=-1, keepdims=True)
    inv_std = lax.rsqrt(variance + NORM_EPS)
    return centred * inv_std, inv_std


def norm_back(gradient, normed, inv_std, gain):
    scaled = gradient * gain
    return inv_std * (
        scaled
        - jnp.mean(scaled, axis=-1, keepdims=True)
        - normed * jnp.mean(scaled * normed, axis=-1, keepdims=True)
    )


def column_sum(values):
    return jnp.sum(values, axis=0, keepdims=True)


def mm_grad(left, right):
    return jnp.einsum("sk,sn->kn", left, right, preferred_element_type=F32)


def gelu_parts(u):
    cdf = 0.5 + 0.5 * lax.erf(u * 0.7071067811865476)
    bell = jnp.exp(u * u * -0.5)
    return u * cdf, cdf + u * (bell * 0.3989422804014327)


class Vectors:
    def __init__(self, arrays):
        self.at, self.size, total = {}, {}, 0
        for name, array in arrays.items():
            self.at[name], self.size[name] = total, array.shape[0]
            total += array.shape[0]
        self.total = total
        self.row = jnp.concatenate(list(arrays.values())).astype(F32).reshape(1, total)

    def of(self, ref, name, first=0, count=None):
        at = self.at[name] + first
        return ref[:, at : at + (self.size[name] - first if count is None else count)]


def group_kernel(place, weight, *outs):
    width = weight.shape[1] // 3
    part = width // 4
    for g in range(4):
        cols = []
        for c in range(3):
            cols.append(weight[:, c * width + g * part : c * width + (g + 1) * part])
            cols.append(jnp.zeros((weight.shape[0], 256 - part), BF16))
        piece = jnp.concatenate(cols, axis=1)
        for k in range(4):

            @pl.when((place[0] + k) % 4 == g)
            def _():
                outs[k][...] = piece


def group_pieces(weight, place):
    rows = weight.shape[0]
    return pl.pallas_call(
        group_kernel,
        grid_spec=pltpu.PrefetchScalarGridSpec(
            num_scalar_prefetch=1,
            grid=(1,),
            in_specs=[pl.BlockSpec(weight.shape, lambda i, s: (0, 0))],
            out_specs=[pl.BlockSpec((rows, 768), lambda i, s: (0, 0))] * 4,
        ),
        out_shape=[shape(rows, 768, BF16)] * 4,
        compiler_params=VMEM_ALL,
    )(place, weight)


def enc_in_kernel(place, *refs, vectors):
    inputs, pieces, vec = refs[:4], refs[4:8], refs[8]
    qkv_ref, low_ref, weight_ref = refs[9:]
    rows, tokens = pieces[0].shape[0], inputs[0].shape[0]
    for k in range(4):
        to = pl.multiple_of(((place[0] + 4 - k) % 4) * rows, 16)
        weight_ref[pl.ds(to, rows), :] = pieces[k][...]
    biases = []
    for first in (0, 768):
        groups = [vectors.of(vec, "enc_qv_bias", first + g * 192, 192) for g in range(4)]
        biases += [pick(groups, place[0]), jnp.zeros((1, 64), F32)]
    bias = jnp.concatenate(biases[:2] + [jnp.zeros((1, 256), F32)] + biases[2:], axis=1)
    scale = jnp.where(lax.broadcasted_iota(jnp.int32, (1, 768), 1) < 256, 0.125, 1.0)
    gain, offset = vectors.of(vec, "enc_norm1_gain"), vectors.of(vec, "enc_norm1_shift")
    for k in range(4):
        normed, _ = norm_parts(inputs[k][...].astype(F32))
        low = (normed * gain + offset).astype(BF16)
        out = pl.ds(k * tokens, tokens)
        low_ref[out, :] = low
        qkv_ref[out, :] = ((dot_nn(low, weight_ref[...]) + bias) * scale).astype(BF16)


def enc_in(inputs, pieces, vectors, place):
    tokens, width = inputs[0].shape
    rows = 4 * tokens
    whole = lambda a: pl.BlockSpec(a.shape, lambda i, s: (0, 0))
    outs = [shape(rows, 768, BF16), shape(rows, width, BF16), shape(width, 768, BF16)]
    return pl.pallas_call(
        functools.partial(enc_in_kernel, vectors=vectors),
        grid_spec=pltpu.PrefetchScalarGridSpec(
            num_scalar_prefetch=1,
            grid=(1,),
            in_specs=[whole(a) for a in (*inputs, *pieces, vectors.row)],
            out_specs=[whole(a) for a in outs],
        ),
        out_shape=outs,
        compiler_params=VMEM_ALL,
        cost_estimate=cost(2 * rows * width * 768, rows * width * 8),
    )(place, *inputs, *pieces, vectors.row)


def restack(wide, stacked):
    for b in range(4):
        stacked[b * 192 : (b + 1) * 192, :] = wide[:, b * 768 : (b + 1) * 768]


MATRIX_SPECS = [
    pl.BlockSpec((768, 768), lambda j, s: (0, 4)),
    pl.BlockSpec((768, 768), lambda j, s: (0, 5 + j)),
    pl.BlockSpec((192, 3072), lambda j, s: (j, 0)),
]


def enc_block_kernel(place, *refs, vectors):
    parts, (x, proj, fc1, fc2, to_dec, send_map, vec) = refs[:4], refs[4:11]
    att_ref, x1_ref, low_ref, act_ref, slope_ref, y_ref, send_ref, total, stacked = refs[11:]
    step = pl.program_id(0)

    @pl.when(step == 0)
    def _():
        groups = [part[...] for part in parts]
        att = jnp.concatenate([pick(groups, (place[0] + 4 - g) % 4) for g in range(4)], axis=1)
        att_ref[...] = att
        x1 = x[...].astype(F32) + (dot_nn(att, proj[...]) + vectors.of(vec, "enc_proj_bias"))
        x1_ref[...] = x1
        normed, _ = norm_parts(x1)
        gain, offset = vectors.of(vec, "enc_norm2_gain"), vectors.of(vec, "enc_norm2_shift")
        low_ref[...] = (normed * gain + offset).astype(BF16)
        total[...] = x1 + vectors.of(vec, "enc_fc2_bias")

    bias = pick([vectors.of(vec, "enc_fc1_bias", j * 768, 768) for j in range(4)], step)
    pre = dot_nn(low_ref[...], fc1[...]) + bias
    act, slope = gelu_parts(pre)
    act = act.astype(BF16)
    act_ref[...] = act
    slope_ref[...] = slope.astype(BF16)
    restack(fc2, stacked)
    total[...] += dot_nn(act, stacked[...])

    @pl.when(step == 3)
    def _():
        y = total[...].astype(BF16)
        y_ref[...] = y
        reduced = dot_nn(y, to_dec[...]).astype(BF16)
        send = dot_nn(send_map[...], reduced).astype(BF16)
        for k in range(4):
            send_ref[k] = send[k * CAP : (k + 1) * CAP, :]


def enc_block(parts, x, matrices, to_dec, send_map, vectors, place):
    rows, width = x.shape
    whole = lambda a: pl.BlockSpec(a.shape, lambda j, s: (0,) * len(a.shape))
    chunk = pl.BlockSpec((rows, 768), lambda j, s: (0, j))
    outs = [
        shape(rows, width, BF16),
        shape(rows, width, F32),
        shape(rows, width, BF16),
        shape(rows, 4 * width, BF16),
        shape(rows, 4 * width, BF16),
        shape(rows, width, BF16),
        jax.ShapeDtypeStruct((4, CAP, DD), BF16),
    ]
    return pl.pallas_call(
        functools.partial(enc_block_kernel, vectors=vectors),
        grid_spec=pltpu.PrefetchScalarGridSpec(
            num_scalar_prefetch=1,
            grid=(4,),
            in_specs=[whole(a) for a in (*parts, x)]
            + MATRIX_SPECS
            + [whole(a) for a in (to_dec, send_map, vectors.row)],
            out_specs=[
                chunk if a.shape[-1] == 4 * width else whole(a) for a in outs
            ],
            scratch_shapes=[pltpu.VMEM((rows, width), F32), pltpu.VMEM((width, width), BF16)],
        ),
        out_shape=outs,
        compiler_params=VMEM_ALL,
        cost_estimate=cost(rows * width * width * 20, width * width * 20, rows * width * 8),
    )(place, *parts, x, *[matrices] * 3, to_dec, send_map, vectors.row)


def enc_block_back_kernel(place, *refs, vectors, first):
    parts, (send_map, to_dec, x1, slope, proj, fc1, fc2, vec) = refs[:4], refs[4:12]
    refs = refs[:12] + refs[12 + first :]
    reduced_ref, gz_ref, gpre_ref, gx1_ref, go_ref = refs[12:17]
    gatt_refs, (fc1_b, fc2_b, gain_g, shift_g, proj_b) = refs[17:21], refs[21:26]
    gy, back, stacked = refs[-3:]
    step = pl.program_id(0)

    @pl.when(step == 0)
    def _():
        rows = jnp.concatenate([part[...] for part in parts], axis=0)
        reduced = dot_nn(send_map[...], rows).astype(BF16)
        reduced_ref[...] = reduced
        grad = dot_nt(reduced, to_dec[...])
        gy[...] = grad
        gz_ref[...] = grad.astype(BF16)
        fc2_b[...] = column_sum(grad.astype(BF16).astype(F32))
        back[...] = jnp.zeros_like(back)

    restack(fc2, stacked)
    gpre = (dot_nt(gz_ref[...], stacked[...]) * slope[...].astype(F32)).astype(BF16)
    gpre_ref[...] = gpre
    fc1_b[...] = column_sum(gpre.astype(F32))
    back[...] += dot_nt(gpre, fc1[...])

    @pl.when(step == 3)
    def _():
        normed, inv_std = norm_parts(x1[...])
        total = back[...]
        gain_g[...] = column_sum(total * normed)
        shift_g[...] = column_sum(total)
        gx1 = gy[...] + norm_back(total, normed, inv_std, vectors.of(vec, "enc_norm2_gain"))
        gx1_ref[...] = gx1
        go = gx1.astype(BF16)
        go_ref[...] = go
        proj_b[...] = column_sum(go.astype(F32))
        gatt = dot_nt(go, proj[...]).astype(BF16)
        groups = [gatt[:, g * 192 : (g + 1) * 192] for g in range(4)]
        for k in range(4):
            gatt_refs[k][...] = pick(groups, (place[0] + k) % 4)


def enc_block_back(parts, send_map, to_dec, x1, slope, matrices, vectors, place, first):
    rows, width = x1.shape
    whole = lambda a: pl.BlockSpec(a.shape, lambda j, s: (0,) * len(a.shape))
    outs = [
        shape(rows, DD, BF16),
        shape(rows, width, BF16),
        shape(rows, 4 * width, BF16),
        shape(rows, width, F32),
        shape(rows, width, BF16),
        *[shape(rows, 192, BF16)] * 4,
        shape(1, 4 * width, F32),
        *[shape(1, width, F32)] * 4,
    ]
    by_chunk = lambda a: pl.BlockSpec((a.shape[0], 768), lambda j, s: (0, j))
    return pl.pallas_call(
        functools.partial(enc_block_back_kernel, vectors=vectors, first=len(first)),
        grid_spec=pltpu.PrefetchScalarGridSpec(
            num_scalar_prefetch=1,
            grid=(4,),
            in_specs=[whole(a) for a in (*parts, send_map, to_dec, x1)]
            + [by_chunk(slope), *MATRIX_SPECS, whole(vectors.row)]
            + [pl.BlockSpec(memory_space=pl.ANY)] * len(first),
            out_specs=[by_chunk(a) if a.shape[-1] == 4 * width else whole(a) for a in outs],
            scratch_shapes=[pltpu.VMEM((rows, width), F32)] * 2
            + [pltpu.VMEM((width, width), BF16)],
        ),
        out_shape=outs,
        compiler_params=VMEM_ALL,
        cost_estimate=cost(rows * width * width * 20, width * width * 20),
    )(place, *parts, send_map, to_dec, x1, slope, *[matrices] * 3, vectors.row, *first)


def enc_in_back_kernel(*refs, vectors):
    inputs, (grad, weight, vec) = refs[:4], refs[4:7]
    own_ref, others, (gain_g, shift_g, grad_sum) = refs[7], refs[8:11], refs[11:]
    tokens = inputs[0].shape[0]
    gains = shifts = 0.0
    for k in range(4):
        part = dot_nt(grad[pl.ds(k * tokens, tokens), :], weight[...])
        normed, _ = norm_parts(inputs[k][...].astype(F32))
        gains = gains + column_sum(part * normed)
        shifts = shifts + column_sum(part)
        if k == 0:
            own_ref[...] = part
        else:
            others[k - 1][...] = part.astype(BF16)
    gain_g[...] = gains
    shift_g[...] = shifts
    grad_sum[...] = column_sum(grad[...].astype(F32))


def enc_in_back(inputs, grad, weight, vectors):
    tokens, width = inputs[0].shape
    outs = [shape(tokens, width, F32)] + [shape(tokens, width, BF16)] * 3
    outs += [shape(1, width, F32)] * 2 + [shape(1, 768, F32)]
    return pl.pallas_call(
        functools.partial(enc_in_back_kernel, vectors=vectors),
        out_shape=outs,
        compiler_params=VMEM_ALL,
        cost_estimate=cost(8 * tokens * width * 768, tokens * width * 32),
    )(*inputs, grad, weight, vectors.row)


def enc_end_kernel(x, gx1, own, a, b, c, vec, out, *, vectors):
    normed, inv_std = norm_parts(x[...].astype(F32))
    back = own[...] + (a[...].astype(F32) + b[...].astype(F32) + c[...].astype(F32))
    out[...] = gx1[...] + norm_back(back, normed, inv_std, vectors.of(vec, "enc_norm1_gain"))


def enc_end(x, gx1, back, vectors):
    return pl.pallas_call(
        functools.partial(enc_end_kernel, vectors=vectors),
        out_shape=shape(*x.shape, F32),
        compiler_params=VMEM_ALL,
    )(x, gx1, *back, vectors.row)


def dec_in_kernel(*refs, vectors):
    parts, (restore, slots, table, weight, vec) = refs[:4], refs[4:9]
    grid_ref, low_ref, qkv_ref = refs[9:]
    rows = jnp.concatenate([part[...] for part in parts], axis=0)
    order = restore[...]
    hot = jnp.where(order == slots[...], 1.0, 0.0).astype(BF16)
    placed = dot_nn(hot, rows)
    grid = placed + jnp.where(order >= VIS, vectors.of(vec, "mask_token"), 0.0) + table[...]
    grid_ref[...] = grid
    normed, _ = norm_parts(grid)
    low = normed * vectors.of(vec, "dec_norm1_gain") + vectors.of(vec, "dec_norm1_shift")
    low = low.astype(BF16)
    low_ref[...] = low
    packed = dot_nn(low, weight[...])
    queries = packed[:, :DD] + vectors.of(vec, "dec_qv_bias", 0, DD)
    qkv_ref[:, :DD] = (queries * 0.125).astype(BF16)
    qkv_ref[:, DD : 2 * DD] = packed[:, DD : 2 * DD].astype(BF16)
    values = packed[:, 2 * DD :] + vectors.of(vec, "dec_qv_bias", DD, DD)
    qkv_ref[:, 2 * DD :] = values.astype(BF16)


def dec_in(parts, restore, slots, table, weight, vectors, tile):
    rows = table.shape[0]
    row = lambda n: pl.BlockSpec((tile, n), lambda i: (i, 0))
    whole = lambda a: pl.BlockSpec(a.shape, lambda i: (0, 0))
    return pl.pallas_call(
        functools.partial(dec_in_kernel, vectors=vectors),
        grid=(rows // tile,),
        in_specs=[whole(a) for a in parts]
        + [row(1), whole(slots), row(DD), whole(weight), whole(vectors.row)],
        out_specs=[row(DD), row(DD), row(3 * DD)],
        out_shape=[shape(rows, DD, F32), shape(rows, DD, BF16), shape(rows, 3 * DD, BF16)],
        compiler_params=VMEM_ALL,
        cost_estimate=cost(rows * DD * DD * 8, rows * DD * 16),
    )(*parts, restore, slots, table, weight, vectors.row)


def dec_in_back_kernel(grad, weight, grid, gx1, restore, slots, vec, *outs, vectors):
    slot_refs, (gain_g, shift_g, mask_g, grad_sum, total) = outs[:4], outs[4:]
    step = pl.program_id(0)

    @pl.when(step == 0)
    def _():
        for ref in (gain_g, shift_g, mask_g, grad_sum, total):
            ref[...] = jnp.zeros_like(ref)

    back = dot_nt(grad[...], weight[...])
    normed, inv_std = norm_parts(grid[...])
    gain_g[...] += column_sum(back * normed)
    shift_g[...] += column_sum(back)
    grad_sum[...] += column_sum(grad[...].astype(F32))
    gx = gx1[...] + norm_back(back, normed, inv_std, vectors.of(vec, "dec_norm1_gain"))
    order = restore[0]
    hot = jnp.where(slots[...] == order, 1.0, 0.0).astype(BF16)
    total[...] += dot_nn(hot, gx.astype(BF16))
    masked = jnp.where(order >= VIS, 1.0, 0.0)
    ones = jnp.broadcast_to(masked, (8, masked.shape[1]))
    mask_g[...] += lax.dot_general(
        ones,
        gx,
        (((1,), (0,)), ((), ())),
        preferred_element_type=F32,
        precision=lax.Precision.HIGHEST,
    )[0:1, :]

    @pl.when(step == pl.num_programs(0) - 1)
    def _():
        for k in range(4):
            slot_refs[k][...] = total[k * CAP : (k + 1) * CAP, :].astype(BF16)


def dec_in_back(grad, weight, grid, gx1, restore, slots, vectors, tile):
    rows = grid.shape[0]
    row = lambda n: pl.BlockSpec((tile, n), lambda i: (i, 0))
    whole = lambda shape: pl.BlockSpec(shape, lambda i: (0, 0))
    sums = [DD, DD, DD, 3 * DD]
    return pl.pallas_call(
        functools.partial(dec_in_back_kernel, vectors=vectors),
        grid=(rows // tile,),
        in_specs=[
            row(3 * DD),
            whole(weight.shape),
            row(DD),
            row(DD),
            pl.BlockSpec((1, 1, tile), lambda i: (i, 0, 0)),
            whole(slots.shape),
            whole(vectors.row.shape),
        ],
        out_specs=[whole((CAP, DD))] * 4 + [whole((1, n)) for n in sums],
        out_shape=[shape(CAP, DD, BF16)] * 4 + [shape(1, n, F32) for n in sums],
        scratch_shapes=[pltpu.VMEM((4 * CAP, DD), F32)],
        compiler_params=VMEM_ALL,
        cost_estimate=cost(rows * DD * DD * 8, rows * DD * 16),
    )(grad, weight, grid, gx1, restore, slots, vectors.row)


def dec_block_kernel(x, att, proj, fc1, fc2, vec, *outs, vectors, chunk):
    x1_ref, low_ref, act_ref, slope_ref, y_ref = outs
    x1 = x[...] + (dot_nn(att[...], proj[...]) + vectors.of(vec, "dec_proj_bias"))
    x1_ref[...] = x1
    normed, _ = norm_parts(x1)
    low = normed * vectors.of(vec, "dec_norm2_gain") + vectors.of(vec, "dec_norm2_shift")
    low = low.astype(BF16)
    low_ref[...] = low
    total = x1 + vectors.of(vec, "dec_fc2_bias")
    hidden = fc1.shape[1]

    def pre_of(c):
        return dot_nn(low, fc1[:, c : c + chunk]) + vectors.of(vec, "dec_fc1_bias", c, chunk)

    pre = pre_of(0)
    for c in range(0, hidden, chunk):
        later = pre_of(c + chunk) if c + chunk < hidden else None
        act, slope = gelu_parts(pre)
        act = act.astype(BF16)
        act_ref[:, c : c + chunk] = act
        slope_ref[:, c : c + chunk] = slope.astype(BF16)
        total = total + dot_nn(act, fc2[c : c + chunk, :])
        pre = later
    y_ref[...] = total.astype(BF16)


def dec_block(x, att, proj, fc1, fc2, vectors, tile, chunk):
    rows, width = x.shape
    hidden = fc1.shape[1]
    row = lambda n: pl.BlockSpec((tile, n), lambda i: (i, 0))
    whole = lambda a: pl.BlockSpec(a.shape, lambda i: (0, 0))
    shapes = [(width, F32), (width, BF16), (hidden, BF16), (hidden, BF16), (width, BF16)]
    return pl.pallas_call(
        functools.partial(dec_block_kernel, vectors=vectors, chunk=chunk),
        grid=(rows // tile,),
        in_specs=[row(width), row(width)] + [whole(a) for a in (proj, fc1, fc2, vectors.row)],
        out_specs=[row(n) for n, _ in shapes],
        out_shape=[shape(rows, n, t) for n, t in shapes],
        compiler_params=VMEM_ALL,
        cost_estimate=cost(rows * hidden * width * 10, rows * hidden * 10, rows * hidden * 2),
    )(x, att, proj, fc1, fc2, vectors.row)


def dec_block_back_kernel(gy, x1, slope, proj, fc1, fc2, vec, *outs, vectors, chunk):
    gpre_ref, gx1_ref, go_ref, gatt_ref, fc1_b, fc2_b, gain_g, shift_g, proj_b = outs

    @pl.when(pl.program_id(0) == 0)
    def _():
        for ref in (fc1_b, fc2_b, gain_g, shift_g, proj_b):
            ref[...] = jnp.zeros_like(ref)

    gz = gy[...]
    fc2_b[...] += column_sum(gz.astype(F32))
    hidden = fc1.shape[1]
    grad = dot_nt(gz, fc2[:chunk, :])
    back = None
    for c in range(0, hidden, chunk):
        later = None
        if c + chunk < hidden:
            later = dot_nt(gz, fc2[c + chunk : c + 2 * chunk, :])
        gpre = (grad * slope[:, c : c + chunk].astype(F32)).astype(BF16)
        gpre_ref[:, c : c + chunk] = gpre
        fc1_b[:, c : c + chunk] += column_sum(gpre.astype(F32))
        part = dot_nt(gpre, fc1[:, c : c + chunk])
        back = part if back is None else back + part
        grad = later
    normed, inv_std = norm_parts(x1[...])
    gain_g[...] += column_sum(back * normed)
    shift_g[...] += column_sum(back)
    gx1 = gz.astype(F32) + norm_back(
        back, normed, inv_std, vectors.of(vec, "dec_norm2_gain")
    )
    gx1_ref[...] = gx1
    go = gx1.astype(BF16)
    go_ref[...] = go
    proj_b[...] += column_sum(go.astype(F32))
    gatt_ref[...] = dot_nt(go, proj[...]).astype(BF16)


def dec_block_back(gy, x1, slope, proj, fc1, fc2, vectors, tile, chunk):
    rows, width = x1.shape
    hidden = fc1.shape[1]
    row = lambda n: pl.BlockSpec((tile, n), lambda i: (i, 0))
    whole = lambda shape: pl.BlockSpec(shape, lambda i: (0, 0))
    consts = [proj, fc1, fc2, vectors.row]
    shapes = [(hidden, BF16), (width, F32), (width, BF16), (width, BF16)]
    sums = [hidden, width, width, width, width]
    return pl.pallas_call(
        functools.partial(dec_block_back_kernel, vectors=vectors, chunk=chunk),
        grid=(rows // tile,),
        in_specs=[row(width), row(width), row(hidden)] + [whole(a.shape) for a in consts],
        out_specs=[row(n) for n, _ in shapes] + [whole((1, n)) for n in sums],
        out_shape=[shape(rows, n, t) for n, t in shapes] + [shape(1, n, F32) for n in sums],
        compiler_params=VMEM_ALL,
        cost_estimate=cost(rows * hidden * width * 10, rows * hidden * 8),
    )(gy, x1, slope, *consts)


def body(
    encoder_input,
    seg_ids,
    vis_slot,
    restore_order,
    enc_norm1_gain,
    enc_norm1_shift,
    enc_qkv_weight,
    enc_qv_bias,
    enc_proj_weight,
    enc_proj_bias,
    enc_norm2_gain,
    enc_norm2_shift,
    enc_fc1_weight,
    enc_fc1_bias,
    enc_fc2_weight,
    enc_fc2_bias,
    to_dec_weight,
    mask_token,
    dec_norm1_gain,
    dec_norm1_shift,
    dec_qkv_weight,
    dec_qv_bias,
    dec_proj_weight,
    dec_proj_bias,
    dec_norm2_gain,
    dec_norm2_shift,
    dec_fc1_weight,
    dec_fc1_bias,
    dec_fc2_weight,
    dec_fc2_bias,
    out_grad,
):
    x_at = lax.axis_index("x")
    core = lax.axis_index("core")
    place = place_of(("x",))
    tokens, width = encoder_input.shape[1:]
    hw = width // 4
    vectors = Vectors(
        {
            "enc_norm1_gain": enc_norm1_gain,
            "enc_norm1_shift": enc_norm1_shift,
            "enc_qv_bias": enc_qv_bias,
            "enc_proj_bias": enc_proj_bias,
            "enc_norm2_gain": enc_norm2_gain,
            "enc_norm2_shift": enc_norm2_shift,
            "enc_fc1_bias": enc_fc1_bias,
            "enc_fc2_bias": enc_fc2_bias,
            "mask_token": mask_token,
            "dec_norm1_gain": dec_norm1_gain,
            "dec_norm1_shift": dec_norm1_shift,
            "dec_qv_bias": dec_qv_bias,
            "dec_proj_bias": dec_proj_bias,
            "dec_norm2_gain": dec_norm2_gain,
            "dec_norm2_shift": dec_norm2_shift,
            "dec_fc1_bias": dec_fc1_bias,
            "dec_fc2_bias": dec_fc2_bias,
        }
    )

    pieces = exchange(group_pieces(enc_qkv_weight, place), "x")
    own_input = encoder_input[0]
    inputs = spread(own_input, "x")

    eighth = hw // 8
    first_row = (core * 4 + lax.axis_index("y")) * eighth
    rows_of = lambda weight, first: lax.dynamic_slice_in_dim(weight, first, eighth, 0)
    strip = [rows_of(enc_fc2_weight, first_row + b * hw) for b in range(4)]
    strip += [rows_of(enc_proj_weight, first_row), rows_of(enc_fc1_weight, first_row)]
    matrices = lax.all_gather(
        jnp.concatenate(strip, axis=1), ("x", "core", "y"), axis=0, tiled=True
    )

    row_seg = seg_ids[0].reshape(4, tokens)
    row_slot = vis_slot[0].reshape(4, tokens)
    position = jnp.arange(tokens)
    earlier = position[None, :] < position[:, None]
    same_clip = row_seg[:, :, None] == row_seg[:, None, :]
    ranks = jnp.sum(jnp.logical_and(same_clip, earlier), axis=-1)
    turn = (x_at - jnp.arange(4)) % 4
    seg_turned = jnp.take(row_seg, turn, axis=0)
    segs = (seg_turned.reshape(4 * tokens, 1), seg_turned.reshape(1, 4 * tokens))
    own_seg = lax.dynamic_index_in_dim(row_seg, x_at, 0, keepdims=False)
    own_rank = lax.dynamic_index_in_dim(ranks, x_at, 0, keepdims=False)
    cap_index = jnp.arange(4 * CAP)
    clip_to = (x_at + cap_index // CAP) % 4
    send_map = jnp.logical_and(
        own_seg[None, :] == clip_to[:, None],
        own_rank[None, :] == (cap_index % CAP)[:, None],
    ).astype(BF16)
    send_back = jnp.logical_and(
        own_seg[:, None] == clip_to[None, :],
        own_rank[:, None] == (cap_index % CAP)[None, :],
    ).astype(BF16)
    chosen = jnp.logical_and(
        seg_turned[:, None, :] == x_at,
        jnp.take(ranks, turn, axis=0)[:, None, :] == jnp.arange(CAP)[None, :, None],
    )
    slot_turned = jnp.take(row_slot, turn, axis=0)
    slot_vis = jnp.sum(jnp.where(chosen, slot_turned[:, None, :] + 1, 0), axis=-1) - 1
    restore_row = restore_order[0, 0]
    restore_col = restore_row[:, None]
    restore_row = restore_row.reshape(2, 1, FULL // 2)
    table = jnp.asarray(sincos_table(FULL, DD))

    qkv, first_in, qkv_mine = enc_in(inputs, pieces, vectors, place)
    att_mine, enc_lse = attend(qkv, segs, 128)
    blocks = att_mine.reshape(4, tokens, 256)
    parts = exchange([blocks[(4 - k) % 4, :, :hw] for k in range(4)], "x")
    attended, enc_x1, second_in, enc_act, enc_slope, enc_low, send_rows = enc_block(
        parts, own_input, matrices, to_dec_weight, send_map, vectors, place
    )

    received = exchange([send_rows[k] for k in range(4)], "x")
    grid, dec_in_low, dec_qkv = dec_in(
        received,
        restore_col,
        slot_vis.reshape(1, 4 * CAP),
        table,
        dec_qkv_weight,
        vectors,
        FULL // 2,
    )
    dec_att, dec_lse = attend(dec_qkv, (), 224)
    dec_x1, dec_second, dec_act, dec_slope, dec_out = dec_block(
        grid, dec_att, dec_proj_weight, dec_fc1_weight, dec_fc2_weight, vectors, FULL // 2, 512
    )

    dec_gz = out_grad[0, 0]
    dec_gpre, dec_gx1, dec_go, dec_gatt, *dec_sums = dec_block_back(
        dec_gz,
        dec_x1,
        dec_slope,
        dec_proj_weight,
        dec_fc1_weight,
        dec_fc2_weight,
        vectors,
        FULL // 2,
        512,
    )
    dec_fc1_b, dec_fc2_b, dec_gain2_g, dec_shift2_g, dec_proj_b = dec_sums
    dec_gqkv = attend_back(dec_qkv, dec_att, dec_gatt, dec_lse, (), 112)
    *slot_grads, dec_gain1_g, dec_shift1_g, mask_g, dec_gqkv_sum = dec_in_back(
        dec_gqkv,
        dec_qkv_weight,
        grid,
        dec_gx1,
        restore_row,
        slot_vis.reshape(4 * CAP, 1),
        vectors,
        FULL // 2,
    )
    low_grad = lambda left, right: mm_grad(left, right).astype(BF16)
    dec_grads = (
        low_grad(dec_in_low, dec_gqkv),
        low_grad(dec_att, dec_go),
        low_grad(dec_second, dec_gpre),
        low_grad(dec_act, dec_gz),
    )

    returned = exchange(slot_grads, "x", -1)
    reduced_grad, enc_gz, enc_gpre, enc_gx1, enc_go, *rest = enc_block_back(
        returned,
        send_back,
        to_dec_weight,
        enc_x1,
        enc_slope,
        matrices,
        vectors,
        place,
        dec_grads,
    )
    gatt_parts, enc_sums = rest[:4], rest[4:]
    enc_fc1_b, enc_fc2_b, enc_gain2_g, enc_shift2_g, enc_proj_b = enc_sums
    columns = lambda array, which: lax.dynamic_slice_in_dim(
        array, which * (array.shape[1] // 2), array.shape[1] // 2, 1
    )

    def halves(make):
        return make(core), make(1 - core)

    early = (
        low_grad(attended, enc_go),
        low_grad(enc_low, reduced_grad),
        low_grad(second_in, enc_gpre),
        low_grad(enc_act, enc_gz),
    )
    gatt_mine = jnp.concatenate(exchange(gatt_parts, "x"), axis=0)
    gatt_mine = jnp.pad(gatt_mine, ((0, 0), (0, 64)))
    gqkv = attend_back(qkv, att_mine, gatt_mine, enc_lse, segs, 128, early)
    own_back, *others, gain1_g, shift1_g, gqkv_sum = enc_in_back(
        inputs, gqkv, qkv_mine, vectors
    )

    qv = jnp.zeros((2, 4, hw), F32)
    qv = lax.dynamic_update_index_in_dim(
        qv, jnp.stack([gqkv_sum[0, :hw], gqkv_sum[0, 512 : 512 + hw]]), x_at, 1
    )
    small = [
        gain1_g,
        shift1_g,
        qv.reshape(1, 2 * width),
        enc_proj_b,
        enc_gain2_g,
        enc_shift2_g,
        enc_fc1_b,
        enc_fc2_b,
        mask_g,
        dec_gain1_g,
        dec_shift1_g,
        dec_gqkv_sum[:, :DD],
        dec_gqkv_sum[:, 2 * DD :],
        dec_proj_b,
        dec_gain2_g,
        dec_shift2_g,
        dec_fc1_b,
        dec_fc2_b,
    ]
    sizes = [v.shape[1] for v in small]
    vector = jnp.concatenate([*small, jnp.zeros((1, 14336 - sum(sizes)), F32)], axis=1)
    terms = spread(vector.reshape(112, 128), "x")
    vector = ((terms[0] + terms[1]) + (terms[2] + terms[3])).reshape(4, 56, 64)
    extra = lax.dynamic_index_in_dim(vector, x_at, 0, keepdims=False).astype(BF16)
    extra = jnp.pad(extra, ((0, width - 56), (0, 0)))

    def qkv_half(which):
        grad = low_grad(columns(first_in, which), gqkv)
        grad = [grad[:, c * 256 : c * 256 + hw] for c in range(3)]
        more = lax.dynamic_slice_in_dim(extra, which * (width // 2), width // 2, 0)
        return jnp.concatenate([*grad, more], axis=1)

    qkv_grad, vector = tail_sum(*halves(qkv_half))
    rest_grads = lax.psum((*dec_grads, *early), ALL)
    vector = vector[:56].reshape(56, 4, 64).transpose(1, 0, 2).reshape(14336)
    sizes[11:13] = [2 * DD]
    cuts = [int(c) for c in np.cumsum(sizes)]
    v = jnp.split(vector, cuts)

    back = exchange([None, *others], "x", -1)
    input_grad = enc_end(own_input, enc_gx1, (own_back, *back[1:]), vectors)

    wide = lambda array: array.astype(F32)
    return (
        dec_out[None, None],
        input_grad[None],
        v[0],
        v[1],
        qkv_grad,
        v[2],
        wide(rest_grads[4]),
        v[3],
        v[4],
        v[5],
        wide(rest_grads[6]),
        v[6],
        wide(rest_grads[7]),
        v[7],
        wide(rest_grads[5]),
        v[8],
        v[9],
        v[10],
        wide(rest_grads[0]),
        v[11],
        wide(rest_grads[1]),
        v[12],
        v[13],
        v[14],
        wide(rest_grads[2]),
        v[15],
        wide(rest_grads[3]),
        v[16],
    )


def solution(mesh):
    fine = Mesh(mesh.devices.reshape(4, 4, 2, 4), ALL)
    row, shared, split = P(WIDE, None), P(), P("x", None)
    return jax.shard_map(
        body,
        mesh=fine,
        in_specs=(
            P(WIDE, "x", None),
            row,
            row,
            P(WIDE, "x", None),
            shared,
            shared,
            split,
            shared,
            split,
            shared,
            shared,
            shared,
            split,
            shared,
            split,
        )
        + (shared,) * 15
        + (P(WIDE, "x", None, None),),
        out_specs=(P(WIDE, "x", None, None), P(WIDE, "x", None)) + (shared,) * 26,
        check_vma=False,
    )
```

```python
import functools

import jax
import jax.numpy as jnp
import numpy as np
from jax import lax
from jax.experimental import pallas as pl
from jax.experimental.pallas import tpu as pltpu
from jax.sharding import Mesh
from jax.sharding import PartitionSpec as P

HEADS = 12
DD = 384
DHEADS = 6
VIS = 157
FULL = 1568
CAP = 64
NORM_EPS = 1e-06
NEG_LARGE = -1e30
ALL = ("z", "y", "core", "x")
WIDE = ("z", "y", "core")
F32 = jnp.float32
BF16 = jnp.bfloat16


def shift(value, axis, step):
    return lax.ppermute(value, axis, [(i, (i + step) % 4) for i in range(4)])


def swap(value):
    return lax.ppermute(value, "core", [(0, 1), (1, 0)])


def spread(piece, axis):
    across = shift(piece, axis, 2)
    return [piece, shift(piece, axis, 1), across, shift(piece, axis, 3)]


def exchange(pieces, axis, sign=1):
    far = shift(pieces[2], axis, 2)
    return [pieces[0], shift(pieces[1], axis, sign), far, shift(pieces[3], axis, -sign)]


def reduce_phase(current, axis):
    rows = current.shape[0] // 4
    index = lax.axis_index(axis)
    got = []
    for step in (2, 1, 3):
        piece = lax.dynamic_slice_in_dim(current, ((index + step) % 4) * rows, rows, 0)
        got.append(shift(piece.astype(BF16), axis, step).astype(F32))
    own = lax.dynamic_slice_in_dim(current, index * rows, rows, 0).astype(F32)
    return own + (got[0] + got[1] + got[2])


def sum_vector(vector):
    vector = vector + swap(vector)
    for axis in ("x", "y", "z"):
        parts = spread(vector, axis)
        vector = (parts[0] + parts[1]) + (parts[2] + parts[3])
    return vector


def pick(values, index):
    low = jnp.where(index == 0, values[0], values[1])
    high = jnp.where(index == 2, values[2], values[3])
    return jnp.where(index < 2, low, high)


def place_of(axes):
    return jnp.stack([lax.axis_index(a) for a in axes]).astype(jnp.int32)


def tail_kernel(place, *refs):
    ins, out, extra = refs[:8], refs[8], refs[9]
    half = pl.program_id(0)
    low = out.shape[0] // 4
    for b in range(4):
        rows = pl.ds(b * low, low)
        parts = [jnp.where(half == 0, ins[k][rows, :], ins[4 + k][rows, :]) for k in range(4)]
        parts = [pick(parts, (place[0] + 4 - g) % 4).astype(F32) for g in range(4)]
        to = pl.multiple_of(((place[2] + 4 - b) % 4) * low, 8)
        for c in range(3):
            out[pl.ds(to, low), c * 768 : (c + 1) * 768] = jnp.concatenate(
                [part[:, c * 192 : (c + 1) * 192] for part in parts], axis=1
            )
        extra[pl.ds(to, low), :] = jnp.concatenate([part[:, 576:] for part in parts], axis=1)


def tail_sum(own_half, other_half):
    current = own_half.astype(F32) + swap(other_half).astype(F32)
    current = reduce_phase(current, "y")
    current = reduce_phase(current, "z")
    parts = spread(current.astype(BF16), "z")
    parts = spread(jnp.concatenate(parts, 0), "y")
    mine = spread(jnp.concatenate(parts, 0), "x")
    theirs = [swap(part) for part in mine]
    rows, cols = mine[0].shape
    piece = pl.BlockSpec((rows // 4, cols), lambda h, a, s: (a, 0))
    return pl.pallas_call(
        tail_kernel,
        grid_spec=pltpu.PrefetchScalarGridSpec(
            num_scalar_prefetch=1,
            grid=(2, 4),
            in_specs=[piece] * 8,
            out_specs=[
                pl.BlockSpec(
                    (rows // 4, 4 * count),
                    lambda h, a, s: (((s[3] + h) % 2) * 4 + (s[1] + 4 - a) % 4, 0),
                )
                for count in (576, 64)
            ],
        ),
        out_shape=[jax.ShapeDtypeStruct((2 * rows, 4 * count), F32) for count in (576, 64)],
        compiler_params=pltpu.CompilerParams(vmem_limit_bytes=40 << 20),
    )(place_of(("x", "y", "z", "core")), *mine, *theirs)


def final_kernel(place, *refs):
    ins, out = refs[:8], refs[8]
    half, step = pl.program_id(0), pl.program_id(1)
    rows = ins[0].shape[0]
    mid, low = rows // 4, rows // 16
    for h in range(2):
        for k in range(4):

            @pl.when(jnp.logical_and(half == h, step == k))
            def _():
                for a in range(4):
                    for b in range(4):
                        to = ((place[1] + 4 - a) % 4) * mid + ((place[2] + 4 - b) % 4) * low
                        at = a * mid + b * low
                        out[pl.ds(pl.multiple_of(to, 8), low), :] = ins[h * 4 + k][
                            at : at + low, :
                        ].astype(F32)


def sum_halves(own_half, other_half, axes, across):
    current = own_half.astype(F32) + swap(other_half).astype(F32)
    for axis in axes:
        current = reduce_phase(current, axis)
    parts = spread(current.astype(BF16), axes[2])
    parts = spread(jnp.concatenate(parts, 0), axes[1])
    mine = spread(jnp.concatenate(parts, 0), axes[0])
    theirs = [swap(part) for part in mine]
    rows, cols = mine[0].shape
    whole = pl.BlockSpec((rows, cols), lambda h, k, s: (0, 0))
    return pl.pallas_call(
        final_kernel,
        grid_spec=pltpu.PrefetchScalarGridSpec(
            num_scalar_prefetch=1,
            grid=(2, 4),
            in_specs=[whole] * 8,
            out_specs=pl.BlockSpec(
                (rows, cols), lambda h, k, s: across((s[0] + 4 - k) % 4, (s[3] + h) % 2)
            ),
        ),
        out_shape=jax.ShapeDtypeStruct(
            (rows * (1 + across(3, 1)[0]), cols * (1 + across(3, 1)[1])), F32
        ),
        compiler_params=pltpu.CompilerParams(vmem_limit_bytes=40 << 20),
        cost_estimate=pl.CostEstimate(
            flops=0, bytes_accessed=rows * cols * 48, transcendentals=0
        ),
    )(place_of(axes + ("core",)), *mine, *theirs)


def dot_nt(left, right):
    return lax.dot_general(left, right, (((1,), (1,)), ((), ())), preferred_element_type=F32)


def dot_nn(left, right):
    return lax.dot_general(left, right, (((1,), (0,)), ((), ())), preferred_element_type=F32)


def low_lanes(rows):
    return lax.broadcasted_iota(jnp.int32, (rows, 128), 1) < 64


def two_heads(ref, at, count):
    pair = ref[pl.ds(at, count), :]
    low, zero = low_lanes(count), jnp.zeros_like(pair)
    return jnp.concatenate([jnp.where(low, pair, zero), jnp.where(low, zero, pair)], axis=0)


def mask_scores(scores, seg_q, seg_k, at, count):
    if seg_q is None:
        return scores
    mine = seg_q[pl.ds(at, count), :]
    allowed = jnp.concatenate([mine, mine], axis=0) == seg_k[...]
    return jnp.where(allowed, scores, NEG_LARGE)


def forward_kernel(*refs, block, masked):
    if masked:
        seg_q, seg_k, q_ref, k_ref, v_ref, out_ref, lse_ref = refs
    else:
        seg_q = seg_k = None
        q_ref, k_ref, v_ref, out_ref, lse_ref = refs
    count = q_ref.shape[0] // block
    low = low_lanes(block)

    def scores_of(i):
        scores = dot_nt(two_heads(q_ref, i * block, block), k_ref[...])
        return mask_scores(scores, seg_q, seg_k, i * block, block)

    scores = scores_of(0)
    for i in range(count):
        later = scores_of(i + 1) if i + 1 < count else None
        peak = jnp.max(scores, axis=1, keepdims=True)
        probs = jnp.exp(scores - peak)
        total = jnp.sum(probs, axis=1, keepdims=True)
        out = dot_nn(probs.astype(BF16), v_ref[...]) * (1.0 / total)
        rows = pl.ds(i * block, block)
        out_ref[rows, :] = jnp.where(low, out[:block], out[block:]).astype(BF16)
        lse = peak + jnp.log(total)
        lse_ref[0, rows, :] = jnp.concatenate([lse[:block], lse[block:]], axis=1)
        scores = later


def backward_kernel(*refs, block, masked, first):
    if masked:
        seg_q, seg_k = refs[:2]
        refs = refs[2:]
    else:
        seg_q = seg_k = None
    q_ref, k_ref, v_ref, out_ref, grad_ref, lse_ref = refs[:6]
    res_ref, k_sum, v_sum = refs[6 + first :]
    length = q_ref.shape[0]
    count = length // block
    low = low_lanes(block)
    pair = pl.program_id(0)
    width = res_ref.shape[1] // 3
    at_q = pl.multiple_of(pair * 128, 128)
    at_k = pl.multiple_of(width + pair * 128, 128)
    at_v = pl.multiple_of(2 * width + pair * 128, 128)

    def front(i):
        queries = two_heads(q_ref, i * block, block)
        grads = two_heads(grad_ref, i * block, block)
        scores = mask_scores(dot_nt(queries, k_ref[...]), seg_q, seg_k, i * block, block)
        return queries, grads, scores, dot_nt(grads, v_ref[...])

    current = front(0)
    for i in range(count):
        later = front(i + 1) if i + 1 < count else None
        queries, grads, scores, probs_grad = current
        rows = pl.ds(i * block, block)
        lse = lse_ref[0, rows, :]
        lse = jnp.concatenate([lse[:, 0:1], lse[:, 1:2]], axis=0)
        inner = grad_ref[rows, :].astype(F32) * out_ref[rows, :].astype(F32)
        zero = jnp.zeros_like(inner)
        inner = jnp.concatenate(
            [
                jnp.sum(jnp.where(low, inner, zero), axis=1, keepdims=True),
                jnp.sum(jnp.where(low, zero, inner), axis=1, keepdims=True),
            ],
            axis=0,
        )
        probs = jnp.exp(scores - lse)
        score_grad = (probs * (probs_grad - inner)).astype(BF16)
        q_grad = dot_nn(score_grad, k_ref[...])
        q_grad = jnp.where(low, q_grad[:block], q_grad[block:]).astype(BF16).astype(F32)
        res_ref[rows, pl.ds(at_q, 128)] = (q_grad * 0.125).astype(BF16)
        v_part = dot_nn(grads.T, probs.astype(BF16))
        k_part = dot_nn(queries.T, score_grad)
        if i == 0:
            k_sum[...] = k_part
            v_sum[...] = v_part
        else:
            k_sum[...] += k_part
            v_sum[...] += v_part
        current = later
    res_ref[:, pl.ds(at_k, 128)] = k_sum[...].T.astype(BF16)
    res_ref[:, pl.ds(at_v, 128)] = v_sum[...].T.astype(BF16)


def attention_specs(length, width, masked):
    pairs = width // 128
    column = lambda first: pl.BlockSpec((length, 128), lambda p: (0, first + p))
    segs = [
        pl.BlockSpec((length, 1), lambda p: (0, 0)),
        pl.BlockSpec((1, length), lambda p: (0, 0)),
    ]
    qkv = [column(0), column(pairs), column(2 * pairs)]
    stat = pl.BlockSpec((1, length, 2), lambda p: (p, 0, 0))
    return pairs, column, (segs if masked else []) + qkv, stat


def attend(qkv, segs, block):
    length, width = qkv.shape[0], qkv.shape[1] // 3
    masked = len(segs) > 0
    pairs, column, ins, stat = attention_specs(length, width, masked)
    work = 2 * pairs * length * length
    return pl.pallas_call(
        functools.partial(forward_kernel, block=block, masked=masked),
        grid=(pairs,),
        in_specs=ins,
        out_specs=[column(0), stat],
        out_shape=[
            jax.ShapeDtypeStruct((length, width), BF16),
            jax.ShapeDtypeStruct((pairs, length, 2), F32),
        ],
        compiler_params=pltpu.CompilerParams(vmem_limit_bytes=56 << 20),
        cost_estimate=pl.CostEstimate(
            flops=work * 64 * 16, bytes_accessed=length * width * 8, transcendentals=work
        ),
    )(*segs, qkv, qkv, qkv)


def attend_back(qkv, out, grad, lse, segs, block, first=()):
    length, width = qkv.shape[0], qkv.shape[1] // 3
    masked = len(segs) > 0
    pairs, column, ins, stat = attention_specs(length, width, masked)
    work = 2 * pairs * length * length
    return pl.pallas_call(
        functools.partial(backward_kernel, block=block, masked=masked, first=len(first)),
        grid=(pairs,),
        in_specs=ins
        + [column(0), column(0), stat]
        + [pl.BlockSpec(memory_space=pl.ANY)] * len(first),
        out_specs=pl.BlockSpec((length, 3 * width), lambda p: (0, 0)),
        out_shape=jax.ShapeDtypeStruct((length, 3 * width), BF16),
        scratch_shapes=[pltpu.VMEM((128, length), F32)] * 2,
        compiler_params=pltpu.CompilerParams(vmem_limit_bytes=56 << 20),
        cost_estimate=pl.CostEstimate(
            flops=work * 64 * 40, bytes_accessed=length * width * 16, transcendentals=work
        ),
    )(*segs, qkv, qkv, qkv, out, grad, lse, *first)


def sincos_table(count_pos, count_col):
    position = np.arange(count_pos).astype(np.float32)[:, None]
    column = np.arange(count_col)
    exponent = (2 * (column // 2)).astype(np.float32) / np.float32(count_col)
    angles = position / np.power(np.float32(10000.0), exponent)[None, :]
    table = np.where(column[None, :] % 2 == 0, np.sin(angles), np.cos(angles))
    return table.astype(np.float32)


VMEM_ALL = pltpu.CompilerParams(vmem_limit_bytes=56 << 20)


def shape(rows, cols, dtype):
    return jax.ShapeDtypeStruct((rows, cols), dtype)


def cost(flops, moved, special=0):
    return pl.CostEstimate(flops=flops, bytes_accessed=moved, transcendentals=special)


def norm_parts(values):
    average = jnp.mean(values, axis=-1, keepdims=True)
    centred = values - average
    variance = jnp.mean(centred * centred, axis=-1, keepdims=True)
    inv_std = lax.rsqrt(variance + NORM_EPS)
    return centred * inv_std, inv_std


def norm_back(gradient, normed, inv_std, gain):
    scaled = gradient * gain
    return inv_std * (
        scaled
        - jnp.mean(scaled, axis=-1, keepdims=True)
        - normed * jnp.mean(scaled * normed, axis=-1, keepdims=True)
    )


def column_sum(values):
    return jnp.sum(values, axis=0, keepdims=True)


def mm_grad(left, right):
    return jnp.einsum("sk,sn->kn", left, right, preferred_element_type=F32)


def gelu_parts(u):
    cdf = 0.5 + 0.5 * lax.erf(u * 0.7071067811865476)
    bell = jnp.exp(u * u * -0.5)
    return u * cdf, cdf + u * (bell * 0.3989422804014327)


class Vectors:
    def __init__(self, arrays):
        self.at, self.size, total = {}, {}, 0
        for name, array in arrays.items():
            self.at[name], self.size[name] = total, array.shape[0]
            total += array.shape[0]
        self.total = total
        self.row = jnp.concatenate(list(arrays.values())).astype(F32).reshape(1, total)

    def of(self, ref, name, first=0, count=None):
        at = self.at[name] + first
        return ref[:, at : at + (self.size[name] - first if count is None else count)]


def group_kernel(place, weight, *outs):
    width = weight.shape[1] // 3
    part = width // 4
    for g in range(4):
        cols = []
        for c in range(3):
            cols.append(weight[:, c * width + g * part : c * width + (g + 1) * part])
            cols.append(jnp.zeros((weight.shape[0], 256 - part), BF16))
        piece = jnp.concatenate(cols, axis=1)
        for k in range(4):

            @pl.when((place[0] + k) % 4 == g)
            def _():
                outs[k][...] = piece


def group_pieces(weight, place):
    rows = weight.shape[0]
    return pl.pallas_call(
        group_kernel,
        grid_spec=pltpu.PrefetchScalarGridSpec(
            num_scalar_prefetch=1,
            grid=(1,),
            in_specs=[pl.BlockSpec(weight.shape, lambda i, s: (0, 0))],
            out_specs=[pl.BlockSpec((rows, 768), lambda i, s: (0, 0))] * 4,
        ),
        out_shape=[shape(rows, 768, BF16)] * 4,
        compiler_params=VMEM_ALL,
    )(place, weight)


def enc_in_kernel(place, *refs, vectors):
    inputs, pieces, vec = refs[:4], refs[4:8], refs[8]
    qkv_ref, low_ref, weight_ref = refs[9:]
    rows, tokens = pieces[0].shape[0], inputs[0].shape[0]
    for k in range(4):
        to = pl.multiple_of(((place[0] + 4 - k) % 4) * rows, 16)
        weight_ref[pl.ds(to, rows), :] = pieces[k][...]
    biases = []
    for first in (0, 768):
        groups = [vectors.of(vec, "enc_qv_bias", first + g * 192, 192) for g in range(4)]
        biases += [pick(groups, place[0]), jnp.zeros((1, 64), F32)]
    bias = jnp.concatenate(biases[:2] + [jnp.zeros((1, 256), F32)] + biases[2:], axis=1)
    scale = jnp.where(lax.broadcasted_iota(jnp.int32, (1, 768), 1) < 256, 0.125, 1.0)
    gain, offset = vectors.of(vec, "enc_norm1_gain"), vectors.of(vec, "enc_norm1_shift")
    for k in range(4):
        normed, _ = norm_parts(inputs[k][...].astype(F32))
        low = (normed * gain + offset).astype(BF16)
        out = pl.ds(k * tokens, tokens)
        low_ref[out, :] = low
        qkv_ref[out, :] = ((dot_nn(low, weight_ref[...]) + bias) * scale).astype(BF16)


def enc_in(inputs, pieces, vectors, place):
    tokens, width = inputs[0].shape
    rows = 4 * tokens
    whole = lambda a: pl.BlockSpec(a.shape, lambda i, s: (0, 0))
    outs = [shape(rows, 768, BF16), shape(rows, width, BF16), shape(width, 768, BF16)]
    return pl.pallas_call(
        functools.partial(enc_in_kernel, vectors=vectors),
        grid_spec=pltpu.PrefetchScalarGridSpec(
            num_scalar_prefetch=1,
            grid=(1,),
            in_specs=[whole(a) for a in (*inputs, *pieces, vectors.row)],
            out_specs=[whole(a) for a in outs],
        ),
        out_shape=outs,
        compiler_params=VMEM_ALL,
        cost_estimate=cost(2 * rows * width * 768, rows * width * 8),
    )(place, *inputs, *pieces, vectors.row)


def restack(wide, stacked):
    for b in range(4):
        stacked[b * 192 : (b + 1) * 192, :] = wide[:, b * 768 : (b + 1) * 768]


MATRIX_SPECS = [
    pl.BlockSpec((768, 768), lambda j, s: (0, 4)),
    pl.BlockSpec((768, 768), lambda j, s: (0, 5 + j)),
    pl.BlockSpec((192, 3072), lambda j, s: (j, 0)),
]


def enc_block_kernel(place, *refs, vectors):
    parts, (x, proj, fc1, fc2, to_dec, send_map, vec) = refs[:4], refs[4:11]
    att_ref, x1_ref, low_ref, act_ref, slope_ref, y_ref, send_ref, total, stacked = refs[11:]
    step = pl.program_id(0)

    @pl.when(step == 0)
    def _():
        groups = [part[...] for part in parts]
        att = jnp.concatenate([pick(groups, (place[0] + 4 - g) % 4) for g in range(4)], axis=1)
        att_ref[...] = att
        x1 = x[...].astype(F32) + (dot_nn(att, proj[...]) + vectors.of(vec, "enc_proj_bias"))
        x1_ref[...] = x1
        normed, _ = norm_parts(x1)
        gain, offset = vectors.of(vec, "enc_norm2_gain"), vectors.of(vec, "enc_norm2_shift")
        low_ref[...] = (normed * gain + offset).astype(BF16)
        total[...] = x1 + vectors.of(vec, "enc_fc2_bias")

    bias = pick([vectors.of(vec, "enc_fc1_bias", j * 768, 768) for j in range(4)], step)
    pre = dot_nn(low_ref[...], fc1[...]) + bias
    act, slope = gelu_parts(pre)
    act = act.astype(BF16)
    act_ref[...] = act
    slope_ref[...] = slope.astype(BF16)
    restack(fc2, stacked)
    total[...] += dot_nn(act, stacked[...])

    @pl.when(step == 3)
    def _():
        y = total[...].astype(BF16)
        y_ref[...] = y
        reduced = dot_nn(y, to_dec[...]).astype(BF16)
        send = dot_nn(send_map[...], reduced).astype(BF16)
        for k in range(4):
            send_ref[k] = send[k * CAP : (k + 1) * CAP, :]


def enc_block(parts, x, matrices, to_dec, send_map, vectors, place):
    rows, width = x.shape
    whole = lambda a: pl.BlockSpec(a.shape, lambda j, s: (0,) * len(a.shape))
    chunk = pl.BlockSpec((rows, 768), lambda j, s: (0, j))
    outs = [
        shape(rows, width, BF16),
        shape(rows, width, F32),
        shape(rows, width, BF16),
        shape(rows, 4 * width, BF16),
        shape(rows, 4 * width, BF16),
        shape(rows, width, BF16),
        jax.ShapeDtypeStruct((4, CAP, DD), BF16),
    ]
    return pl.pallas_call(
        functools.partial(enc_block_kernel, vectors=vectors),
        grid_spec=pltpu.PrefetchScalarGridSpec(
            num_scalar_prefetch=1,
            grid=(4,),
            in_specs=[whole(a) for a in (*parts, x)]
            + MATRIX_SPECS
            + [whole(a) for a in (to_dec, send_map, vectors.row)],
            out_specs=[
                chunk if a.shape[-1] == 4 * width else whole(a) for a in outs
            ],
            scratch_shapes=[pltpu.VMEM((rows, width), F32), pltpu.VMEM((width, width), BF16)],
        ),
        out_shape=outs,
        compiler_params=VMEM_ALL,
        cost_estimate=cost(rows * width * width * 20, width * width * 20, rows * width * 8),
    )(place, *parts, x, *[matrices] * 3, to_dec, send_map, vectors.row)


def enc_block_back_kernel(place, *refs, vectors, first):
    parts, (send_map, to_dec, x1, slope, proj, fc1, fc2, vec) = refs[:4], refs[4:12]
    refs = refs[:12] + refs[12 + first :]
    reduced_ref, gz_ref, gpre_ref, gx1_ref, go_ref = refs[12:17]
    gatt_refs, (fc1_b, fc2_b, gain_g, shift_g, proj_b) = refs[17:21], refs[21:26]
    gy, back, stacked = refs[-3:]
    step = pl.program_id(0)

    @pl.when(step == 0)
    def _():
        rows = jnp.concatenate([part[...] for part in parts], axis=0)
        reduced = dot_nn(send_map[...], rows).astype(BF16)
        reduced_ref[...] = reduced
        grad = dot_nt(reduced, to_dec[...])
        gy[...] = grad
        gz_ref[...] = grad.astype(BF16)
        fc2_b[...] = column_sum(grad.astype(BF16).astype(F32))
        back[...] = jnp.zeros_like(back)

    restack(fc2, stacked)
    gpre = (dot_nt(gz_ref[...], stacked[...]) * slope[...].astype(F32)).astype(BF16)
    gpre_ref[...] = gpre
    fc1_b[...] = column_sum(gpre.astype(F32))
    back[...] += dot_nt(gpre, fc1[...])

    @pl.when(step == 3)
    def _():
        normed, inv_std = norm_parts(x1[...])
        total = back[...]
        gain_g[...] = column_sum(total * normed)
        shift_g[...] = column_sum(total)
        gx1 = gy[...] + norm_back(total, normed, inv_std, vectors.of(vec, "enc_norm2_gain"))
        gx1_ref[...] = gx1
        go = gx1.astype(BF16)
        go_ref[...] = go
        proj_b[...] = column_sum(go.astype(F32))
        gatt = dot_nt(go, proj[...]).astype(BF16)
        groups = [gatt[:, g * 192 : (g + 1) * 192] for g in range(4)]
        for k in range(4):
            gatt_refs[k][...] = pick(groups, (place[0] + k) % 4)


def enc_block_back(parts, send_map, to_dec, x1, slope, matrices, vectors, place, first=()):
    rows, width = x1.shape
    whole = lambda a: pl.BlockSpec(a.shape, lambda j, s: (0,) * len(a.shape))
    outs = [
        shape(rows, DD, BF16),
        shape(rows, width, BF16),
        shape(rows, 4 * width, BF16),
        shape(rows, width, F32),
        shape(rows, width, BF16),
        *[shape(rows, 192, BF16)] * 4,
        shape(1, 4 * width, F32),
        *[shape(1, width, F32)] * 4,
    ]
    by_chunk = lambda a: pl.BlockSpec((a.shape[0], 768), lambda j, s: (0, j))
    return pl.pallas_call(
        functools.partial(enc_block_back_kernel, vectors=vectors, first=len(first)),
        grid_spec=pltpu.PrefetchScalarGridSpec(
            num_scalar_prefetch=1,
            grid=(4,),
            in_specs=[whole(a) for a in (*parts, send_map, to_dec, x1)]
            + [by_chunk(slope), *MATRIX_SPECS, whole(vectors.row)]
            + [pl.BlockSpec(memory_space=pl.ANY)] * len(first),
            out_specs=[by_chunk(a) if a.shape[-1] == 4 * width else whole(a) for a in outs],
            scratch_shapes=[pltpu.VMEM((rows, width), F32)] * 2
            + [pltpu.VMEM((width, width), BF16)],
        ),
        out_shape=outs,
        compiler_params=VMEM_ALL,
        cost_estimate=cost(rows * width * width * 20, width * width * 20),
    )(place, *parts, send_map, to_dec, x1, slope, *[matrices] * 3, vectors.row, *first)


def enc_in_back_kernel(*refs, vectors):
    inputs, (grad, weight, vec) = refs[:4], refs[4:7]
    own_ref, others, (gain_g, shift_g, grad_sum) = refs[7], refs[8:11], refs[11:]
    tokens = inputs[0].shape[0]
    gains = shifts = 0.0
    for k in range(4):
        part = dot_nt(grad[pl.ds(k * tokens, tokens), :], weight[...])
        normed, _ = norm_parts(inputs[k][...].astype(F32))
        gains = gains + column_sum(part * normed)
        shifts = shifts + column_sum(part)
        if k == 0:
            own_ref[...] = part
        else:
            others[k - 1][...] = part.astype(BF16)
    gain_g[...] = gains
    shift_g[...] = shifts
    grad_sum[...] = column_sum(grad[...].astype(F32))


def enc_in_back(inputs, grad, weight, vectors):
    tokens, width = inputs[0].shape
    outs = [shape(tokens, width, F32)] + [shape(tokens, width, BF16)] * 3
    outs += [shape(1, width, F32)] * 2 + [shape(1, 768, F32)]
    return pl.pallas_call(
        functools.partial(enc_in_back_kernel, vectors=vectors),
        out_shape=outs,
        compiler_params=VMEM_ALL,
        cost_estimate=cost(8 * tokens * width * 768, tokens * width * 32),
    )(*inputs, grad, weight, vectors.row)


def enc_end_kernel(x, gx1, own, a, b, c, vec, out, *, vectors):
    normed, inv_std = norm_parts(x[...].astype(F32))
    back = own[...] + (a[...].astype(F32) + b[...].astype(F32) + c[...].astype(F32))
    out[...] = gx1[...] + norm_back(back, normed, inv_std, vectors.of(vec, "enc_norm1_gain"))


def enc_end(x, gx1, back, vectors):
    return pl.pallas_call(
        functools.partial(enc_end_kernel, vectors=vectors),
        out_shape=shape(*x.shape, F32),
        compiler_params=VMEM_ALL,
    )(x, gx1, *back, vectors.row)


def dec_in_kernel(*refs, vectors):
    parts, (restore, slots, table, weight, vec) = refs[:4], refs[4:9]
    grid_ref, low_ref, qkv_ref = refs[9:]
    rows = jnp.concatenate([part[...] for part in parts], axis=0)
    order = restore[...]
    hot = jnp.where(order == slots[...], 1.0, 0.0).astype(BF16)
    placed = dot_nn(hot, rows)
    grid = placed + jnp.where(order >= VIS, vectors.of(vec, "mask_token"), 0.0) + table[...]
    grid_ref[...] = grid
    normed, _ = norm_parts(grid)
    low = normed * vectors.of(vec, "dec_norm1_gain") + vectors.of(vec, "dec_norm1_shift")
    low = low.astype(BF16)
    low_ref[...] = low
    packed = dot_nn(low, weight[...])
    queries = packed[:, :DD] + vectors.of(vec, "dec_qv_bias", 0, DD)
    qkv_ref[:, :DD] = (queries * 0.125).astype(BF16)
    qkv_ref[:, DD : 2 * DD] = packed[:, DD : 2 * DD].astype(BF16)
    values = packed[:, 2 * DD :] + vectors.of(vec, "dec_qv_bias", DD, DD)
    qkv_ref[:, 2 * DD :] = values.astype(BF16)


def dec_in(parts, restore, slots, table, weight, vectors, tile):
    rows = table.shape[0]
    row = lambda n: pl.BlockSpec((tile, n), lambda i: (i, 0))
    whole = lambda a: pl.BlockSpec(a.shape, lambda i: (0, 0))
    return pl.pallas_call(
        functools.partial(dec_in_kernel, vectors=vectors),
        grid=(rows // tile,),
        in_specs=[whole(a) for a in parts]
        + [row(1), whole(slots), row(DD), whole(weight), whole(vectors.row)],
        out_specs=[row(DD), row(DD), row(3 * DD)],
        out_shape=[shape(rows, DD, F32), shape(rows, DD, BF16), shape(rows, 3 * DD, BF16)],
        compiler_params=VMEM_ALL,
        cost_estimate=cost(rows * DD * DD * 8, rows * DD * 16),
    )(*parts, restore, slots, table, weight, vectors.row)


def dec_in_back_kernel(grad, weight, grid, gx1, restore, slots, vec, *outs, vectors):
    slot_refs, (gain_g, shift_g, mask_g, grad_sum, total) = outs[:4], outs[4:]
    step = pl.program_id(0)

    @pl.when(step == 0)
    def _():
        for ref in (gain_g, shift_g, mask_g, grad_sum, total):
            ref[...] = jnp.zeros_like(ref)

    back = dot_nt(grad[...], weight[...])
    normed, inv_std = norm_parts(grid[...])
    gain_g[...] += column_sum(back * normed)
    shift_g[...] += column_sum(back)
    grad_sum[...] += column_sum(grad[...].astype(F32))
    gx = gx1[...] + norm_back(back, normed, inv_std, vectors.of(vec, "dec_norm1_gain"))
    order = restore[0]
    hot = jnp.where(slots[...] == order, 1.0, 0.0).astype(BF16)
    total[...] += dot_nn(hot, gx.astype(BF16))
    masked = jnp.where(order >= VIS, 1.0, 0.0)
    ones = jnp.broadcast_to(masked, (8, masked.shape[1]))
    mask_g[...] += lax.dot_general(
        ones,
        gx,
        (((1,), (0,)), ((), ())),
        preferred_element_type=F32,
        precision=lax.Precision.HIGHEST,
    )[0:1, :]

    @pl.when(step == pl.num_programs(0) - 1)
    def _():
        for k in range(4):
            slot_refs[k][...] = total[k * CAP : (k + 1) * CAP, :].astype(BF16)


def dec_in_back(grad, weight, grid, gx1, restore, slots, vectors, tile):
    rows = grid.shape[0]
    row = lambda n: pl.BlockSpec((tile, n), lambda i: (i, 0))
    whole = lambda shape: pl.BlockSpec(shape, lambda i: (0, 0))
    sums = [DD, DD, DD, 3 * DD]
    return pl.pallas_call(
        functools.partial(dec_in_back_kernel, vectors=vectors),
        grid=(rows // tile,),
        in_specs=[
            row(3 * DD),
            whole(weight.shape),
            row(DD),
            row(DD),
            pl.BlockSpec((1, 1, tile), lambda i: (i, 0, 0)),
            whole(slots.shape),
            whole(vectors.row.shape),
        ],
        out_specs=[whole((CAP, DD))] * 4 + [whole((1, n)) for n in sums],
        out_shape=[shape(CAP, DD, BF16)] * 4 + [shape(1, n, F32) for n in sums],
        scratch_shapes=[pltpu.VMEM((4 * CAP, DD), F32)],
        compiler_params=VMEM_ALL,
        cost_estimate=cost(rows * DD * DD * 8, rows * DD * 16),
    )(grad, weight, grid, gx1, restore, slots, vectors.row)


def dec_block_kernel(x, att, proj, fc1, fc2, vec, *outs, vectors, chunk):
    x1_ref, low_ref, act_ref, slope_ref, y_ref = outs
    x1 = x[...] + (dot_nn(att[...], proj[...]) + vectors.of(vec, "dec_proj_bias"))
    x1_ref[...] = x1
    normed, _ = norm_parts(x1)
    low = normed * vectors.of(vec, "dec_norm2_gain") + vectors.of(vec, "dec_norm2_shift")
    low = low.astype(BF16)
    low_ref[...] = low
    total = x1 + vectors.of(vec, "dec_fc2_bias")
    hidden = fc1.shape[1]

    def pre_of(c):
        return dot_nn(low, fc1[:, c : c + chunk]) + vectors.of(vec, "dec_fc1_bias", c, chunk)

    pre = pre_of(0)
    for c in range(0, hidden, chunk):
        later = pre_of(c + chunk) if c + chunk < hidden else None
        act, slope = gelu_parts(pre)
        act = act.astype(BF16)
        act_ref[:, c : c + chunk] = act
        slope_ref[:, c : c + chunk] = slope.astype(BF16)
        total = total + dot_nn(act, fc2[c : c + chunk, :])
        pre = later
    y_ref[...] = total.astype(BF16)


def dec_block(x, att, proj, fc1, fc2, vectors, tile, chunk):
    rows, width = x.shape
    hidden = fc1.shape[1]
    row = lambda n: pl.BlockSpec((tile, n), lambda i: (i, 0))
    whole = lambda a: pl.BlockSpec(a.shape, lambda i: (0, 0))
    shapes = [(width, F32), (width, BF16), (hidden, BF16), (hidden, BF16), (width, BF16)]
    return pl.pallas_call(
        functools.partial(dec_block_kernel, vectors=vectors, chunk=chunk),
        grid=(rows // tile,),
        in_specs=[row(width), row(width)] + [whole(a) for a in (proj, fc1, fc2, vectors.row)],
        out_specs=[row(n) for n, _ in shapes],
        out_shape=[shape(rows, n, t) for n, t in shapes],
        compiler_params=VMEM_ALL,
        cost_estimate=cost(rows * hidden * width * 10, rows * hidden * 10, rows * hidden * 2),
    )(x, att, proj, fc1, fc2, vectors.row)


def dec_block_back_kernel(gy, x1, slope, proj, fc1, fc2, vec, *outs, vectors, chunk):
    gpre_ref, gx1_ref, go_ref, gatt_ref, fc1_b, fc2_b, gain_g, shift_g, proj_b = outs

    @pl.when(pl.program_id(0) == 0)
    def _():
        for ref in (fc1_b, fc2_b, gain_g, shift_g, proj_b):
            ref[...] = jnp.zeros_like(ref)

    gz = gy[...]
    fc2_b[...] += column_sum(gz.astype(F32))
    hidden = fc1.shape[1]
    grad = dot_nt(gz, fc2[:chunk, :])
    back = None
    for c in range(0, hidden, chunk):
        later = None
        if c + chunk < hidden:
            later = dot_nt(gz, fc2[c + chunk : c + 2 * chunk, :])
        gpre = (grad * slope[:, c : c + chunk].astype(F32)).astype(BF16)
        gpre_ref[:, c : c + chunk] = gpre
        fc1_b[:, c : c + chunk] += column_sum(gpre.astype(F32))
        part = dot_nt(gpre, fc1[:, c : c + chunk])
        back = part if back is None else back + part
        grad = later
    normed, inv_std = norm_parts(x1[...])
    gain_g[...] += column_sum(back * normed)
    shift_g[...] += column_sum(back)
    gx1 = gz.astype(F32) + norm_back(
        back, normed, inv_std, vectors.of(vec, "dec_norm2_gain")
    )
    gx1_ref[...] = gx1
    go = gx1.astype(BF16)
    go_ref[...] = go
    proj_b[...] += column_sum(go.astype(F32))
    gatt_ref[...] = dot_nt(go, proj[...]).astype(BF16)


def dec_block_back(gy, x1, slope, proj, fc1, fc2, vectors, tile, chunk):
    rows, width = x1.shape
    hidden = fc1.shape[1]
    row = lambda n: pl.BlockSpec((tile, n), lambda i: (i, 0))
    whole = lambda shape: pl.BlockSpec(shape, lambda i: (0, 0))
    consts = [proj, fc1, fc2, vectors.row]
    shapes = [(hidden, BF16), (width, F32), (width, BF16), (width, BF16)]
    sums = [hidden, width, width, width, width]
    return pl.pallas_call(
        functools.partial(dec_block_back_kernel, vectors=vectors, chunk=chunk),
        grid=(rows // tile,),
        in_specs=[row(width), row(width), row(hidden)] + [whole(a.shape) for a in consts],
        out_specs=[row(n) for n, _ in shapes] + [whole((1, n)) for n in sums],
        out_shape=[shape(rows, n, t) for n, t in shapes] + [shape(1, n, F32) for n in sums],
        compiler_params=VMEM_ALL,
        cost_estimate=cost(rows * hidden * width * 10, rows * hidden * 8),
    )(gy, x1, slope, *consts)


def body(
    encoder_input,
    seg_ids,
    vis_slot,
    restore_order,
    enc_norm1_gain,
    enc_norm1_shift,
    enc_qkv_weight,
    enc_qv_bias,
    enc_proj_weight,
    enc_proj_bias,
    enc_norm2_gain,
    enc_norm2_shift,
    enc_fc1_weight,
    enc_fc1_bias,
    enc_fc2_weight,
    enc_fc2_bias,
    to_dec_weight,
    mask_token,
    dec_norm1_gain,
    dec_norm1_shift,
    dec_qkv_weight,
    dec_qv_bias,
    dec_proj_weight,
    dec_proj_bias,
    dec_norm2_gain,
    dec_norm2_shift,
    dec_fc1_weight,
    dec_fc1_bias,
    dec_fc2_weight,
    dec_fc2_bias,
    out_grad,
):
    x_at = lax.axis_index("x")
    core = lax.axis_index("core")
    place = place_of(("x",))
    tokens, width = encoder_input.shape[1:]
    hw = width // 4
    vectors = Vectors(
        {
            "enc_norm1_gain": enc_norm1_gain,
            "enc_norm1_shift": enc_norm1_shift,
            "enc_qv_bias": enc_qv_bias,
            "enc_proj_bias": enc_proj_bias,
            "enc_norm2_gain": enc_norm2_gain,
            "enc_norm2_shift": enc_norm2_shift,
            "enc_fc1_bias": enc_fc1_bias,
            "enc_fc2_bias": enc_fc2_bias,
            "mask_token": mask_token,
            "dec_norm1_gain": dec_norm1_gain,
            "dec_norm1_shift": dec_norm1_shift,
            "dec_qv_bias": dec_qv_bias,
            "dec_proj_bias": dec_proj_bias,
            "dec_norm2_gain": dec_norm2_gain,
            "dec_norm2_shift": dec_norm2_shift,
            "dec_fc1_bias": dec_fc1_bias,
            "dec_fc2_bias": dec_fc2_bias,
        }
    )

    pieces = exchange(group_pieces(enc_qkv_weight, place), "x")
    own_input = encoder_input[0]
    inputs = spread(own_input, "x")

    eighth = hw // 8
    first_row = (core * 4 + lax.axis_index("y")) * eighth
    rows_of = lambda weight, first: lax.dynamic_slice_in_dim(weight, first, eighth, 0)
    strip = [rows_of(enc_fc2_weight, first_row + b * hw) for b in range(4)]
    strip += [rows_of(enc_proj_weight, first_row), rows_of(enc_fc1_weight, first_row)]
    matrices = lax.all_gather(
        jnp.concatenate(strip, axis=1), ("x", "core", "y"), axis=0, tiled=True
    )

    row_seg = seg_ids[0].reshape(4, tokens)
    row_slot = vis_slot[0].reshape(4, tokens)
    position = jnp.arange(tokens)
    earlier = position[None, :] < position[:, None]
    same_clip = row_seg[:, :, None] == row_seg[:, None, :]
    ranks = jnp.sum(jnp.logical_and(same_clip, earlier), axis=-1)
    turn = (x_at - jnp.arange(4)) % 4
    seg_turned = jnp.take(row_seg, turn, axis=0)
    segs = (seg_turned.reshape(4 * tokens, 1), seg_turned.reshape(1, 4 * tokens))
    own_seg = lax.dynamic_index_in_dim(row_seg, x_at, 0, keepdims=False)
    own_rank = lax.dynamic_index_in_dim(ranks, x_at, 0, keepdims=False)
    cap_index = jnp.arange(4 * CAP)
    clip_to = (x_at + cap_index // CAP) % 4
    send_map = jnp.logical_and(
        own_seg[None, :] == clip_to[:, None],
        own_rank[None, :] == (cap_index % CAP)[:, None],
    ).astype(BF16)
    send_back = jnp.logical_and(
        own_seg[:, None] == clip_to[None, :],
        own_rank[:, None] == (cap_index % CAP)[None, :],
    ).astype(BF16)
    chosen = jnp.logical_and(
        seg_turned[:, None, :] == x_at,
        jnp.take(ranks, turn, axis=0)[:, None, :] == jnp.arange(CAP)[None, :, None],
    )
    slot_turned = jnp.take(row_slot, turn, axis=0)
    slot_vis = jnp.sum(jnp.where(chosen, slot_turned[:, None, :] + 1, 0), axis=-1) - 1
    restore_row = restore_order[0, 0]
    restore_col = restore_row[:, None]
    restore_row = restore_row.reshape(2, 1, FULL // 2)
    table = jnp.asarray(sincos_table(FULL, DD))

    qkv, first_in, qkv_mine = enc_in(inputs, pieces, vectors, place)
    att_mine, enc_lse = attend(qkv, segs, 128)
    blocks = att_mine.reshape(4, tokens, 256)
    parts = exchange([blocks[(4 - k) % 4, :, :hw] for k in range(4)], "x")
    attended, enc_x1, second_in, enc_act, enc_slope, enc_low, send_rows = enc_block(
        parts, own_input, matrices, to_dec_weight, send_map, vectors, place
    )

    received = exchange([send_rows[k] for k in range(4)], "x")
    grid, dec_in_low, dec_qkv = dec_in(
        received,
        restore_col,
        slot_vis.reshape(1, 4 * CAP),
        table,
        dec_qkv_weight,
        vectors,
        FULL // 2,
    )
    dec_att, dec_lse = attend(dec_qkv, (), 224)
    dec_x1, dec_second, dec_act, dec_slope, dec_out = dec_block(
        grid, dec_att, dec_proj_weight, dec_fc1_weight, dec_fc2_weight, vectors, FULL // 2, 512
    )

    dec_gz = out_grad[0, 0]
    dec_gpre, dec_gx1, dec_go, dec_gatt, *dec_sums = dec_block_back(
        dec_gz,
        dec_x1,
        dec_slope,
        dec_proj_weight,
        dec_fc1_weight,
        dec_fc2_weight,
        vectors,
        FULL // 2,
        512,
    )
    dec_fc1_b, dec_fc2_b, dec_gain2_g, dec_shift2_g, dec_proj_b = dec_sums
    dec_gqkv = attend_back(dec_qkv, dec_att, dec_gatt, dec_lse, (), 112)
    *slot_grads, dec_gain1_g, dec_shift1_g, mask_g, dec_gqkv_sum = dec_in_back(
        dec_gqkv,
        dec_qkv_weight,
        grid,
        dec_gx1,
        restore_row,
        slot_vis.reshape(4 * CAP, 1),
        vectors,
        FULL // 2,
    )
    low_grad = lambda left, right: mm_grad(left, right).astype(BF16)

    returned = exchange(slot_grads, "x", -1)
    reduced_grad, enc_gz, enc_gpre, enc_gx1, enc_go, *rest = enc_block_back(
        returned,
        send_back,
        to_dec_weight,
        enc_x1,
        enc_slope,
        matrices,
        vectors,
        place,
    )
    gatt_parts, enc_sums = rest[:4], rest[4:]
    enc_fc1_b, enc_fc2_b, enc_gain2_g, enc_shift2_g, enc_proj_b = enc_sums
    columns = lambda array, which: lax.dynamic_slice_in_dim(
        array, which * (array.shape[1] // 2), array.shape[1] // 2, 1
    )

    def halves(make):
        return make(core), make(1 - core)

    early = (
        low_grad(enc_low, reduced_grad),
        low_grad(second_in, enc_gpre),
        low_grad(enc_act, enc_gz),
    )
    gatt_mine = jnp.concatenate(exchange(gatt_parts, "x"), axis=0)
    gatt_mine = jnp.pad(gatt_mine, ((0, 0), (0, 64)))
    def finish():
        gqkv = attend_back(qkv, att_mine, gatt_mine, enc_lse, segs, 128, early)
        own_back, *others, gain1_g, shift1_g, gqkv_sum = enc_in_back(
            inputs, gqkv, qkv_mine, vectors
        )

        qv = jnp.zeros((2, 4, hw), F32)
        qv = lax.dynamic_update_index_in_dim(
            qv, jnp.stack([gqkv_sum[0, :hw], gqkv_sum[0, 512 : 512 + hw]]), x_at, 1
        )
        small = [
            gain1_g,
            shift1_g,
            qv.reshape(1, 2 * width),
            enc_proj_b,
            enc_gain2_g,
            enc_shift2_g,
            enc_fc1_b,
            enc_fc2_b,
            mask_g,
            dec_gain1_g,
            dec_shift1_g,
            dec_gqkv_sum[:, :DD],
            dec_gqkv_sum[:, 2 * DD :],
            dec_proj_b,
            dec_gain2_g,
            dec_shift2_g,
            dec_fc1_b,
            dec_fc2_b,
        ]
        sizes = [v.shape[1] for v in small]
        vector = jnp.concatenate([*small, jnp.zeros((1, 14336 - sum(sizes)), F32)], axis=1)
        terms = spread(vector.reshape(112, 128), "x")
        vector = ((terms[0] + terms[1]) + (terms[2] + terms[3])).reshape(4, 56, 64)
        extra = lax.dynamic_index_in_dim(vector, x_at, 0, keepdims=False).astype(BF16)
        extra = jnp.pad(extra, ((0, width - 56), (0, 0)))

        def qkv_half(which):
            grad = low_grad(columns(first_in, which), gqkv)
            grad = [grad[:, c * 256 : c * 256 + hw] for c in range(3)]
            more = lax.dynamic_slice_in_dim(extra, which * (width // 2), width // 2, 0)
            return jnp.concatenate([*grad, more], axis=1)


        blocks = lambda grad: [grad[:, k * DD : (k + 1) * DD] for k in range(grad.shape[1] // DD)]
        proj = low_grad(attended, enc_go)
        first = blocks(low_grad(dec_in_low, dec_gqkv)) + [low_grad(dec_att, dec_go)]
        first += blocks(low_grad(dec_second, dec_gpre))
        last = [low_grad(dec_act, dec_gz)] + blocks(proj[:DD]) + blocks(proj[DD:])
        both = jnp.stack([jnp.concatenate(first, axis=0), jnp.concatenate(last, axis=0)])
        mine, other = halves(
            lambda which: lax.dynamic_index_in_dim(both, which, 0, keepdims=False)
        )
        dec_sum = sum_halves(mine, other, ("z", "y", "x"), lambda k, c: (4 * c + k, 0))
        qkv_sum, vec_sum = tail_sum(*halves(qkv_half))
        back = exchange([None, *others], "x", -1)
        gx = enc_end(own_input, enc_gx1, (own_back, *back[1:]), vectors)
        return dec_sum, qkv_sum, vec_sum, gx

    def nothing():
        return tuple(
            jnp.zeros(dims, F32)
            for dims in ((16 * DD, DD), (width, 3 * width), (width, 256), (tokens, width))
        )

    rest_grads = lax.psum(early, ALL)
    dec_sum, qkv_grad, vector, input_grad = lax.cond(seg_ids[0, 0] >= 0, finish, nothing)
    rows_of = lambda first, count: dec_sum[first * DD : (first + count) * DD]
    beside = lambda first, count: jnp.concatenate(
        [rows_of(first + k, 1) for k in range(count)], axis=1
    )
    proj_grad = jnp.concatenate([beside(12, 2), beside(14, 2)], axis=0)
    vector = vector[:56].reshape(56, 4, 64).transpose(1, 0, 2).reshape(14336)
    sizes = [width, width, 2 * width, width, width, width, 4 * width, width, DD]
    sizes += [DD, DD, 2 * DD, DD, DD, DD, 4 * DD, DD]
    cuts = [int(c) for c in np.cumsum(sizes)]
    v = jnp.split(vector, cuts)

    wide = lambda array: array.astype(F32)
    return (
        dec_out[None, None],
        input_grad[None],
        v[0],
        v[1],
        qkv_grad,
        v[2],
        proj_grad,
        v[3],
        v[4],
        v[5],
        wide(rest_grads[1]),
        v[6],
        wide(rest_grads[2]),
        v[7],
        wide(rest_grads[0]),
        v[8],
        v[9],
        v[10],
        beside(0, 3),
        v[11],
        rows_of(3, 1),
        v[12],
        v[13],
        v[14],
        beside(4, 4),
        v[15],
        rows_of(8, 4),
        v[16],
    )


def solution(mesh):
    fine = Mesh(mesh.devices.reshape(4, 4, 2, 4), ALL)
    row, shared, split = P(WIDE, None), P(), P("x", None)
    return jax.shard_map(
        body,
        mesh=fine,
        in_specs=(
            P(WIDE, "x", None),
            row,
            row,
            P(WIDE, "x", None),
            shared,
            shared,
            split,
            shared,
            split,
            shared,
            shared,
            shared,
            split,
            shared,
            split,
        )
        + (shared,) * 15
        + (P(WIDE, "x", None, None),),
        out_specs=(P(WIDE, "x", None, None), P(WIDE, "x", None)) + (shared,) * 26,
        check_vma=False,
    )
```

```python
import functools

import jax
import jax.numpy as jnp
import numpy as np
from jax import lax
from jax.experimental import pallas as pl
from jax.experimental.pallas import tpu as pltpu
from jax.sharding import Mesh
from jax.sharding import PartitionSpec as P

HEADS = 12
DD = 384
DHEADS = 6
VIS = 157
FULL = 1568
CAP = 64
NORM_EPS = 1e-06
NEG_LARGE = -1e30
ALL = ("z", "y", "core", "x")
WIDE = ("z", "y", "core")
F32 = jnp.float32
BF16 = jnp.bfloat16


def shift(value, axis, step):
    return lax.ppermute(value, axis, [(i, (i + step) % 4) for i in range(4)])


def swap(value):
    return lax.ppermute(value, "core", [(0, 1), (1, 0)])


def spread(piece, axis):
    across = shift(piece, axis, 2)
    return [piece, shift(piece, axis, 1), across, shift(piece, axis, 3)]


def exchange(pieces, axis, sign=1):
    far = shift(pieces[2], axis, 2)
    return [pieces[0], shift(pieces[1], axis, sign), far, shift(pieces[3], axis, -sign)]


def reduce_phase(current, axis):
    rows = current.shape[0] // 4
    index = lax.axis_index(axis)
    got = []
    for step in (2, 1, 3):
        piece = lax.dynamic_slice_in_dim(current, ((index + step) % 4) * rows, rows, 0)
        got.append(shift(piece.astype(BF16), axis, step).astype(F32))
    own = lax.dynamic_slice_in_dim(current, index * rows, rows, 0).astype(F32)
    return own + (got[0] + got[1] + got[2])


def sum_vector(vector):
    vector = vector + swap(vector)
    for axis in ("x", "y", "z"):
        parts = spread(vector, axis)
        vector = (parts[0] + parts[1]) + (parts[2] + parts[3])
    return vector


def pick(values, index):
    low = jnp.where(index == 0, values[0], values[1])
    high = jnp.where(index == 2, values[2], values[3])
    return jnp.where(index < 2, low, high)


def place_of(axes):
    return jnp.stack([lax.axis_index(a) for a in axes]).astype(jnp.int32)


def tail_kernel(place, *refs):
    ins, out, extra = refs[:8], refs[8], refs[9]
    half = pl.program_id(0)
    low = out.shape[0] // 4
    for b in range(4):
        rows = pl.ds(b * low, low)
        parts = [jnp.where(half == 0, ins[k][rows, :], ins[4 + k][rows, :]) for k in range(4)]
        parts = [pick(parts, (place[0] + 4 - g) % 4).astype(F32) for g in range(4)]
        to = pl.multiple_of(((place[2] + 4 - b) % 4) * low, 8)
        for c in range(3):
            out[pl.ds(to, low), c * 768 : (c + 1) * 768] = jnp.concatenate(
                [part[:, c * 192 : (c + 1) * 192] for part in parts], axis=1
            )
        extra[pl.ds(to, low), :] = jnp.concatenate([part[:, 576:] for part in parts], axis=1)


def tail_sum(own_half, other_half):
    current = own_half.astype(F32) + swap(other_half).astype(F32)
    current = reduce_phase(current, "y")
    current = reduce_phase(current, "z")
    parts = spread(current.astype(BF16), "z")
    parts = spread(jnp.concatenate(parts, 0), "y")
    mine = spread(jnp.concatenate(parts, 0), "x")
    theirs = [swap(part) for part in mine]
    rows, cols = mine[0].shape
    piece = pl.BlockSpec((rows // 4, cols), lambda h, a, s: (a, 0))
    return pl.pallas_call(
        tail_kernel,
        grid_spec=pltpu.PrefetchScalarGridSpec(
            num_scalar_prefetch=1,
            grid=(2, 4),
            in_specs=[piece] * 8,
            out_specs=[
                pl.BlockSpec(
                    (rows // 4, 4 * count),
                    lambda h, a, s: (((s[3] + h) % 2) * 4 + (s[1] + 4 - a) % 4, 0),
                )
                for count in (576, 64)
            ],
        ),
        out_shape=[jax.ShapeDtypeStruct((2 * rows, 4 * count), F32) for count in (576, 64)],
        compiler_params=pltpu.CompilerParams(vmem_limit_bytes=40 << 20),
    )(place_of(("x", "y", "z", "core")), *mine, *theirs)


def dot_nt(left, right):
    return lax.dot_general(left, right, (((1,), (1,)), ((), ())), preferred_element_type=F32)


def dot_nn(left, right):
    return lax.dot_general(left, right, (((1,), (0,)), ((), ())), preferred_element_type=F32)


def low_lanes(rows):
    return lax.broadcasted_iota(jnp.int32, (rows, 128), 1) < 64


def two_heads(ref, at, count):
    pair = ref[pl.ds(at, count), :]
    low, zero = low_lanes(count), jnp.zeros_like(pair)
    return jnp.concatenate([jnp.where(low, pair, zero), jnp.where(low, zero, pair)], axis=0)


def mask_scores(scores, seg_q, seg_k, at, count):
    if seg_q is None:
        return scores
    mine = seg_q[pl.ds(at, count), :]
    allowed = jnp.concatenate([mine, mine], axis=0) == seg_k[...]
    return jnp.where(allowed, scores, NEG_LARGE)


def forward_kernel(*refs, block, masked):
    if masked:
        seg_q, seg_k, q_ref, k_ref, v_ref, out_ref, lse_ref = refs
    else:
        seg_q = seg_k = None
        q_ref, k_ref, v_ref, out_ref, lse_ref = refs
    count = q_ref.shape[0] // block
    low = low_lanes(block)

    def scores_of(i):
        scores = dot_nt(two_heads(q_ref, i * block, block), k_ref[...])
        return mask_scores(scores, seg_q, seg_k, i * block, block)

    scores = scores_of(0)
    for i in range(count):
        later = scores_of(i + 1) if i + 1 < count else None
        peak = jnp.max(scores, axis=1, keepdims=True)
        probs = jnp.exp(scores - peak)
        total = jnp.sum(probs, axis=1, keepdims=True)
        out = dot_nn(probs.astype(BF16), v_ref[...]) * (1.0 / total)
        rows = pl.ds(i * block, block)
        out_ref[rows, :] = jnp.where(low, out[:block], out[block:]).astype(BF16)
        lse = peak + jnp.log(total)
        lse_ref[0, rows, :] = jnp.concatenate([lse[:block], lse[block:]], axis=1)
        scores = later


def backward_kernel(*refs, block, masked, first):
    if masked:
        seg_q, seg_k = refs[:2]
        refs = refs[2:]
    else:
        seg_q = seg_k = None
    q_ref, k_ref, v_ref, out_ref, grad_ref, lse_ref = refs[:6]
    res_ref, k_sum, v_sum = refs[6 + first :]
    length = q_ref.shape[0]
    count = length // block
    low = low_lanes(block)
    pair = pl.program_id(0)
    width = res_ref.shape[1] // 3
    at_q = pl.multiple_of(pair * 128, 128)
    at_k = pl.multiple_of(width + pair * 128, 128)
    at_v = pl.multiple_of(2 * width + pair * 128, 128)

    def front(i):
        queries = two_heads(q_ref, i * block, block)
        grads = two_heads(grad_ref, i * block, block)
        scores = mask_scores(dot_nt(queries, k_ref[...]), seg_q, seg_k, i * block, block)
        return queries, grads, scores, dot_nt(grads, v_ref[...])

    current = front(0)
    for i in range(count):
        later = front(i + 1) if i + 1 < count else None
        queries, grads, scores, probs_grad = current
        rows = pl.ds(i * block, block)
        lse = lse_ref[0, rows, :]
        lse = jnp.concatenate([lse[:, 0:1], lse[:, 1:2]], axis=0)
        inner = grad_ref[rows, :].astype(F32) * out_ref[rows, :].astype(F32)
        zero = jnp.zeros_like(inner)
        inner = jnp.concatenate(
            [
                jnp.sum(jnp.where(low, inner, zero), axis=1, keepdims=True),
                jnp.sum(jnp.where(low, zero, inner), axis=1, keepdims=True),
            ],
            axis=0,
        )
        probs = jnp.exp(scores - lse)
        score_grad = (probs * (probs_grad - inner)).astype(BF16)
        q_grad = dot_nn(score_grad, k_ref[...])
        q_grad = jnp.where(low, q_grad[:block], q_grad[block:]).astype(BF16).astype(F32)
        res_ref[rows, pl.ds(at_q, 128)] = (q_grad * 0.125).astype(BF16)
        v_part = dot_nn(grads.T, probs.astype(BF16))
        k_part = dot_nn(queries.T, score_grad)
        if i == 0:
            k_sum[...] = k_part
            v_sum[...] = v_part
        else:
            k_sum[...] += k_part
            v_sum[...] += v_part
        current = later
    res_ref[:, pl.ds(at_k, 128)] = k_sum[...].T.astype(BF16)
    res_ref[:, pl.ds(at_v, 128)] = v_sum[...].T.astype(BF16)


def attention_specs(length, width, masked):
    pairs = width // 128
    column = lambda first: pl.BlockSpec((length, 128), lambda p: (0, first + p))
    segs = [
        pl.BlockSpec((length, 1), lambda p: (0, 0)),
        pl.BlockSpec((1, length), lambda p: (0, 0)),
    ]
    qkv = [column(0), column(pairs), column(2 * pairs)]
    stat = pl.BlockSpec((1, length, 2), lambda p: (p, 0, 0))
    return pairs, column, (segs if masked else []) + qkv, stat


def attend(qkv, segs, block):
    length, width = qkv.shape[0], qkv.shape[1] // 3
    masked = len(segs) > 0
    pairs, column, ins, stat = attention_specs(length, width, masked)
    work = 2 * pairs * length * length
    return pl.pallas_call(
        functools.partial(forward_kernel, block=block, masked=masked),
        grid=(pairs,),
        in_specs=ins,
        out_specs=[column(0), stat],
        out_shape=[
            jax.ShapeDtypeStruct((length, width), BF16),
            jax.ShapeDtypeStruct((pairs, length, 2), F32),
        ],
        compiler_params=pltpu.CompilerParams(vmem_limit_bytes=56 << 20),
        cost_estimate=pl.CostEstimate(
            flops=work * 64 * 16, bytes_accessed=length * width * 8, transcendentals=work
        ),
    )(*segs, qkv, qkv, qkv)


def attend_back(qkv, out, grad, lse, segs, block, first=()):
    length, width = qkv.shape[0], qkv.shape[1] // 3
    masked = len(segs) > 0
    pairs, column, ins, stat = attention_specs(length, width, masked)
    work = 2 * pairs * length * length
    return pl.pallas_call(
        functools.partial(backward_kernel, block=block, masked=masked, first=len(first)),
        grid=(pairs,),
        in_specs=ins
        + [column(0), column(0), stat]
        + [pl.BlockSpec(memory_space=pl.ANY)] * len(first),
        out_specs=pl.BlockSpec((length, 3 * width), lambda p: (0, 0)),
        out_shape=jax.ShapeDtypeStruct((length, 3 * width), BF16),
        scratch_shapes=[pltpu.VMEM((128, length), F32)] * 2,
        compiler_params=pltpu.CompilerParams(vmem_limit_bytes=56 << 20),
        cost_estimate=pl.CostEstimate(
            flops=work * 64 * 40, bytes_accessed=length * width * 16, transcendentals=work
        ),
    )(*segs, qkv, qkv, qkv, out, grad, lse, *first)


def sincos_table(count_pos, count_col):
    position = np.arange(count_pos).astype(np.float32)[:, None]
    column = np.arange(count_col)
    exponent = (2 * (column // 2)).astype(np.float32) / np.float32(count_col)
    angles = position / np.power(np.float32(10000.0), exponent)[None, :]
    table = np.where(column[None, :] % 2 == 0, np.sin(angles), np.cos(angles))
    return table.astype(np.float32)


VMEM_ALL = pltpu.CompilerParams(vmem_limit_bytes=56 << 20)


def shape(rows, cols, dtype):
    return jax.ShapeDtypeStruct((rows, cols), dtype)


def cost(flops, moved, special=0):
    return pl.CostEstimate(flops=flops, bytes_accessed=moved, transcendentals=special)


def norm_parts(values):
    average = jnp.mean(values, axis=-1, keepdims=True)
    centred = values - average
    variance = jnp.mean(centred * centred, axis=-1, keepdims=True)
    inv_std = lax.rsqrt(variance + NORM_EPS)
    return centred * inv_std, inv_std


def norm_back(gradient, normed, inv_std, gain):
    scaled = gradient * gain
    return inv_std * (
        scaled
        - jnp.mean(scaled, axis=-1, keepdims=True)
        - normed * jnp.mean(scaled * normed, axis=-1, keepdims=True)
    )


def column_sum(values):
    return jnp.sum(values, axis=0, keepdims=True)


def mm_grad(left, right):
    return jnp.einsum("sk,sn->kn", left, right, preferred_element_type=F32)


def gelu_parts(u):
    cdf = 0.5 + 0.5 * lax.erf(u * 0.7071067811865476)
    bell = jnp.exp(u * u * -0.5)
    return u * cdf, cdf + u * (bell * 0.3989422804014327)


class Vectors:
    def __init__(self, arrays):
        self.at, self.size, total = {}, {}, 0
        for name, array in arrays.items():
            self.at[name], self.size[name] = total, array.shape[0]
            total += array.shape[0]
        self.total = total
        self.row = jnp.concatenate(list(arrays.values())).astype(F32).reshape(1, total)

    def of(self, ref, name, first=0, count=None):
        at = self.at[name] + first
        return ref[:, at : at + (self.size[name] - first if count is None else count)]


def group_kernel(place, weight, inputs, *outs):
    width = weight.shape[1] // 3
    part = width // 4
    rows = inputs.shape[0]
    for k in range(3):
        outs[1 + k][:rows, :] = inputs[...]
    for g in range(4):
        cols = []
        for c in range(3):
            cols.append(weight[:, c * width + g * part : c * width + (g + 1) * part])
            cols.append(jnp.zeros((weight.shape[0], 256 - part), BF16))
        piece = jnp.concatenate(cols, axis=1)

        @pl.when(place[0] == g)
        def _():
            outs[0][...] = piece

        for k in range(1, 4):

            @pl.when((place[0] + k) % 4 == g)
            def _():
                outs[k][rows:, :] = piece


def group_pieces(weight, inputs, place):
    rows, count = weight.shape[0], inputs.shape[0]
    outs = [shape(rows, 768, BF16)] + [shape(count + rows, 768, BF16)] * 3
    whole = lambda a: pl.BlockSpec(a.shape, lambda i, s: (0, 0))
    return pl.pallas_call(
        group_kernel,
        grid_spec=pltpu.PrefetchScalarGridSpec(
            num_scalar_prefetch=1,
            grid=(1,),
            in_specs=[whole(weight), whole(inputs)],
            out_specs=[whole(a) for a in outs],
        ),
        out_shape=outs,
        compiler_params=VMEM_ALL,
    )(place, weight, inputs)


def enc_in_kernel(place, *refs, vectors):
    own, piece, others, vec = refs[0], refs[1], refs[2:5], refs[5]
    qkv_ref, low_ref, weight_ref = refs[6:]
    tokens, rows = own.shape[0], piece.shape[0]
    weight_ref[pl.ds(pl.multiple_of(place[0] * rows, 16), rows), :] = piece[...]
    for k in range(1, 4):
        to = pl.multiple_of(((place[0] + 4 - k) % 4) * rows, 16)
        weight_ref[pl.ds(to, rows), :] = others[k - 1][tokens:, :]
    biases = []
    for first in (0, 768):
        groups = [vectors.of(vec, "enc_qv_bias", first + g * 192, 192) for g in range(4)]
        biases += [pick(groups, place[0]), jnp.zeros((1, 64), F32)]
    bias = jnp.concatenate(biases[:2] + [jnp.zeros((1, 256), F32)] + biases[2:], axis=1)
    scale = jnp.where(lax.broadcasted_iota(jnp.int32, (1, 768), 1) < 256, 0.125, 1.0)
    gain, offset = vectors.of(vec, "enc_norm1_gain"), vectors.of(vec, "enc_norm1_shift")
    for k in range(4):
        inputs = own[...] if k == 0 else others[k - 1][:tokens, :]
        normed, _ = norm_parts(inputs.astype(F32))
        low = (normed * gain + offset).astype(BF16)
        out = pl.ds(k * tokens, tokens)
        low_ref[out, :] = low
        qkv_ref[out, :] = ((dot_nn(low, weight_ref[...]) + bias) * scale).astype(BF16)


def enc_in(own, piece, others, vectors, place):
    tokens, width = own.shape
    rows = 4 * tokens
    whole = lambda a: pl.BlockSpec(a.shape, lambda i, s: (0, 0))
    outs = [shape(rows, 768, BF16), shape(rows, width, BF16), shape(width, 768, BF16)]
    return pl.pallas_call(
        functools.partial(enc_in_kernel, vectors=vectors),
        grid_spec=pltpu.PrefetchScalarGridSpec(
            num_scalar_prefetch=1,
            grid=(1,),
            in_specs=[whole(a) for a in (own, piece, *others, vectors.row)],
            out_specs=[whole(a) for a in outs],
        ),
        out_shape=outs,
        compiler_params=VMEM_ALL,
        cost_estimate=cost(2 * rows * width * 768, rows * width * 8),
    )(place, own, piece, *others, vectors.row)


MATRIX_SPECS = [
    pl.BlockSpec((1, 768, 768), lambda j, s: (4, 0, 0)),
    pl.BlockSpec((1, 768, 768), lambda j, s: (5 + j, 0, 0)),
    pl.BlockSpec((4, 192, 768), lambda j, s: (0, j, 0)),
]


def enc_block_kernel(place, *refs, vectors):
    parts, (x, proj, fc1, fc2, to_dec, send_map, vec) = refs[:4], refs[4:11]
    att_ref, x1_ref, low_ref, act_ref, slope_ref, y_ref, *sends, total = refs[11:]
    step = pl.program_id(0)

    @pl.when(step == 0)
    def _():
        groups = [part[...] for part in parts]
        att = jnp.concatenate([pick(groups, (place[0] + 4 - g) % 4) for g in range(4)], axis=1)
        att_ref[...] = att
        x1 = x[...].astype(F32) + (dot_nn(att, proj[0]) + vectors.of(vec, "enc_proj_bias"))
        x1_ref[...] = x1
        normed, _ = norm_parts(x1)
        gain, offset = vectors.of(vec, "enc_norm2_gain"), vectors.of(vec, "enc_norm2_shift")
        low_ref[...] = (normed * gain + offset).astype(BF16)
        total[...] = x1 + vectors.of(vec, "enc_fc2_bias")

    bias = pick([vectors.of(vec, "enc_fc1_bias", j * 768, 768) for j in range(4)], step)
    pre = dot_nn(low_ref[...], fc1[0]) + bias
    act, slope = gelu_parts(pre)
    act = act.astype(BF16)
    act_ref[...] = act
    slope_ref[...] = slope.astype(BF16)
    total[...] += dot_nn(act, fc2[...].reshape(768, 768))

    @pl.when(step == 3)
    def _():
        y = total[...].astype(BF16)
        y_ref[...] = y
        reduced = dot_nn(y, to_dec[...]).astype(BF16)
        send = dot_nn(send_map[...], reduced).astype(BF16)
        for k in range(4):
            sends[k][...] = send[k * CAP : (k + 1) * CAP, :]


def enc_block(parts, x, matrices, to_dec, send_map, vectors, place):
    rows, width = x.shape
    whole = lambda a: pl.BlockSpec(a.shape, lambda j, s: (0,) * len(a.shape))
    chunk = pl.BlockSpec((rows, 768), lambda j, s: (0, j))
    outs = [
        shape(rows, width, BF16),
        shape(rows, width, F32),
        shape(rows, width, BF16),
        shape(rows, 4 * width, BF16),
        shape(rows, 4 * width, BF16),
        shape(rows, width, BF16),
        *[shape(CAP, DD, BF16)] * 4,
    ]
    return pl.pallas_call(
        functools.partial(enc_block_kernel, vectors=vectors),
        grid_spec=pltpu.PrefetchScalarGridSpec(
            num_scalar_prefetch=1,
            grid=(4,),
            in_specs=[whole(a) for a in (*parts, x)]
            + MATRIX_SPECS
            + [whole(a) for a in (to_dec, send_map, vectors.row)],
            out_specs=[
                chunk if a.shape[-1] == 4 * width else whole(a) for a in outs
            ],
            scratch_shapes=[pltpu.VMEM((rows, width), F32)],
        ),
        out_shape=outs,
        compiler_params=VMEM_ALL,
        cost_estimate=cost(rows * width * width * 20, width * width * 20, rows * width * 8),
    )(place, *parts, x, *[matrices] * 3, to_dec, send_map, vectors.row)


def enc_block_back_kernel(place, *refs, vectors, first):
    parts, (send_map, to_dec, x1, slope, proj, fc1, fc2, vec) = refs[:4], refs[4:12]
    refs = refs[:12] + refs[12 + first :]
    reduced_ref, gz_ref, gpre_ref, gx1_ref, go_ref = refs[12:17]
    gatt_refs, (fc1_b, fc2_b, gain_g, shift_g, proj_b) = refs[17:21], refs[21:26]
    gy, back = refs[-2:]
    step = pl.program_id(0)

    @pl.when(step == 0)
    def _():
        rows = jnp.concatenate([part[...] for part in parts], axis=0)
        reduced = dot_nn(send_map[...], rows).astype(BF16)
        reduced_ref[...] = reduced
        grad = dot_nt(reduced, to_dec[...])
        gy[...] = grad
        gz_ref[...] = grad.astype(BF16)
        fc2_b[...] = column_sum(grad.astype(BF16).astype(F32))
        back[...] = jnp.zeros_like(back)

    gpre = (dot_nt(gz_ref[...], fc2[...].reshape(768, 768)) * slope[...].astype(F32)).astype(BF16)
    gpre_ref[...] = gpre
    fc1_b[...] = column_sum(gpre.astype(F32))
    back[...] += dot_nt(gpre, fc1[0])

    @pl.when(step == 3)
    def _():
        normed, inv_std = norm_parts(x1[...])
        total = back[...]
        gain_g[...] = column_sum(total * normed)
        shift_g[...] = column_sum(total)
        gx1 = gy[...] + norm_back(total, normed, inv_std, vectors.of(vec, "enc_norm2_gain"))
        gx1_ref[...] = gx1
        go = gx1.astype(BF16)
        go_ref[...] = go
        proj_b[...] = column_sum(go.astype(F32))
        gatt = dot_nt(go, proj[0]).astype(BF16)
        groups = [gatt[:, g * 192 : (g + 1) * 192] for g in range(4)]
        for k in range(4):
            gatt_refs[k][...] = pick(groups, (place[0] + k) % 4)


def enc_block_back(parts, send_map, to_dec, x1, slope, matrices, vectors, place, first=()):
    rows, width = x1.shape
    whole = lambda a: pl.BlockSpec(a.shape, lambda j, s: (0,) * len(a.shape))
    outs = [
        shape(rows, DD, BF16),
        shape(rows, width, BF16),
        shape(rows, 4 * width, BF16),
        shape(rows, width, F32),
        shape(rows, width, BF16),
        *[shape(rows, 192, BF16)] * 4,
        shape(1, 4 * width, F32),
        *[shape(1, width, F32)] * 4,
    ]
    by_chunk = lambda a: pl.BlockSpec((a.shape[0], 768), lambda j, s: (0, j))
    return pl.pallas_call(
        functools.partial(enc_block_back_kernel, vectors=vectors, first=len(first)),
        grid_spec=pltpu.PrefetchScalarGridSpec(
            num_scalar_prefetch=1,
            grid=(4,),
            in_specs=[whole(a) for a in (*parts, send_map, to_dec, x1)]
            + [by_chunk(slope), *MATRIX_SPECS, whole(vectors.row)]
            + [pl.BlockSpec(memory_space=pl.ANY)] * len(first),
            out_specs=[by_chunk(a) if a.shape[-1] == 4 * width else whole(a) for a in outs],
            scratch_shapes=[pltpu.VMEM((rows, width), F32)] * 2,
        ),
        out_shape=outs,
        compiler_params=VMEM_ALL,
        cost_estimate=cost(rows * width * width * 20, width * width * 20),
    )(place, *parts, send_map, to_dec, x1, slope, *[matrices] * 3, vectors.row, *first)


def enc_in_back_kernel(*refs, vectors):
    inputs, (grad, weight, vec) = refs[:4], refs[4:7]
    own_ref, others, (gain_g, shift_g, grad_sum) = refs[7], refs[8:11], refs[11:]
    tokens = inputs[0].shape[0]
    gains = shifts = 0.0
    for k in range(4):
        part = dot_nt(grad[pl.ds(k * tokens, tokens), :], weight[...])
        normed, _ = norm_parts(inputs[k][:tokens, :].astype(F32))
        gains = gains + column_sum(part * normed)
        shifts = shifts + column_sum(part)
        if k == 0:
            own_ref[...] = part
        else:
            others[k - 1][...] = part.astype(BF16)
    gain_g[...] = gains
    shift_g[...] = shifts
    grad_sum[...] = column_sum(grad[...].astype(F32))


def enc_in_back(inputs, grad, weight, vectors):
    tokens, width = inputs[0].shape
    outs = [shape(tokens, width, F32)] + [shape(tokens, width, BF16)] * 3
    outs += [shape(1, width, F32)] * 2 + [shape(1, 768, F32)]
    return pl.pallas_call(
        functools.partial(enc_in_back_kernel, vectors=vectors),
        out_shape=outs,
        compiler_params=VMEM_ALL,
        cost_estimate=cost(8 * tokens * width * 768, tokens * width * 32),
    )(*inputs, grad, weight, vectors.row)


def enc_end_kernel(x, gx1, own, a, b, c, vec, out, *, vectors):
    normed, inv_std = norm_parts(x[...].astype(F32))
    back = own[...] + (a[...].astype(F32) + b[...].astype(F32) + c[...].astype(F32))
    out[...] = gx1[...] + norm_back(back, normed, inv_std, vectors.of(vec, "enc_norm1_gain"))


def enc_end(x, gx1, back, vectors):
    return pl.pallas_call(
        functools.partial(enc_end_kernel, vectors=vectors),
        out_shape=shape(*x.shape, F32),
        compiler_params=VMEM_ALL,
    )(x, gx1, *back, vectors.row)


def dec_in_kernel(*refs, vectors):
    parts, (restore, slots, table, weight, vec) = refs[:4], refs[4:9]
    grid_ref, low_ref, qkv_ref = refs[9:]
    rows = jnp.concatenate([part[...] for part in parts], axis=0)
    order = restore[...]
    hot = jnp.where(order == slots[...], 1.0, 0.0).astype(BF16)
    placed = dot_nn(hot, rows)
    grid = placed + jnp.where(order >= VIS, vectors.of(vec, "mask_token"), 0.0) + table[...]
    grid_ref[...] = grid
    normed, _ = norm_parts(grid)
    low = normed * vectors.of(vec, "dec_norm1_gain") + vectors.of(vec, "dec_norm1_shift")
    low = low.astype(BF16)
    low_ref[...] = low
    packed = dot_nn(low, weight[...])
    queries = packed[:, :DD] + vectors.of(vec, "dec_qv_bias", 0, DD)
    qkv_ref[:, :DD] = (queries * 0.125).astype(BF16)
    qkv_ref[:, DD : 2 * DD] = packed[:, DD : 2 * DD].astype(BF16)
    values = packed[:, 2 * DD :] + vectors.of(vec, "dec_qv_bias", DD, DD)
    qkv_ref[:, 2 * DD :] = values.astype(BF16)


def dec_in(parts, restore, slots, table, weight, vectors, tile):
    rows = table.shape[0]
    row = lambda n: pl.BlockSpec((tile, n), lambda i: (i, 0))
    whole = lambda a: pl.BlockSpec(a.shape, lambda i: (0, 0))
    return pl.pallas_call(
        functools.partial(dec_in_kernel, vectors=vectors),
        grid=(rows // tile,),
        in_specs=[whole(a) for a in parts]
        + [row(1), whole(slots), row(DD), whole(weight), whole(vectors.row)],
        out_specs=[row(DD), row(DD), row(3 * DD)],
        out_shape=[shape(rows, DD, F32), shape(rows, DD, BF16), shape(rows, 3 * DD, BF16)],
        compiler_params=VMEM_ALL,
        cost_estimate=cost(rows * DD * DD * 8, rows * DD * 16),
    )(*parts, restore, slots, table, weight, vectors.row)


def dec_in_back_kernel(grad, weight, grid, gx1, restore, slots, vec, *outs, vectors):
    slot_refs, (gain_g, shift_g, mask_g, grad_sum, total) = outs[:4], outs[4:]
    step = pl.program_id(0)

    @pl.when(step == 0)
    def _():
        for ref in (gain_g, shift_g, mask_g, grad_sum, total):
            ref[...] = jnp.zeros_like(ref)

    back = dot_nt(grad[...], weight[...])
    normed, inv_std = norm_parts(grid[...])
    gain_g[...] += column_sum(back * normed)
    shift_g[...] += column_sum(back)
    grad_sum[...] += column_sum(grad[...].astype(F32))
    gx = gx1[...] + norm_back(back, normed, inv_std, vectors.of(vec, "dec_norm1_gain"))
    order = restore[0]
    hot = jnp.where(slots[...] == order, 1.0, 0.0).astype(BF16)
    total[...] += dot_nn(hot, gx.astype(BF16))
    masked = jnp.where(order >= VIS, 1.0, 0.0)
    ones = jnp.broadcast_to(masked, (8, masked.shape[1]))
    mask_g[...] += lax.dot_general(
        ones,
        gx,
        (((1,), (0,)), ((), ())),
        preferred_element_type=F32,
        precision=lax.Precision.HIGHEST,
    )[0:1, :]

    @pl.when(step == pl.num_programs(0) - 1)
    def _():
        for k in range(4):
            slot_refs[k][...] = total[k * CAP : (k + 1) * CAP, :].astype(BF16)


def dec_in_back(grad, weight, grid, gx1, restore, slots, vectors, tile):
    rows = grid.shape[0]
    row = lambda n: pl.BlockSpec((tile, n), lambda i: (i, 0))
    whole = lambda shape: pl.BlockSpec(shape, lambda i: (0, 0))
    sums = [DD, DD, DD, 3 * DD]
    return pl.pallas_call(
        functools.partial(dec_in_back_kernel, vectors=vectors),
        grid=(rows // tile,),
        in_specs=[
            row(3 * DD),
            whole(weight.shape),
            row(DD),
            row(DD),
            pl.BlockSpec((1, 1, tile), lambda i: (i, 0, 0)),
            whole(slots.shape),
            whole(vectors.row.shape),
        ],
        out_specs=[whole((CAP, DD))] * 4 + [whole((1, n)) for n in sums],
        out_shape=[shape(CAP, DD, BF16)] * 4 + [shape(1, n, F32) for n in sums],
        scratch_shapes=[pltpu.VMEM((4 * CAP, DD), F32)],
        compiler_params=VMEM_ALL,
        cost_estimate=cost(rows * DD * DD * 8, rows * DD * 16),
    )(grad, weight, grid, gx1, restore, slots, vectors.row)


def dec_mid_kernel(x, att, gy, proj, fc1, fc2, vec, *outs, vectors, chunk):
    low_ref, act_ref, gpre_ref, y_ref, gx1_ref, go_ref, gatt_ref = outs[:7]
    (fc1_b, fc2_b, gain_g, shift_g, proj_b), slope = outs[7:12], outs[12]

    @pl.when(pl.program_id(0) == 0)
    def _():
        for ref in (fc1_b, fc2_b, gain_g, shift_g, proj_b):
            ref[...] = jnp.zeros_like(ref)

    hidden = fc1.shape[1]
    gain = vectors.of(vec, "dec_norm2_gain")
    x1 = x[...] + (dot_nn(att[...], proj[...]) + vectors.of(vec, "dec_proj_bias"))
    normed, inv_std = norm_parts(x1)
    low = (normed * gain + vectors.of(vec, "dec_norm2_shift")).astype(BF16)
    low_ref[...] = low
    total = x1 + vectors.of(vec, "dec_fc2_bias")

    def pre_of(c):
        return dot_nn(low, fc1[:, c : c + chunk]) + vectors.of(vec, "dec_fc1_bias", c, chunk)

    pre = pre_of(0)
    for c in range(0, hidden, chunk):
        later = pre_of(c + chunk) if c + chunk < hidden else None
        act, rise = gelu_parts(pre)
        act = act.astype(BF16)
        act_ref[:, c : c + chunk] = act
        slope[:, c : c + chunk] = rise.astype(BF16)
        total = total + dot_nn(act, fc2[c : c + chunk, :])
        pre = later
    y_ref[...] = total.astype(BF16)

    gz = gy[...]
    fc2_b[...] += column_sum(gz.astype(F32))
    grad = dot_nt(gz, fc2[:chunk, :])
    back = None
    for c in range(0, hidden, chunk):
        later = None
        if c + chunk < hidden:
            later = dot_nt(gz, fc2[c + chunk : c + 2 * chunk, :])
        gpre = (grad * slope[:, c : c + chunk].astype(F32)).astype(BF16)
        gpre_ref[:, c : c + chunk] = gpre
        fc1_b[:, c : c + chunk] += column_sum(gpre.astype(F32))
        part = dot_nt(gpre, fc1[:, c : c + chunk])
        back = part if back is None else back + part
        grad = later
    gain_g[...] += column_sum(back * normed)
    shift_g[...] += column_sum(back)
    gx1 = gz.astype(F32) + norm_back(back, normed, inv_std, gain)
    gx1_ref[...] = gx1
    go = gx1.astype(BF16)
    go_ref[...] = go
    proj_b[...] += column_sum(go.astype(F32))
    gatt_ref[...] = dot_nt(go, proj[...]).astype(BF16)


def dec_mid(x, att, gy, proj, fc1, fc2, vectors, tile, chunk):
    rows, width = x.shape
    hidden = fc1.shape[1]
    row = lambda n: pl.BlockSpec((tile, n), lambda i: (i, 0))
    whole = lambda shape: pl.BlockSpec(shape, lambda i: (0, 0))
    consts = (proj, fc1, fc2, vectors.row)
    shapes = [(width, BF16), (hidden, BF16), (hidden, BF16), (width, BF16)]
    shapes += [(width, F32), (width, BF16), (width, BF16)]
    sums = [hidden, width, width, width, width]
    return pl.pallas_call(
        functools.partial(dec_mid_kernel, vectors=vectors, chunk=chunk),
        grid=(rows // tile,),
        in_specs=[row(width)] * 3 + [whole(a.shape) for a in consts],
        out_specs=[row(n) for n, _ in shapes] + [whole((1, n)) for n in sums],
        out_shape=[shape(rows, n, t) for n, t in shapes] + [shape(1, n, F32) for n in sums],
        scratch_shapes=[pltpu.VMEM((tile, hidden), BF16)],
        compiler_params=VMEM_ALL,
        cost_estimate=cost(rows * hidden * width * 20, rows * hidden * 12, rows * hidden * 2),
    )(x, att, gy, *consts)


def body(
    encoder_input,
    seg_ids,
    vis_slot,
    restore_order,
    enc_norm1_gain,
    enc_norm1_shift,
    enc_qkv_weight,
    enc_qv_bias,
    enc_proj_weight,
    enc_proj_bias,
    enc_norm2_gain,
    enc_norm2_shift,
    enc_fc1_weight,
    enc_fc1_bias,
    enc_fc2_weight,
    enc_fc2_bias,
    to_dec_weight,
    mask_token,
    dec_norm1_gain,
    dec_norm1_shift,
    dec_qkv_weight,
    dec_qv_bias,
    dec_proj_weight,
    dec_proj_bias,
    dec_norm2_gain,
    dec_norm2_shift,
    dec_fc1_weight,
    dec_fc1_bias,
    dec_fc2_weight,
    dec_fc2_bias,
    out_grad,
):
    x_at = lax.axis_index("x")
    core = lax.axis_index("core")
    place = place_of(("x",))
    tokens, width = encoder_input.shape[1:]
    hw = width // 4
    vectors = Vectors(
        {
            "enc_norm1_gain": enc_norm1_gain,
            "enc_norm1_shift": enc_norm1_shift,
            "enc_qv_bias": enc_qv_bias,
            "enc_proj_bias": enc_proj_bias,
            "enc_norm2_gain": enc_norm2_gain,
            "enc_norm2_shift": enc_norm2_shift,
            "enc_fc1_bias": enc_fc1_bias,
            "enc_fc2_bias": enc_fc2_bias,
            "mask_token": mask_token,
            "dec_norm1_gain": dec_norm1_gain,
            "dec_norm1_shift": dec_norm1_shift,
            "dec_qv_bias": dec_qv_bias,
            "dec_proj_bias": dec_proj_bias,
            "dec_norm2_gain": dec_norm2_gain,
            "dec_norm2_shift": dec_norm2_shift,
            "dec_fc1_bias": dec_fc1_bias,
            "dec_fc2_bias": dec_fc2_bias,
        }
    )

    own_input = encoder_input[0]
    piece, *others = exchange(group_pieces(enc_qkv_weight, own_input, place), "x")
    inputs = [own_input, *others]

    eighth = hw // 8
    first_row = (core * 4 + lax.axis_index("y")) * eighth
    rows_of = lambda stack: lax.dynamic_slice_in_dim(stack, first_row, eighth, 1)
    strip = [
        rows_of(enc_fc2_weight.reshape(4, hw, width)),
        rows_of(enc_proj_weight[None]),
    ]
    fc1_rows = lax.dynamic_slice_in_dim(enc_fc1_weight, first_row, eighth, 0)
    strip += [fc1_rows[None, :, k * width : (k + 1) * width] for k in range(4)]
    matrices = lax.all_gather(
        jnp.concatenate(strip, axis=0), ("x", "core", "y"), axis=1, tiled=True
    )

    row_seg = seg_ids[0].reshape(4, tokens)
    row_slot = vis_slot[0].reshape(4, tokens)
    position = jnp.arange(tokens)
    earlier = position[None, :] < position[:, None]
    same_clip = row_seg[:, :, None] == row_seg[:, None, :]
    ranks = jnp.sum(jnp.logical_and(same_clip, earlier), axis=-1)
    turn = (x_at - jnp.arange(4)) % 4
    seg_turned = jnp.take(row_seg, turn, axis=0)
    segs = (seg_turned.reshape(4 * tokens, 1), seg_turned.reshape(1, 4 * tokens))
    own_seg = lax.dynamic_index_in_dim(row_seg, x_at, 0, keepdims=False)
    own_rank = lax.dynamic_index_in_dim(ranks, x_at, 0, keepdims=False)
    cap_index = jnp.arange(4 * CAP)
    clip_to = (x_at + cap_index // CAP) % 4
    send_map = jnp.logical_and(
        own_seg[None, :] == clip_to[:, None],
        own_rank[None, :] == (cap_index % CAP)[:, None],
    ).astype(BF16)
    send_back = jnp.logical_and(
        own_seg[:, None] == clip_to[None, :],
        own_rank[:, None] == (cap_index % CAP)[None, :],
    ).astype(BF16)
    chosen = jnp.logical_and(
        seg_turned[:, None, :] == x_at,
        jnp.take(ranks, turn, axis=0)[:, None, :] == jnp.arange(CAP)[None, :, None],
    )
    slot_turned = jnp.take(row_slot, turn, axis=0)
    slot_vis = jnp.sum(jnp.where(chosen, slot_turned[:, None, :] + 1, 0), axis=-1) - 1
    restore_row = restore_order[0, 0]
    restore_col = restore_row[:, None]
    restore_row = restore_row.reshape(2, 1, FULL // 2)
    table = jnp.asarray(sincos_table(FULL, DD))

    qkv, first_in, qkv_mine = enc_in(own_input, piece, others, vectors, place)
    att_mine, enc_lse = attend(qkv, segs, 128)
    blocks = att_mine.reshape(4, tokens, 256)
    parts = exchange([blocks[(4 - k) % 4, :, :hw] for k in range(4)], "x")
    attended, enc_x1, second_in, enc_act, enc_slope, enc_low, *sends = enc_block(
        parts, own_input, matrices, to_dec_weight, send_map, vectors, place
    )

    received = exchange(sends, "x")
    grid, dec_in_low, dec_qkv = dec_in(
        received,
        restore_col,
        slot_vis.reshape(1, 4 * CAP),
        table,
        dec_qkv_weight,
        vectors,
        FULL // 2,
    )
    dec_att, dec_lse = attend(dec_qkv, (), 224)

    dec_gz = out_grad[0, 0]
    dec_second, dec_act, dec_gpre, dec_out, dec_gx1, dec_go, dec_gatt, *dec_sums = dec_mid(
        grid,
        dec_att,
        dec_gz,
        dec_proj_weight,
        dec_fc1_weight,
        dec_fc2_weight,
        vectors,
        FULL // 2,
        512,
    )
    dec_fc1_b, dec_fc2_b, dec_gain2_g, dec_shift2_g, dec_proj_b = dec_sums
    dec_gqkv = attend_back(dec_qkv, dec_att, dec_gatt, dec_lse, (), 112)
    *slot_grads, dec_gain1_g, dec_shift1_g, mask_g, dec_gqkv_sum = dec_in_back(
        dec_gqkv,
        dec_qkv_weight,
        grid,
        dec_gx1,
        restore_row,
        slot_vis.reshape(4 * CAP, 1),
        vectors,
        FULL // 2,
    )
    low_grad = lambda left, right: mm_grad(left, right).astype(BF16)
    slot_grads, dec_in_low, dec_att, dec_second, dec_act = lax.optimization_barrier(
        (slot_grads, dec_in_low, dec_att, dec_second, dec_act)
    )
    dec_early = (low_grad(dec_second, dec_gpre), low_grad(dec_act, dec_gz))

    returned = exchange(slot_grads, "x", -1)
    reduced_grad, enc_gz, enc_gpre, enc_gx1, enc_go, *rest = enc_block_back(
        returned,
        send_back,
        to_dec_weight,
        enc_x1,
        enc_slope,
        matrices,
        vectors,
        place,
        dec_early,
    )
    gatt_parts, enc_sums = rest[:4], rest[4:]
    enc_fc1_b, enc_fc2_b, enc_gain2_g, enc_shift2_g, enc_proj_b = enc_sums
    columns = lambda array, which: lax.dynamic_slice_in_dim(
        array, which * (array.shape[1] // 2), array.shape[1] // 2, 1
    )

    def halves(make):
        return make(core), make(1 - core)

    early = (
        *dec_early,
        low_grad(dec_in_low, dec_gqkv),
        low_grad(dec_att, dec_go),
        low_grad(enc_low, reduced_grad),
        low_grad(attended, enc_go),
        low_grad(second_in, enc_gpre),
        low_grad(enc_act, enc_gz),
    )
    gatt_mine = jnp.concatenate(exchange(gatt_parts, "x"), axis=0)
    gatt_mine = jnp.pad(gatt_mine, ((0, 0), (0, 64)))
    def finish():
        gqkv = attend_back(qkv, att_mine, gatt_mine, enc_lse, segs, 128, early)
        own_back, *others, gain1_g, shift1_g, gqkv_sum = enc_in_back(
            inputs, gqkv, qkv_mine, vectors
        )

        qv = jnp.zeros((2, 4, hw), F32)
        qv = lax.dynamic_update_index_in_dim(
            qv, jnp.stack([gqkv_sum[0, :hw], gqkv_sum[0, 512 : 512 + hw]]), x_at, 1
        )
        small = [
            gain1_g,
            shift1_g,
            qv.reshape(1, 2 * width),
            enc_proj_b,
            enc_gain2_g,
            enc_shift2_g,
            enc_fc1_b,
            enc_fc2_b,
            mask_g,
            dec_gain1_g,
            dec_shift1_g,
            dec_gqkv_sum[:, :DD],
            dec_gqkv_sum[:, 2 * DD :],
            dec_proj_b,
            dec_gain2_g,
            dec_shift2_g,
            dec_fc1_b,
            dec_fc2_b,
        ]
        sizes = [v.shape[1] for v in small]
        vector = jnp.concatenate([*small, jnp.zeros((1, 14336 - sum(sizes)), F32)], axis=1)
        terms = spread(vector.reshape(112, 128), "x")
        vector = ((terms[0] + terms[1]) + (terms[2] + terms[3])).reshape(4, 56, 64)
        extra = lax.dynamic_index_in_dim(vector, x_at, 0, keepdims=False).astype(BF16)
        extra = jnp.pad(extra, ((0, width - 56), (0, 0)))

        def qkv_half(which):
            grad = low_grad(columns(first_in, which), gqkv)
            grad = [grad[:, c * 256 : c * 256 + hw] for c in range(3)]
            more = lax.dynamic_slice_in_dim(extra, which * (width // 2), width // 2, 0)
            return jnp.concatenate([*grad, more], axis=1)


        qkv_sum, vec_sum = tail_sum(*halves(qkv_half))
        back = exchange([None, *others], "x", -1)
        gx = enc_end(own_input, enc_gx1, (own_back, *back[1:]), vectors)
        return qkv_sum, vec_sum, gx

    def nothing():
        return tuple(
            jnp.zeros(dims, F32)
            for dims in ((width, 3 * width), (width, 256), (tokens, width))
        )

    rest_grads = lax.psum(early, ALL)
    qkv_grad, vector, input_grad = lax.cond(seg_ids[0, 0] >= 0, finish, nothing)
    vector = vector[:56].reshape(56, 4, 64).transpose(1, 0, 2).reshape(14336)
    sizes = [width, width, 2 * width, width, width, width, 4 * width, width, DD]
    sizes += [DD, DD, 2 * DD, DD, DD, DD, 4 * DD, DD]
    cuts = [int(c) for c in np.cumsum(sizes)]
    v = jnp.split(vector, cuts)

    wide = lambda array: array.astype(F32)
    return (
        dec_out[None, None],
        input_grad[None],
        v[0],
        v[1],
        qkv_grad,
        v[2],
        wide(rest_grads[5]),
        v[3],
        v[4],
        v[5],
        wide(rest_grads[6]),
        v[6],
        wide(rest_grads[7]),
        v[7],
        wide(rest_grads[4]),
        v[8],
        v[9],
        v[10],
        wide(rest_grads[2]),
        v[11],
        wide(rest_grads[3]),
        v[12],
        v[13],
        v[14],
        wide(rest_grads[0]),
        v[15],
        wide(rest_grads[1]),
        v[16],
    )


def solution(mesh):
    fine = Mesh(mesh.devices.reshape(4, 4, 2, 4), ALL)
    row, shared, split = P(WIDE, None), P(), P("x", None)
    return jax.shard_map(
        body,
        mesh=fine,
        in_specs=(
            P(WIDE, "x", None),
            row,
            row,
            P(WIDE, "x", None),
            shared,
            shared,
            split,
            shared,
            split,
            shared,
            shared,
            shared,
            split,
            shared,
            split,
        )
        + (shared,) * 15
        + (P(WIDE, "x", None, None),),
        out_specs=(P(WIDE, "x", None, None), P(WIDE, "x", None)) + (shared,) * 26,
        check_vma=False,
    )
```

```python
import functools

import jax
import jax.numpy as jnp
import numpy as np
from jax import lax
from jax.experimental import pallas as pl
from jax.experimental.pallas import tpu as pltpu
from jax.sharding import Mesh
from jax.sharding import PartitionSpec as P

HEADS = 12
DD = 384
DHEADS = 6
VIS = 157
FULL = 1568
CAP = 64
NORM_EPS = 1e-06
NEG_LARGE = -1e30
ALL = ("z", "y", "core", "x")
WIDE = ("z", "y", "core")
F32 = jnp.float32
BF16 = jnp.bfloat16


def shift(value, axis, step):
    return lax.ppermute(value, axis, [(i, (i + step) % 4) for i in range(4)])


def swap(value):
    return lax.ppermute(value, "core", [(0, 1), (1, 0)])


def spread(piece, axis):
    across = shift(piece, axis, 2)
    return [piece, shift(piece, axis, 1), across, shift(piece, axis, 3)]


def exchange(pieces, axis, sign=1):
    far = shift(pieces[2], axis, 2)
    return [pieces[0], shift(pieces[1], axis, sign), far, shift(pieces[3], axis, -sign)]


def reduce_phase(current, axis):
    rows = current.shape[0] // 4
    index = lax.axis_index(axis)
    got = []
    for step in (2, 1, 3):
        piece = lax.dynamic_slice_in_dim(current, ((index + step) % 4) * rows, rows, 0)
        got.append(shift(piece.astype(BF16), axis, step).astype(F32))
    own = lax.dynamic_slice_in_dim(current, index * rows, rows, 0).astype(F32)
    return own + (got[0] + got[1] + got[2])


def sum_vector(vector):
    vector = vector + swap(vector)
    for axis in ("x", "y", "z"):
        parts = spread(vector, axis)
        vector = (parts[0] + parts[1]) + (parts[2] + parts[3])
    return vector


def pick(values, index):
    low = jnp.where(index == 0, values[0], values[1])
    high = jnp.where(index == 2, values[2], values[3])
    return jnp.where(index < 2, low, high)


def place_of(axes):
    return jnp.stack([lax.axis_index(a) for a in axes]).astype(jnp.int32)


def tail_kernel(place, *refs):
    ins, out, extra = refs[:8], refs[8], refs[9]
    half = pl.program_id(0)
    low = out.shape[0] // 4
    for b in range(4):
        rows = pl.ds(b * low, low)
        parts = [jnp.where(half == 0, ins[k][rows, :], ins[4 + k][rows, :]) for k in range(4)]
        parts = [pick(parts, (place[0] + 4 - g) % 4).astype(F32) for g in range(4)]
        to = pl.multiple_of(((place[2] + 4 - b) % 4) * low, 8)
        for c in range(3):
            out[pl.ds(to, low), c * 768 : (c + 1) * 768] = jnp.concatenate(
                [part[:, c * 192 : (c + 1) * 192] for part in parts], axis=1
            )
        extra[pl.ds(to, low), :] = jnp.concatenate([part[:, 576:] for part in parts], axis=1)


def tail_sum(own_half, other_half):
    current = own_half.astype(F32) + swap(other_half).astype(F32)
    current = reduce_phase(current, "y")
    current = reduce_phase(current, "z")
    parts = spread(current.astype(BF16), "z")
    parts = spread(jnp.concatenate(parts, 0), "y")
    mine = spread(jnp.concatenate(parts, 0), "x")
    theirs = [swap(part) for part in mine]
    rows, cols = mine[0].shape
    piece = pl.BlockSpec((rows // 4, cols), lambda h, a, s: (a, 0))
    return pl.pallas_call(
        tail_kernel,
        grid_spec=pltpu.PrefetchScalarGridSpec(
            num_scalar_prefetch=1,
            grid=(2, 4),
            in_specs=[piece] * 8,
            out_specs=[
                pl.BlockSpec(
                    (rows // 4, 4 * count),
                    lambda h, a, s: (((s[3] + h) % 2) * 4 + (s[1] + 4 - a) % 4, 0),
                )
                for count in (576, 64)
            ],
        ),
        out_shape=[jax.ShapeDtypeStruct((2 * rows, 4 * count), F32) for count in (576, 64)],
        compiler_params=pltpu.CompilerParams(vmem_limit_bytes=40 << 20),
    )(place_of(("x", "y", "z", "core")), *mine, *theirs)


def dot_nt(left, right):
    return lax.dot_general(left, right, (((1,), (1,)), ((), ())), preferred_element_type=F32)


def dot_nn(left, right):
    return lax.dot_general(left, right, (((1,), (0,)), ((), ())), preferred_element_type=F32)


def low_lanes(rows):
    return lax.broadcasted_iota(jnp.int32, (rows, 128), 1) < 64


def two_heads(ref, at, count):
    pair = ref[pl.ds(at, count), :]
    low, zero = low_lanes(count), jnp.zeros_like(pair)
    return jnp.concatenate([jnp.where(low, pair, zero), jnp.where(low, zero, pair)], axis=0)


def mask_scores(scores, seg_q, seg_k, at, count):
    if seg_q is None:
        return scores
    mine = seg_q[pl.ds(at, count), :]
    allowed = jnp.concatenate([mine, mine], axis=0) == seg_k[...]
    return jnp.where(allowed, scores, NEG_LARGE)


def forward_kernel(*refs, block, masked):
    if masked:
        seg_q, seg_k, q_ref, k_ref, v_ref, out_ref, lse_ref = refs
    else:
        seg_q = seg_k = None
        q_ref, k_ref, v_ref, out_ref, lse_ref = refs
    count = q_ref.shape[0] // block
    low = low_lanes(block)

    def scores_of(i):
        scores = dot_nt(two_heads(q_ref, i * block, block), k_ref[...])
        return mask_scores(scores, seg_q, seg_k, i * block, block)

    scores = scores_of(0)
    for i in range(count):
        later = scores_of(i + 1) if i + 1 < count else None
        peak = jnp.max(scores, axis=1, keepdims=True)
        probs = jnp.exp(scores - peak)
        total = jnp.sum(probs, axis=1, keepdims=True)
        out = dot_nn(probs.astype(BF16), v_ref[...]) * (1.0 / total)
        rows = pl.ds(i * block, block)
        out_ref[rows, :] = jnp.where(low, out[:block], out[block:]).astype(BF16)
        lse = peak + jnp.log(total)
        lse_ref[0, rows, :] = jnp.concatenate([lse[:block], lse[block:]], axis=1)
        scores = later


def backward_kernel(*refs, block, masked, first):
    if masked:
        seg_q, seg_k = refs[:2]
        refs = refs[2:]
    else:
        seg_q = seg_k = None
    q_ref, k_ref, v_ref, out_ref, grad_ref, lse_ref = refs[:6]
    res_ref, k_sum, v_sum = refs[6 + first :]
    length = q_ref.shape[0]
    count = length // block
    low = low_lanes(block)
    pair = pl.program_id(0)
    width = res_ref.shape[1] // 3
    at_q = pl.multiple_of(pair * 128, 128)
    at_k = pl.multiple_of(width + pair * 128, 128)
    at_v = pl.multiple_of(2 * width + pair * 128, 128)

    def front(i):
        queries = two_heads(q_ref, i * block, block)
        grads = two_heads(grad_ref, i * block, block)
        scores = mask_scores(dot_nt(queries, k_ref[...]), seg_q, seg_k, i * block, block)
        return queries, grads, scores, dot_nt(grads, v_ref[...])

    current = front(0)
    for i in range(count):
        later = front(i + 1) if i + 1 < count else None
        queries, grads, scores, probs_grad = current
        rows = pl.ds(i * block, block)
        lse = lse_ref[0, rows, :]
        lse = jnp.concatenate([lse[:, 0:1], lse[:, 1:2]], axis=0)
        inner = grad_ref[rows, :].astype(F32) * out_ref[rows, :].astype(F32)
        zero = jnp.zeros_like(inner)
        inner = jnp.concatenate(
            [
                jnp.sum(jnp.where(low, inner, zero), axis=1, keepdims=True),
                jnp.sum(jnp.where(low, zero, inner), axis=1, keepdims=True),
            ],
            axis=0,
        )
        probs = jnp.exp(scores - lse)
        score_grad = (probs * (probs_grad - inner)).astype(BF16)
        q_grad = dot_nn(score_grad, k_ref[...])
        q_grad = jnp.where(low, q_grad[:block], q_grad[block:]).astype(BF16).astype(F32)
        res_ref[rows, pl.ds(at_q, 128)] = (q_grad * 0.125).astype(BF16)
        v_part = dot_nn(grads.T, probs.astype(BF16))
        k_part = dot_nn(queries.T, score_grad)
        if i == 0:
            k_sum[...] = k_part
            v_sum[...] = v_part
        else:
            k_sum[...] += k_part
            v_sum[...] += v_part
        current = later
    res_ref[:, pl.ds(at_k, 128)] = k_sum[...].T.astype(BF16)
    res_ref[:, pl.ds(at_v, 128)] = v_sum[...].T.astype(BF16)


def attention_specs(length, width, masked):
    pairs = width // 128
    column = lambda first: pl.BlockSpec((length, 128), lambda p: (0, first + p))
    segs = [
        pl.BlockSpec((length, 1), lambda p: (0, 0)),
        pl.BlockSpec((1, length), lambda p: (0, 0)),
    ]
    qkv = [column(0), column(pairs), column(2 * pairs)]
    stat = pl.BlockSpec((1, length, 2), lambda p: (p, 0, 0))
    return pairs, column, (segs if masked else []) + qkv, stat


def attend(qkv, segs, block):
    length, width = qkv.shape[0], qkv.shape[1] // 3
    masked = len(segs) > 0
    pairs, column, ins, stat = attention_specs(length, width, masked)
    work = 2 * pairs * length * length
    return pl.pallas_call(
        functools.partial(forward_kernel, block=block, masked=masked),
        grid=(pairs,),
        in_specs=ins,
        out_specs=[column(0), stat],
        out_shape=[
            jax.ShapeDtypeStruct((length, width), BF16),
            jax.ShapeDtypeStruct((pairs, length, 2), F32),
        ],
        compiler_params=pltpu.CompilerParams(vmem_limit_bytes=56 << 20),
        cost_estimate=pl.CostEstimate(
            flops=work * 64 * 16, bytes_accessed=length * width * 8, transcendentals=work
        ),
    )(*segs, qkv, qkv, qkv)


def attend_back(qkv, out, grad, lse, segs, block, first=()):
    length, width = qkv.shape[0], qkv.shape[1] // 3
    masked = len(segs) > 0
    pairs, column, ins, stat = attention_specs(length, width, masked)
    work = 2 * pairs * length * length
    return pl.pallas_call(
        functools.partial(backward_kernel, block=block, masked=masked, first=len(first)),
        grid=(pairs,),
        in_specs=ins
        + [column(0), column(0), stat]
        + [pl.BlockSpec(memory_space=pl.ANY)] * len(first),
        out_specs=pl.BlockSpec((length, 3 * width), lambda p: (0, 0)),
        out_shape=jax.ShapeDtypeStruct((length, 3 * width), BF16),
        scratch_shapes=[pltpu.VMEM((128, length), F32)] * 2,
        compiler_params=pltpu.CompilerParams(vmem_limit_bytes=56 << 20),
        cost_estimate=pl.CostEstimate(
            flops=work * 64 * 40, bytes_accessed=length * width * 16, transcendentals=work
        ),
    )(*segs, qkv, qkv, qkv, out, grad, lse, *first)


def sincos_table(count_pos, count_col):
    position = np.arange(count_pos).astype(np.float32)[:, None]
    column = np.arange(count_col)
    exponent = (2 * (column // 2)).astype(np.float32) / np.float32(count_col)
    angles = position / np.power(np.float32(10000.0), exponent)[None, :]
    table = np.where(column[None, :] % 2 == 0, np.sin(angles), np.cos(angles))
    return table.astype(np.float32)


VMEM_ALL = pltpu.CompilerParams(vmem_limit_bytes=56 << 20)


def shape(rows, cols, dtype):
    return jax.ShapeDtypeStruct((rows, cols), dtype)


def cost(flops, moved, special=0):
    return pl.CostEstimate(flops=flops, bytes_accessed=moved, transcendentals=special)


def norm_parts(values):
    average = jnp.mean(values, axis=-1, keepdims=True)
    centred = values - average
    variance = jnp.mean(centred * centred, axis=-1, keepdims=True)
    inv_std = lax.rsqrt(variance + NORM_EPS)
    return centred * inv_std, inv_std


def norm_back(gradient, normed, inv_std, gain):
    scaled = gradient * gain
    return inv_std * (
        scaled
        - jnp.mean(scaled, axis=-1, keepdims=True)
        - normed * jnp.mean(scaled * normed, axis=-1, keepdims=True)
    )


def column_sum(values):
    return jnp.sum(values, axis=0, keepdims=True)


def mm_grad(left, right):
    return jnp.einsum("sk,sn->kn", left, right, preferred_element_type=F32)


def gelu_parts(u):
    cdf = 0.5 + 0.5 * lax.erf(u * 0.7071067811865476)
    bell = jnp.exp(u * u * -0.5)
    return u * cdf, cdf + u * (bell * 0.3989422804014327)


class Vectors:
    def __init__(self, arrays):
        self.at, self.size, total = {}, {}, 0
        for name, array in arrays.items():
            self.at[name], self.size[name] = total, array.shape[0]
            total += array.shape[0]
        self.total = total
        self.row = jnp.concatenate(list(arrays.values())).astype(F32).reshape(1, total)

    def of(self, ref, name, first=0, count=None):
        at = self.at[name] + first
        return ref[:, at : at + (self.size[name] - first if count is None else count)]


def group_kernel(place, weight, inputs, *outs):
    width = weight.shape[1] // 3
    part = width // 4
    rows = inputs.shape[0]
    for k in range(3):
        outs[1 + k][:rows, :] = inputs[...]
    for g in range(4):
        cols = []
        for c in range(3):
            cols.append(weight[:, c * width + g * part : c * width + (g + 1) * part])
            cols.append(jnp.zeros((weight.shape[0], 256 - part), BF16))
        piece = jnp.concatenate(cols, axis=1)

        @pl.when(place[0] == g)
        def _():
            outs[0][...] = piece

        half = piece.shape[0] // 2
        own = jnp.where(place[1] == 0, piece[:half], piece[half:])
        for k in range(1, 4):

            @pl.when((place[0] + k) % 4 == g)
            def _():
                outs[k][rows:, :] = own


def group_pieces(weight, inputs, place):
    rows, count = weight.shape[0], inputs.shape[0]
    outs = [shape(rows, 768, BF16)] + [shape(count + rows // 2, 768, BF16)] * 3
    whole = lambda a: pl.BlockSpec(a.shape, lambda i, s: (0, 0))
    return pl.pallas_call(
        group_kernel,
        grid_spec=pltpu.PrefetchScalarGridSpec(
            num_scalar_prefetch=1,
            grid=(1,),
            in_specs=[whole(weight), whole(inputs)],
            out_specs=[whole(a) for a in outs],
        ),
        out_shape=outs,
        compiler_params=VMEM_ALL,
    )(place, weight, inputs)


def enc_in_kernel(place, *refs, vectors):
    own, piece, others, swapped, vec = refs[0], refs[1], refs[2:5], refs[5], refs[6]
    qkv_ref, low_ref, weight_ref = refs[7:]
    tokens, rows = own.shape[0], piece.shape[0]
    half = rows // 2
    weight_ref[pl.ds(pl.multiple_of(place[0] * rows, 16), rows), :] = piece[...]
    for k in range(1, 4):
        to = ((place[0] + 4 - k) % 4) * rows
        mine = pl.multiple_of(to + place[1] * half, 16)
        weight_ref[pl.ds(mine, half), :] = others[k - 1][tokens:, :]
        rest = pl.multiple_of(to + (1 - place[1]) * half, 16)
        weight_ref[pl.ds(rest, half), :] = swapped[(k - 1) * half : k * half, :]
    biases = []
    for first in (0, 768):
        groups = [vectors.of(vec, "enc_qv_bias", first + g * 192, 192) for g in range(4)]
        biases += [pick(groups, place[0]), jnp.zeros((1, 64), F32)]
    bias = jnp.concatenate(biases[:2] + [jnp.zeros((1, 256), F32)] + biases[2:], axis=1)
    scale = jnp.where(lax.broadcasted_iota(jnp.int32, (1, 768), 1) < 256, 0.125, 1.0)
    gain, offset = vectors.of(vec, "enc_norm1_gain"), vectors.of(vec, "enc_norm1_shift")
    for k in range(4):
        inputs = own[...] if k == 0 else others[k - 1][:tokens, :]
        normed, _ = norm_parts(inputs.astype(F32))
        low = (normed * gain + offset).astype(BF16)
        out = pl.ds(k * tokens, tokens)
        low_ref[out, :] = low
        qkv_ref[out, :] = ((dot_nn(low, weight_ref[...]) + bias) * scale).astype(BF16)


def enc_in(own, piece, others, swapped, vectors, place):
    tokens, width = own.shape
    rows = 4 * tokens
    whole = lambda a: pl.BlockSpec(a.shape, lambda i, s: (0, 0))
    outs = [shape(rows, 768, BF16), shape(rows, width, BF16), shape(width, 768, BF16)]
    return pl.pallas_call(
        functools.partial(enc_in_kernel, vectors=vectors),
        grid_spec=pltpu.PrefetchScalarGridSpec(
            num_scalar_prefetch=1,
            grid=(1,),
            in_specs=[whole(a) for a in (own, piece, *others, swapped, vectors.row)],
            out_specs=[whole(a) for a in outs],
        ),
        out_shape=outs,
        compiler_params=VMEM_ALL,
        cost_estimate=cost(2 * rows * width * 768, rows * width * 8),
    )(place, own, piece, *others, swapped, vectors.row)


MATRIX_SPECS = [
    pl.BlockSpec((1, 768, 768), lambda j, s: (4, 0, 0)),
    pl.BlockSpec((1, 768, 768), lambda j, s: (5 + j, 0, 0)),
    pl.BlockSpec((4, 192, 768), lambda j, s: (0, j, 0)),
]


def enc_block_kernel(place, *refs, vectors):
    parts, (x, proj, fc1, fc2, to_dec, send_map, vec) = refs[:4], refs[4:11]
    att_ref, x1_ref, low_ref, act_ref, slope_ref, y_ref, *sends, total = refs[11:]
    step = pl.program_id(0)

    @pl.when(step == 0)
    def _():
        groups = [part[...] for part in parts]
        att = jnp.concatenate([pick(groups, (place[0] + 4 - g) % 4) for g in range(4)], axis=1)
        att_ref[...] = att
        x1 = x[...].astype(F32) + (dot_nn(att, proj[0]) + vectors.of(vec, "enc_proj_bias"))
        x1_ref[...] = x1
        normed, _ = norm_parts(x1)
        gain, offset = vectors.of(vec, "enc_norm2_gain"), vectors.of(vec, "enc_norm2_shift")
        low_ref[...] = (normed * gain + offset).astype(BF16)
        total[...] = x1 + vectors.of(vec, "enc_fc2_bias")

    bias = pick([vectors.of(vec, "enc_fc1_bias", j * 768, 768) for j in range(4)], step)
    pre = dot_nn(low_ref[...], fc1[0]) + bias
    act, slope = gelu_parts(pre)
    act = act.astype(BF16)
    act_ref[...] = act
    slope_ref[...] = slope.astype(BF16)
    total[...] += dot_nn(act, fc2[...].reshape(768, 768))

    @pl.when(step == 3)
    def _():
        y = total[...].astype(BF16)
        y_ref[...] = y
        reduced = dot_nn(y, to_dec[...]).astype(BF16)
        send = dot_nn(send_map[...], reduced).astype(BF16)
        for k in range(4):
            sends[k][...] = send[k * CAP : (k + 1) * CAP, :]


def enc_block(parts, x, matrices, to_dec, send_map, vectors, place):
    rows, width = x.shape
    whole = lambda a: pl.BlockSpec(a.shape, lambda j, s: (0,) * len(a.shape))
    chunk = pl.BlockSpec((rows, 768), lambda j, s: (0, j))
    outs = [
        shape(rows, width, BF16),
        shape(rows, width, F32),
        shape(rows, width, BF16),
        shape(rows, 4 * width, BF16),
        shape(rows, 4 * width, BF16),
        shape(rows, width, BF16),
        *[shape(CAP, DD, BF16)] * 4,
    ]
    return pl.pallas_call(
        functools.partial(enc_block_kernel, vectors=vectors),
        grid_spec=pltpu.PrefetchScalarGridSpec(
            num_scalar_prefetch=1,
            grid=(4,),
            in_specs=[whole(a) for a in (*parts, x)]
            + MATRIX_SPECS
            + [whole(a) for a in (to_dec, send_map, vectors.row)],
            out_specs=[
                chunk if a.shape[-1] == 4 * width else whole(a) for a in outs
            ],
            scratch_shapes=[pltpu.VMEM((rows, width), F32)],
        ),
        out_shape=outs,
        compiler_params=VMEM_ALL,
        cost_estimate=cost(rows * width * width * 20, width * width * 20, rows * width * 8),
    )(place, *parts, x, *[matrices] * 3, to_dec, send_map, vectors.row)


def enc_block_back_kernel(place, *refs, vectors, first):
    parts, (send_map, to_dec, x1, y, low, att) = refs[:4], refs[4:10]
    act, slope, proj, fc1, fc2, vec = refs[10:16]
    refs = refs[16 + first :]
    fc1_g, fc2_g, fc1_b, gx1_ref, proj_g, to_dec_g = refs[:6]
    gatt_refs, (fc2_b, gain_g, shift_g, proj_b) = refs[6:10], refs[10:14]
    gz, gy, back, low_turned = refs[14:]
    step = pl.program_id(0)

    @pl.when(step == 0)
    def _():
        rows = jnp.concatenate([part[...] for part in parts], axis=0)
        reduced = dot_nn(send_map[...], rows).astype(BF16)
        to_dec_g[...] = dot_nn(y[...].T, reduced).astype(BF16)
        grad = dot_nt(reduced, to_dec[...])
        gy[...] = grad
        gz[...] = grad.astype(BF16)
        fc2_b[...] = column_sum(grad.astype(BF16).astype(F32))
        back[...] = jnp.zeros_like(back)
        low_turned[...] = low[...].T

    fc2_g[...] = dot_nn(act[...].T, gz[...]).astype(BF16)
    gpre = dot_nt(gz[...], fc2[...].reshape(768, 768)) * slope[...].astype(F32)
    gpre = gpre.astype(BF16)
    fc1_b[...] = column_sum(gpre.astype(F32))
    fc1_g[...] = dot_nn(low_turned[...], gpre).astype(BF16)
    back[...] += dot_nt(gpre, fc1[0])

    @pl.when(step == 3)
    def _():
        normed, inv_std = norm_parts(x1[...])
        total = back[...]
        gain_g[...] = column_sum(total * normed)
        shift_g[...] = column_sum(total)
        gx1 = gy[...] + norm_back(total, normed, inv_std, vectors.of(vec, "enc_norm2_gain"))
        gx1_ref[...] = gx1
        go = gx1.astype(BF16)
        proj_b[...] = column_sum(go.astype(F32))
        proj_g[...] = dot_nn(att[...].T, go).astype(BF16)
        gatt = dot_nt(go, proj[0]).astype(BF16)
        groups = [gatt[:, g * 192 : (g + 1) * 192] for g in range(4)]
        for k in range(4):
            gatt_refs[k][...] = pick(groups, (place[0] + k) % 4)


def enc_block_back(
    parts, send_map, to_dec, x1, y, low, att, act, slope, matrices, vectors, place, first
):
    rows, width = x1.shape
    whole = lambda a: pl.BlockSpec(a.shape, lambda j, s: (0,) * len(a.shape))
    columns = lambda count: pl.BlockSpec((count, 768), lambda j, s: (0, j))
    rest = [
        shape(rows, width, F32),
        shape(width, width, BF16),
        shape(width, DD, BF16),
        *[shape(rows, 192, BF16)] * 4,
        *[shape(1, width, F32)] * 4,
    ]
    return pl.pallas_call(
        functools.partial(enc_block_back_kernel, vectors=vectors, first=len(first)),
        grid_spec=pltpu.PrefetchScalarGridSpec(
            num_scalar_prefetch=1,
            grid=(4,),
            in_specs=[whole(a) for a in (*parts, send_map, to_dec, x1, y, low, att)]
            + [columns(rows), columns(rows), *MATRIX_SPECS, whole(vectors.row)]
            + [pl.BlockSpec(memory_space=pl.ANY)] * len(first),
            out_specs=[
                columns(width),
                pl.BlockSpec((768, width), lambda j, s: (j, 0)),
                columns(1),
            ]
            + [whole(a) for a in rest],
            scratch_shapes=[
                pltpu.VMEM((rows, width), BF16),
                pltpu.VMEM((rows, width), F32),
                pltpu.VMEM((rows, width), F32),
                pltpu.VMEM((width, rows), BF16),
            ],
        ),
        out_shape=[
            shape(width, 4 * width, BF16),
            shape(4 * width, width, BF16),
            shape(1, 4 * width, F32),
            *rest,
        ],
        compiler_params=VMEM_ALL,
        cost_estimate=cost(rows * width * width * 40, width * width * 40),
    )(
        place,
        *parts,
        send_map,
        to_dec,
        x1,
        y,
        low,
        att,
        act,
        slope,
        *[matrices] * 3,
        vectors.row,
        *first,
    )


def enc_in_back_kernel(*refs, vectors):
    inputs, (grad, weight, vec) = refs[:4], refs[4:7]
    own_ref, others, (gain_g, shift_g, grad_sum) = refs[7], refs[8:11], refs[11:]
    tokens = inputs[0].shape[0]
    gains = shifts = 0.0
    for k in range(4):
        part = dot_nt(grad[pl.ds(k * tokens, tokens), :], weight[...])
        normed, _ = norm_parts(inputs[k][:tokens, :].astype(F32))
        gains = gains + column_sum(part * normed)
        shifts = shifts + column_sum(part)
        if k == 0:
            own_ref[...] = part
        else:
            others[k - 1][...] = part.astype(BF16)
    gain_g[...] = gains
    shift_g[...] = shifts
    grad_sum[...] = column_sum(grad[...].astype(F32))


def enc_in_back(inputs, grad, weight, vectors):
    tokens, width = inputs[0].shape
    outs = [shape(tokens, width, F32)] + [shape(tokens, width, BF16)] * 3
    outs += [shape(1, width, F32)] * 2 + [shape(1, 768, F32)]
    return pl.pallas_call(
        functools.partial(enc_in_back_kernel, vectors=vectors),
        out_shape=outs,
        compiler_params=VMEM_ALL,
        cost_estimate=cost(8 * tokens * width * 768, tokens * width * 32),
    )(*inputs, grad, weight, vectors.row)


def enc_end_kernel(x, gx1, own, a, b, c, vec, out, *, vectors):
    normed, inv_std = norm_parts(x[...].astype(F32))
    back = own[...] + (a[...].astype(F32) + b[...].astype(F32) + c[...].astype(F32))
    out[...] = gx1[...] + norm_back(back, normed, inv_std, vectors.of(vec, "enc_norm1_gain"))


def enc_end(x, gx1, back, vectors):
    return pl.pallas_call(
        functools.partial(enc_end_kernel, vectors=vectors),
        out_shape=shape(*x.shape, F32),
        compiler_params=VMEM_ALL,
    )(x, gx1, *back, vectors.row)


def dec_in_kernel(*refs, vectors):
    parts, (restore, slots, table, weight, vec) = refs[:4], refs[4:9]
    grid_ref, low_ref, qkv_ref = refs[9:]
    rows = jnp.concatenate([part[...] for part in parts], axis=0)
    order = restore[...]
    hot = jnp.where(order == slots[...], 1.0, 0.0).astype(BF16)
    placed = dot_nn(hot, rows)
    grid = placed + jnp.where(order >= VIS, vectors.of(vec, "mask_token"), 0.0) + table[...]
    grid_ref[...] = grid
    normed, _ = norm_parts(grid)
    low = normed * vectors.of(vec, "dec_norm1_gain") + vectors.of(vec, "dec_norm1_shift")
    low = low.astype(BF16)
    low_ref[...] = low
    packed = dot_nn(low, weight[...])
    queries = packed[:, :DD] + vectors.of(vec, "dec_qv_bias", 0, DD)
    qkv_ref[:, :DD] = (queries * 0.125).astype(BF16)
    qkv_ref[:, DD : 2 * DD] = packed[:, DD : 2 * DD].astype(BF16)
    values = packed[:, 2 * DD :] + vectors.of(vec, "dec_qv_bias", DD, DD)
    qkv_ref[:, 2 * DD :] = values.astype(BF16)


def dec_in(parts, restore, slots, table, weight, vectors, tile):
    rows = table.shape[0]
    row = lambda n: pl.BlockSpec((tile, n), lambda i: (i, 0))
    whole = lambda a: pl.BlockSpec(a.shape, lambda i: (0, 0))
    return pl.pallas_call(
        functools.partial(dec_in_kernel, vectors=vectors),
        grid=(rows // tile,),
        in_specs=[whole(a) for a in parts]
        + [row(1), whole(slots), row(DD), whole(weight), whole(vectors.row)],
        out_specs=[row(DD), row(DD), row(3 * DD)],
        out_shape=[shape(rows, DD, F32), shape(rows, DD, BF16), shape(rows, 3 * DD, BF16)],
        compiler_params=VMEM_ALL,
        cost_estimate=cost(rows * DD * DD * 8, rows * DD * 16),
    )(*parts, restore, slots, table, weight, vectors.row)


def dec_in_back_kernel(grad, weight, grid, gx1, restore, column, slots, vec, *outs, vectors):
    slot_refs, (gain_g, shift_g, mask_g, grad_sum, total) = outs[:4], outs[4:]
    step = pl.program_id(0)

    @pl.when(step == 0)
    def _():
        for ref in (gain_g, shift_g, mask_g, grad_sum, total):
            ref[...] = jnp.zeros_like(ref)

    back = dot_nt(grad[...], weight[...])
    normed, inv_std = norm_parts(grid[...])
    gain_g[...] += column_sum(back * normed)
    shift_g[...] += column_sum(back)
    grad_sum[...] += column_sum(grad[...].astype(F32))
    gx = gx1[...] + norm_back(back, normed, inv_std, vectors.of(vec, "dec_norm1_gain"))
    order = restore[0]
    hot = jnp.where(slots[...] == order, 1.0, 0.0).astype(BF16)
    total[...] += dot_nn(hot, gx.astype(BF16))
    mask_g[...] += column_sum(jnp.where(column[...] >= VIS, gx, 0.0))

    @pl.when(step == pl.num_programs(0) - 1)
    def _():
        for k in range(4):
            slot_refs[k][...] = total[k * CAP : (k + 1) * CAP, :].astype(BF16)


def dec_in_back(grad, weight, grid, gx1, restore, column, slots, vectors, tile):
    rows = grid.shape[0]
    row = lambda n: pl.BlockSpec((tile, n), lambda i: (i, 0))
    whole = lambda shape: pl.BlockSpec(shape, lambda i: (0, 0))
    sums = [DD, DD, DD, 3 * DD]
    return pl.pallas_call(
        functools.partial(dec_in_back_kernel, vectors=vectors),
        grid=(rows // tile,),
        in_specs=[
            row(3 * DD),
            whole(weight.shape),
            row(DD),
            row(DD),
            pl.BlockSpec((1, 1, tile), lambda i: (i, 0, 0)),
            row(1),
            whole(slots.shape),
            whole(vectors.row.shape),
        ],
        out_specs=[whole((CAP, DD))] * 4 + [whole((1, n)) for n in sums],
        out_shape=[shape(CAP, DD, BF16)] * 4 + [shape(1, n, F32) for n in sums],
        scratch_shapes=[pltpu.VMEM((4 * CAP, DD), F32)],
        compiler_params=VMEM_ALL,
        cost_estimate=cost(rows * DD * DD * 8, rows * DD * 16),
    )(grad, weight, grid, gx1, restore, column, slots, vectors.row)


def dec_mid_kernel(x, att, gy, proj, fc1, fc2, vec, *outs, vectors, chunk):
    y_ref, gx1_ref, go_ref, gatt_ref, fc1_g, fc2_g = outs[:6]
    (fc1_b, fc2_b, gain_g, shift_g, proj_b), (act_ref, slope, fc1_sum, fc2_sum) = (
        outs[6:11],
        outs[11:],
    )
    step = pl.program_id(0)

    @pl.when(step == 0)
    def _():
        for ref in (fc1_b, fc2_b, gain_g, shift_g, proj_b, fc1_sum, fc2_sum):
            ref[...] = jnp.zeros_like(ref)

    hidden = fc1.shape[1]
    gain = vectors.of(vec, "dec_norm2_gain")
    x1 = x[...] + (dot_nn(att[...], proj[...]) + vectors.of(vec, "dec_proj_bias"))
    normed, inv_std = norm_parts(x1)
    low = (normed * gain + vectors.of(vec, "dec_norm2_shift")).astype(BF16)
    total = x1 + vectors.of(vec, "dec_fc2_bias")

    def pre_of(c):
        return dot_nn(low, fc1[:, c : c + chunk]) + vectors.of(vec, "dec_fc1_bias", c, chunk)

    pre = pre_of(0)
    for c in range(0, hidden, chunk):
        later = pre_of(c + chunk) if c + chunk < hidden else None
        act, rise = gelu_parts(pre)
        act = act.astype(BF16)
        act_ref[:, c : c + chunk] = act
        slope[:, c : c + chunk] = rise.astype(BF16)
        total = total + dot_nn(act, fc2[c : c + chunk, :])
        pre = later
    y_ref[...] = total.astype(BF16)

    gz = gy[...]
    gz_turned = gz.T
    low_turned = low.T
    fc2_b[...] += column_sum(gz.astype(F32))
    grad = dot_nt(gz, fc2[:chunk, :])
    back = None
    for c in range(0, hidden, chunk):
        later = None
        if c + chunk < hidden:
            later = dot_nt(gz, fc2[c + chunk : c + 2 * chunk, :])
        fc2_sum[:, c : c + chunk] += dot_nn(gz_turned, act_ref[:, c : c + chunk])
        gpre = (grad * slope[:, c : c + chunk].astype(F32)).astype(BF16)
        fc1_b[:, c : c + chunk] += column_sum(gpre.astype(F32))
        fc1_sum[:, c : c + chunk] += dot_nn(low_turned, gpre)
        part = dot_nt(gpre, fc1[:, c : c + chunk])
        back = part if back is None else back + part
        grad = later
    gain_g[...] += column_sum(back * normed)
    shift_g[...] += column_sum(back)
    gx1 = gz.astype(F32) + norm_back(back, normed, inv_std, gain)
    gx1_ref[...] = gx1
    go = gx1.astype(BF16)
    go_ref[...] = go
    proj_b[...] += column_sum(go.astype(F32))
    gatt_ref[...] = dot_nt(go, proj[...]).astype(BF16)

    @pl.when(step == pl.num_programs(0) - 1)
    def _():
        fc1_g[...] = fc1_sum[...].astype(BF16)
        for c in range(0, hidden, chunk):
            fc2_g[c : c + chunk, :] = fc2_sum[:, c : c + chunk].T.astype(BF16)


def dec_mid(x, att, gy, proj, fc1, fc2, vectors, tile, chunk):
    rows, width = x.shape
    hidden = fc1.shape[1]
    row = lambda n: pl.BlockSpec((tile, n), lambda i: (i, 0))
    whole = lambda shape: pl.BlockSpec(shape, lambda i: (0, 0))
    consts = (proj, fc1, fc2, vectors.row)
    shapes = [(width, BF16), (width, F32), (width, BF16), (width, BF16)]
    fixed = [shape(width, hidden, BF16), shape(hidden, width, BF16)]
    fixed += [shape(1, n, F32) for n in (hidden, width, width, width, width)]
    return pl.pallas_call(
        functools.partial(dec_mid_kernel, vectors=vectors, chunk=chunk),
        grid=(rows // tile,),
        in_specs=[row(width)] * 3 + [whole(a.shape) for a in consts],
        out_specs=[row(n) for n, _ in shapes] + [whole(a.shape) for a in fixed],
        out_shape=[shape(rows, n, t) for n, t in shapes] + fixed,
        scratch_shapes=[pltpu.VMEM((tile, hidden), BF16)] * 2
        + [pltpu.VMEM((width, hidden), F32)] * 2,
        compiler_params=VMEM_ALL,
        cost_estimate=cost(rows * hidden * width * 28, rows * width * 20, rows * hidden * 2),
    )(x, att, gy, *consts)


def widen_kernel(*refs):
    count = len(refs) // 2
    for k in range(count):
        refs[count + k][...] = refs[k][...].astype(F32)


def widen(arrays):
    piece = lambda a: pl.BlockSpec((a.shape[0] // 8, a.shape[1]), lambda i: (i, 0))
    return pl.pallas_call(
        widen_kernel,
        grid=(8,),
        in_specs=[piece(a) for a in arrays],
        out_specs=[piece(a) for a in arrays],
        out_shape=[shape(*a.shape, F32) for a in arrays],
        compiler_params=VMEM_ALL,
        cost_estimate=cost(0, sum(a.shape[0] * a.shape[1] * 6 for a in arrays)),
    )(*arrays)


def body(
    encoder_input,
    seg_ids,
    vis_slot,
    restore_order,
    enc_norm1_gain,
    enc_norm1_shift,
    enc_qkv_weight,
    enc_qv_bias,
    enc_proj_weight,
    enc_proj_bias,
    enc_norm2_gain,
    enc_norm2_shift,
    enc_fc1_weight,
    enc_fc1_bias,
    enc_fc2_weight,
    enc_fc2_bias,
    to_dec_weight,
    mask_token,
    dec_norm1_gain,
    dec_norm1_shift,
    dec_qkv_weight,
    dec_qv_bias,
    dec_proj_weight,
    dec_proj_bias,
    dec_norm2_gain,
    dec_norm2_shift,
    dec_fc1_weight,
    dec_fc1_bias,
    dec_fc2_weight,
    dec_fc2_bias,
    out_grad,
):
    x_at = lax.axis_index("x")
    core = lax.axis_index("core")
    place = place_of(("x", "core"))
    tokens, width = encoder_input.shape[1:]
    hw = width // 4
    vectors = Vectors(
        {
            "enc_norm1_gain": enc_norm1_gain,
            "enc_norm1_shift": enc_norm1_shift,
            "enc_qv_bias": enc_qv_bias,
            "enc_proj_bias": enc_proj_bias,
            "enc_norm2_gain": enc_norm2_gain,
            "enc_norm2_shift": enc_norm2_shift,
            "enc_fc1_bias": enc_fc1_bias,
            "enc_fc2_bias": enc_fc2_bias,
            "mask_token": mask_token,
            "dec_norm1_gain": dec_norm1_gain,
            "dec_norm1_shift": dec_norm1_shift,
            "dec_qv_bias": dec_qv_bias,
            "dec_proj_bias": dec_proj_bias,
            "dec_norm2_gain": dec_norm2_gain,
            "dec_norm2_shift": dec_norm2_shift,
            "dec_fc1_bias": dec_fc1_bias,
            "dec_fc2_bias": dec_fc2_bias,
        }
    )

    own_input = encoder_input[0]
    piece, *others = exchange(group_pieces(enc_qkv_weight, own_input, place), "x")
    swapped = swap(jnp.concatenate([other[tokens:] for other in others], axis=0))
    inputs = [own_input, *others]

    eighth = hw // 8
    first_row = (core * 4 + lax.axis_index("y")) * eighth
    rows_of = lambda stack: lax.dynamic_slice_in_dim(stack, first_row, eighth, 1)
    strip = [
        rows_of(enc_fc2_weight.reshape(4, hw, width)),
        rows_of(enc_proj_weight[None]),
    ]
    fc1_rows = lax.dynamic_slice_in_dim(enc_fc1_weight, first_row, eighth, 0)
    strip += [fc1_rows[None, :, k * width : (k + 1) * width] for k in range(4)]
    matrices = lax.all_gather(
        jnp.concatenate(strip, axis=0), ("x", "core", "y"), axis=1, tiled=True
    )

    row_seg = seg_ids[0].reshape(4, tokens)
    row_slot = vis_slot[0].reshape(4, tokens)
    position = jnp.arange(tokens)
    earlier = position[None, :] < position[:, None]
    same_clip = row_seg[:, :, None] == row_seg[:, None, :]
    ranks = jnp.sum(jnp.logical_and(same_clip, earlier), axis=-1)
    turn = (x_at - jnp.arange(4)) % 4
    seg_turned = jnp.take(row_seg, turn, axis=0)
    segs = (seg_turned.reshape(4 * tokens, 1), seg_turned.reshape(1, 4 * tokens))
    own_seg = lax.dynamic_index_in_dim(row_seg, x_at, 0, keepdims=False)
    own_rank = lax.dynamic_index_in_dim(ranks, x_at, 0, keepdims=False)
    cap_index = jnp.arange(4 * CAP)
    clip_to = (x_at + cap_index // CAP) % 4
    send_map = jnp.logical_and(
        own_seg[None, :] == clip_to[:, None],
        own_rank[None, :] == (cap_index % CAP)[:, None],
    ).astype(BF16)
    send_back = jnp.logical_and(
        own_seg[:, None] == clip_to[None, :],
        own_rank[:, None] == (cap_index % CAP)[None, :],
    ).astype(BF16)
    chosen = jnp.logical_and(
        seg_turned[:, None, :] == x_at,
        jnp.take(ranks, turn, axis=0)[:, None, :] == jnp.arange(CAP)[None, :, None],
    )
    slot_turned = jnp.take(row_slot, turn, axis=0)
    slot_vis = jnp.sum(jnp.where(chosen, slot_turned[:, None, :] + 1, 0), axis=-1) - 1
    restore_row = restore_order[0, 0]
    restore_col = restore_row[:, None]
    restore_row = restore_row.reshape(2, 1, FULL // 2)
    table = jnp.asarray(sincos_table(FULL, DD))

    qkv, first_in, qkv_mine = enc_in(own_input, piece, others, swapped, vectors, place)
    att_mine, enc_lse = attend(qkv, segs, 128)
    blocks = att_mine.reshape(4, tokens, 256)
    parts = exchange([blocks[(4 - k) % 4, :, :hw] for k in range(4)], "x")
    attended, enc_x1, second_in, enc_act, enc_slope, enc_low, *sends = enc_block(
        parts, own_input, matrices, to_dec_weight, send_map, vectors, place
    )

    received = exchange(sends, "x")
    grid, dec_in_low, dec_qkv = dec_in(
        received,
        restore_col,
        slot_vis.reshape(1, 4 * CAP),
        table,
        dec_qkv_weight,
        vectors,
        FULL // 2,
    )
    dec_att, dec_lse = attend(dec_qkv, (), 224)

    dec_gz = out_grad[0, 0]
    dec_out, dec_gx1, dec_go, dec_gatt, dec_fc1_g, dec_fc2_g, *dec_sums = dec_mid(
        grid,
        dec_att,
        dec_gz,
        dec_proj_weight,
        dec_fc1_weight,
        dec_fc2_weight,
        vectors,
        FULL // 2,
        512,
    )
    dec_fc1_b, dec_fc2_b, dec_gain2_g, dec_shift2_g, dec_proj_b = dec_sums
    dec_gqkv = attend_back(dec_qkv, dec_att, dec_gatt, dec_lse, (), 112)
    *slot_grads, dec_gain1_g, dec_shift1_g, mask_g, dec_gqkv_sum = dec_in_back(
        dec_gqkv,
        dec_qkv_weight,
        grid,
        dec_gx1,
        restore_row,
        restore_col,
        slot_vis.reshape(4 * CAP, 1),
        vectors,
        FULL // 2,
    )
    low_grad = lambda left, right: mm_grad(left, right).astype(BF16)
    slot_grads, dec_in_low, dec_att = lax.optimization_barrier((slot_grads, dec_in_low, dec_att))
    low_grad = lambda left, right: mm_grad(left, right).astype(BF16)
    dec_early = (low_grad(dec_in_low, dec_gqkv), low_grad(dec_att, dec_go), dec_fc1_g, dec_fc2_g)

    returned = exchange(slot_grads, "x", -1)
    enc_fc1_g, enc_fc2_g, enc_fc1_b, enc_gx1, enc_proj_g, to_dec_g, *rest = enc_block_back(
        returned,
        send_back,
        to_dec_weight,
        enc_x1,
        enc_low,
        second_in,
        attended,
        enc_act,
        enc_slope,
        matrices,
        vectors,
        place,
        dec_early[:2],
    )
    gatt_parts, (enc_fc2_b, enc_gain2_g, enc_shift2_g, enc_proj_b) = rest[:4], rest[4:]
    columns = lambda array, which: lax.dynamic_slice_in_dim(
        array, which * (array.shape[1] // 2), array.shape[1] // 2, 1
    )

    def halves(make):
        return make(core), make(1 - core)

    early = (*dec_early, enc_proj_g, enc_fc1_g, enc_fc2_g, to_dec_g)
    gatt_mine = jnp.concatenate(exchange(gatt_parts, "x"), axis=0)
    gatt_mine = jnp.pad(gatt_mine, ((0, 0), (0, 64)))
    def finish():
        gqkv = attend_back(qkv, att_mine, gatt_mine, enc_lse, segs, 128, early)
        own_back, *others, gain1_g, shift1_g, gqkv_sum = enc_in_back(
            inputs, gqkv, qkv_mine, vectors
        )

        qv = jnp.zeros((2, 4, hw), F32)
        qv = lax.dynamic_update_index_in_dim(
            qv, jnp.stack([gqkv_sum[0, :hw], gqkv_sum[0, 512 : 512 + hw]]), x_at, 1
        )
        small = [
            gain1_g,
            shift1_g,
            qv.reshape(1, 2 * width),
            enc_proj_b,
            enc_gain2_g,
            enc_shift2_g,
            enc_fc1_b,
            enc_fc2_b,
            mask_g,
            dec_gain1_g,
            dec_shift1_g,
            dec_gqkv_sum[:, :DD],
            dec_gqkv_sum[:, 2 * DD :],
            dec_proj_b,
            dec_gain2_g,
            dec_shift2_g,
            dec_fc1_b,
            dec_fc2_b,
        ]
        sizes = [v.shape[1] for v in small]
        vector = jnp.concatenate([*small, jnp.zeros((1, 14336 - sum(sizes)), F32)], axis=1)
        terms = spread(vector.reshape(112, 128), "x")
        vector = ((terms[0] + terms[1]) + (terms[2] + terms[3])).reshape(4, 56, 64)
        extra = lax.dynamic_index_in_dim(vector, x_at, 0, keepdims=False).astype(BF16)
        extra = jnp.pad(extra, ((0, width - 56), (0, 0)))

        def qkv_half(which):
            grad = low_grad(columns(first_in, which), gqkv)
            grad = [grad[:, c * 256 : c * 256 + hw] for c in range(3)]
            more = lax.dynamic_slice_in_dim(extra, which * (width // 2), width // 2, 0)
            return jnp.concatenate([*grad, more], axis=1)


        qkv_sum, vec_sum = tail_sum(*halves(qkv_half))
        back = exchange([None, *others], "x", -1)
        gx = enc_end(own_input, enc_gx1, (own_back, *back[1:]), vectors)
        return qkv_sum, vec_sum, gx

    def nothing():
        return tuple(
            jnp.zeros(dims, F32)
            for dims in ((width, 3 * width), (width, 256), (tokens, width))
        )

    rest_grads = lax.psum(early, ALL)
    qkv_grad, vector, input_grad = lax.cond(seg_ids[0, 0] >= 0, finish, nothing)
    vector = vector[:56].reshape(56, 4, 64).transpose(1, 0, 2).reshape(14336)
    sizes = [width, width, 2 * width, width, width, width, 4 * width, width, DD]
    sizes += [DD, DD, 2 * DD, DD, DD, DD, 4 * DD, DD]
    cuts = [int(c) for c in np.cumsum(sizes)]
    v = jnp.split(vector, cuts)

    dec_qkv_g, dec_proj_g, dec_fc1_g, dec_fc2_g, *rest_grads = widen(rest_grads)
    enc_proj_g, enc_fc1_g, enc_fc2_g, to_dec_g = rest_grads
    return (
        dec_out[None, None],
        input_grad[None],
        v[0],
        v[1],
        qkv_grad,
        v[2],
        enc_proj_g,
        v[3],
        v[4],
        v[5],
        enc_fc1_g,
        v[6],
        enc_fc2_g,
        v[7],
        to_dec_g,
        v[8],
        v[9],
        v[10],
        dec_qkv_g,
        v[11],
        dec_proj_g,
        v[12],
        v[13],
        v[14],
        dec_fc1_g,
        v[15],
        dec_fc2_g,
        v[16],
    )


def solution(mesh):
    fine = Mesh(mesh.devices.reshape(4, 4, 2, 4), ALL)
    row, shared, split = P(WIDE, None), P(), P("x", None)
    return jax.shard_map(
        body,
        mesh=fine,
        in_specs=(
            P(WIDE, "x", None),
            row,
            row,
            P(WIDE, "x", None),
            shared,
            shared,
            split,
            shared,
            split,
            shared,
            shared,
            shared,
            split,
            shared,
            split,
        )
        + (shared,) * 15
        + (P(WIDE, "x", None, None),),
        out_specs=(P(WIDE, "x", None, None), P(WIDE, "x", None)) + (shared,) * 26,
        check_vma=False,
    )
```

```python
import functools

import jax
import jax.numpy as jnp
import numpy as np
from jax import lax
from jax.experimental import pallas as pl
from jax.experimental.pallas import tpu as pltpu
from jax.sharding import Mesh
from jax.sharding import PartitionSpec as P

HEADS = 12
DD = 384
DHEADS = 6
VIS = 157
FULL = 1568
CAP = 64
NORM_EPS = 1e-06
NEG_LARGE = -1e30
ALL = ("z", "y", "core", "x")
WIDE = ("z", "y", "core")
F32 = jnp.float32
BF16 = jnp.bfloat16


def room(mebibytes):
    return pltpu.CompilerParams(vmem_limit_bytes=mebibytes << 20)


def shift(value, axis, step):
    return lax.ppermute(value, axis, [(i, (i + step) % 4) for i in range(4)])


def swap(value):
    return lax.ppermute(value, "core", [(0, 1), (1, 0)])


def spread(piece, axis):
    across = shift(piece, axis, 2)
    return [piece, shift(piece, axis, 1), across, shift(piece, axis, 3)]


def exchange(pieces, axis, sign=1):
    far = shift(pieces[2], axis, 2)
    return [pieces[0], shift(pieces[1], axis, sign), far, shift(pieces[3], axis, -sign)]


def reduce_phase(current, axis):
    rows = current.shape[0] // 4
    index = lax.axis_index(axis)
    got = []
    for step in (2, 1, 3):
        piece = lax.dynamic_slice_in_dim(current, ((index + step) % 4) * rows, rows, 0)
        got.append(shift(piece.astype(BF16), axis, step).astype(F32))
    own = lax.dynamic_slice_in_dim(current, index * rows, rows, 0).astype(F32)
    return own + (got[0] + got[1] + got[2])


def sum_vector(vector):
    vector = vector + swap(vector)
    for axis in ("x", "y", "z"):
        parts = spread(vector, axis)
        vector = (parts[0] + parts[1]) + (parts[2] + parts[3])
    return vector


def pick(values, index):
    low = jnp.where(index == 0, values[0], values[1])
    high = jnp.where(index == 2, values[2], values[3])
    return jnp.where(index < 2, low, high)


def place_of(axes):
    return jnp.stack([lax.axis_index(a) for a in axes]).astype(jnp.int32)


def tail_kernel(place, *refs):
    ins, out, extra = refs[:8], refs[8], refs[9]
    half = pl.program_id(0)
    low = out.shape[0] // 4
    for b in range(4):
        rows = pl.ds(b * low, low)
        parts = [jnp.where(half == 0, ins[k][rows, :], ins[4 + k][rows, :]) for k in range(4)]
        parts = [pick(parts, (place[0] + 4 - g) % 4).astype(F32) for g in range(4)]
        to = pl.multiple_of(((place[2] + 4 - b) % 4) * low, 8)
        for c in range(3):
            out[pl.ds(to, low), c * 768 : (c + 1) * 768] = jnp.concatenate(
                [part[:, c * 192 : (c + 1) * 192] for part in parts], axis=1
            )
        extra[pl.ds(to, low), :] = jnp.concatenate([part[:, 576:] for part in parts], axis=1)


def tail_sum(own_half, other_half):
    current = own_half.astype(F32) + swap(other_half).astype(F32)
    current = reduce_phase(current, "y")
    current = reduce_phase(current, "z")
    parts = spread(current.astype(BF16), "z")
    parts = spread(jnp.concatenate(parts, 0), "y")
    mine = spread(jnp.concatenate(parts, 0), "x")
    theirs = [swap(part) for part in mine]
    rows, cols = mine[0].shape
    piece = pl.BlockSpec((rows // 4, cols), lambda h, a, s: (a, 0))
    return pl.pallas_call(
        tail_kernel,
        grid_spec=pltpu.PrefetchScalarGridSpec(
            num_scalar_prefetch=1,
            grid=(2, 4),
            in_specs=[piece] * 8,
            out_specs=[
                pl.BlockSpec(
                    (rows // 4, 4 * count),
                    lambda h, a, s: (((s[3] + h) % 2) * 4 + (s[1] + 4 - a) % 4, 0),
                )
                for count in (576, 64)
            ],
        ),
        out_shape=[jax.ShapeDtypeStruct((2 * rows, 4 * count), F32) for count in (576, 64)],
        compiler_params=room(16),
    )(place_of(("x", "y", "z", "core")), *mine, *theirs)


def dot_nt(left, right):
    return lax.dot_general(left, right, (((1,), (1,)), ((), ())), preferred_element_type=F32)


def dot_nn(left, right):
    return lax.dot_general(left, right, (((1,), (0,)), ((), ())), preferred_element_type=F32)


def low_lanes(rows):
    return lax.broadcasted_iota(jnp.int32, (rows, 128), 1) < 64


def two_heads(ref, at, count):
    pair = ref[pl.ds(at, count), :]
    low, zero = low_lanes(count), jnp.zeros_like(pair)
    return jnp.concatenate([jnp.where(low, pair, zero), jnp.where(low, zero, pair)], axis=0)


def mask_scores(scores, seg_q, seg_k, at, count):
    if seg_q is None:
        return scores
    mine = seg_q[pl.ds(at, count), :]
    allowed = jnp.concatenate([mine, mine], axis=0) == seg_k[...]
    return jnp.where(allowed, scores, NEG_LARGE)


def forward_kernel(*refs, block, masked):
    if masked:
        seg_q, seg_k, q_ref, k_ref, v_ref, out_ref, lse_ref = refs
    else:
        seg_q = seg_k = None
        q_ref, k_ref, v_ref, out_ref, lse_ref = refs
    count = q_ref.shape[0] // block
    low = low_lanes(block)

    def scores_of(i):
        scores = dot_nt(two_heads(q_ref, i * block, block), k_ref[...])
        return mask_scores(scores, seg_q, seg_k, i * block, block)

    scores = scores_of(0)
    for i in range(count):
        later = scores_of(i + 1) if i + 1 < count else None
        peak = jnp.max(scores, axis=1, keepdims=True)
        probs = jnp.exp(scores - peak)
        total = jnp.sum(probs, axis=1, keepdims=True)
        out = dot_nn(probs.astype(BF16), v_ref[...]) * (1.0 / total)
        rows = pl.ds(i * block, block)
        out_ref[rows, :] = jnp.where(low, out[:block], out[block:]).astype(BF16)
        lse = peak + jnp.log(total)
        lse_ref[0, rows, :] = jnp.concatenate([lse[:block], lse[block:]], axis=1)
        scores = later


def backward_kernel(*refs, block, masked, first):
    if masked:
        seg_q, seg_k = refs[:2]
        refs = refs[2:]
    else:
        seg_q = seg_k = None
    q_ref, k_ref, v_ref, out_ref, grad_ref, lse_ref = refs[:6]
    res_ref, k_sum, v_sum = refs[6 + first :]
    length = q_ref.shape[0]
    count = length // block
    low = low_lanes(block)
    pair = pl.program_id(0)
    width = res_ref.shape[1] // 3
    at_q = pl.multiple_of(pair * 128, 128)
    at_k = pl.multiple_of(width + pair * 128, 128)
    at_v = pl.multiple_of(2 * width + pair * 128, 128)

    def front(i):
        queries = two_heads(q_ref, i * block, block)
        grads = two_heads(grad_ref, i * block, block)
        scores = mask_scores(dot_nt(queries, k_ref[...]), seg_q, seg_k, i * block, block)
        return queries, grads, scores, dot_nt(grads, v_ref[...])

    current = front(0)
    for i in range(count):
        later = front(i + 1) if i + 1 < count else None
        queries, grads, scores, probs_grad = current
        rows = pl.ds(i * block, block)
        lse = lse_ref[0, rows, :]
        lse = jnp.concatenate([lse[:, 0:1], lse[:, 1:2]], axis=0)
        inner = grad_ref[rows, :].astype(F32) * out_ref[rows, :].astype(F32)
        zero = jnp.zeros_like(inner)
        inner = jnp.concatenate(
            [
                jnp.sum(jnp.where(low, inner, zero), axis=1, keepdims=True),
                jnp.sum(jnp.where(low, zero, inner), axis=1, keepdims=True),
            ],
            axis=0,
        )
        probs = jnp.exp(scores - lse)
        score_grad = (probs * (probs_grad - inner)).astype(BF16)
        q_grad = dot_nn(score_grad, k_ref[...])
        q_grad = jnp.where(low, q_grad[:block], q_grad[block:]).astype(BF16).astype(F32)
        res_ref[rows, pl.ds(at_q, 128)] = (q_grad * 0.125).astype(BF16)
        v_part = dot_nn(grads.T, probs.astype(BF16))
        k_part = dot_nn(queries.T, score_grad)
        if i == 0:
            k_sum[...] = k_part
            v_sum[...] = v_part
        else:
            k_sum[...] += k_part
            v_sum[...] += v_part
        current = later
    res_ref[:, pl.ds(at_k, 128)] = k_sum[...].T.astype(BF16)
    res_ref[:, pl.ds(at_v, 128)] = v_sum[...].T.astype(BF16)


def attention_specs(length, width, masked):
    pairs = width // 128
    column = lambda first: pl.BlockSpec((length, 128), lambda p: (0, first + p))
    segs = [
        pl.BlockSpec((length, 1), lambda p: (0, 0)),
        pl.BlockSpec((1, length), lambda p: (0, 0)),
    ]
    qkv = [column(0), column(pairs), column(2 * pairs)]
    stat = pl.BlockSpec((1, length, 2), lambda p: (p, 0, 0))
    return pairs, column, (segs if masked else []) + qkv, stat


def attend(qkv, segs, block):
    length, width = qkv.shape[0], qkv.shape[1] // 3
    masked = len(segs) > 0
    pairs, column, ins, stat = attention_specs(length, width, masked)
    work = 2 * pairs * length * length
    return pl.pallas_call(
        functools.partial(forward_kernel, block=block, masked=masked),
        grid=(pairs,),
        in_specs=ins,
        out_specs=[column(0), stat],
        out_shape=[
            jax.ShapeDtypeStruct((length, width), BF16),
            jax.ShapeDtypeStruct((pairs, length, 2), F32),
        ],
        compiler_params=room(26),
        cost_estimate=pl.CostEstimate(
            flops=work * 64 * 16, bytes_accessed=length * width * 8, transcendentals=work
        ),
    )(*segs, qkv, qkv, qkv)


def attend_back(qkv, out, grad, lse, segs, block, first=()):
    length, width = qkv.shape[0], qkv.shape[1] // 3
    masked = len(segs) > 0
    pairs, column, ins, stat = attention_specs(length, width, masked)
    work = 2 * pairs * length * length
    return pl.pallas_call(
        functools.partial(backward_kernel, block=block, masked=masked, first=len(first)),
        grid=(pairs,),
        in_specs=ins
        + [column(0), column(0), stat]
        + [pl.BlockSpec(memory_space=pl.ANY)] * len(first),
        out_specs=pl.BlockSpec((length, 3 * width), lambda p: (0, 0)),
        out_shape=jax.ShapeDtypeStruct((length, 3 * width), BF16),
        scratch_shapes=[pltpu.VMEM((128, length), F32)] * 2,
        compiler_params=room(27),
        cost_estimate=pl.CostEstimate(
            flops=work * 64 * 40, bytes_accessed=length * width * 16, transcendentals=work
        ),
    )(*segs, qkv, qkv, qkv, out, grad, lse, *first)


def sincos_table(count_pos, count_col):
    position = np.arange(count_pos).astype(np.float32)[:, None]
    column = np.arange(count_col)
    exponent = (2 * (column // 2)).astype(np.float32) / np.float32(count_col)
    angles = position / np.power(np.float32(10000.0), exponent)[None, :]
    table = np.where(column[None, :] % 2 == 0, np.sin(angles), np.cos(angles))
    return table.astype(np.float32)


def shape(rows, cols, dtype):
    return jax.ShapeDtypeStruct((rows, cols), dtype)


def cost(flops, moved, special=0):
    return pl.CostEstimate(flops=flops, bytes_accessed=moved, transcendentals=special)


def norm_parts(values):
    average = jnp.mean(values, axis=-1, keepdims=True)
    centred = values - average
    variance = jnp.mean(centred * centred, axis=-1, keepdims=True)
    inv_std = lax.rsqrt(variance + NORM_EPS)
    return centred * inv_std, inv_std


def norm_back(gradient, normed, inv_std, gain):
    scaled = gradient * gain
    return inv_std * (
        scaled
        - jnp.mean(scaled, axis=-1, keepdims=True)
        - normed * jnp.mean(scaled * normed, axis=-1, keepdims=True)
    )


def column_sum(values):
    return jnp.sum(values, axis=0, keepdims=True)


def mm_grad(left, right):
    return jnp.einsum("sk,sn->kn", left, right, preferred_element_type=F32)


def gelu_parts(u):
    cdf = 0.5 + 0.5 * lax.erf(u * 0.7071067811865476)
    bell = jnp.exp(u * u * -0.5)
    return u * cdf, cdf + u * (bell * 0.3989422804014327)


class Vectors:
    def __init__(self, arrays):
        self.at, self.size, total = {}, {}, 0
        for name, array in arrays.items():
            self.at[name], self.size[name] = total, array.shape[0]
            total += array.shape[0]
        self.total = total
        self.row = jnp.concatenate(list(arrays.values())).astype(F32).reshape(1, total)

    def of(self, ref, name, first=0, count=None):
        at = self.at[name] + first
        return ref[:, at : at + (self.size[name] - first if count is None else count)]


def group_kernel(place, weight, inputs, *outs):
    width = weight.shape[1] // 3
    part = width // 4
    rows = inputs.shape[0]
    for k in range(3):
        outs[1 + k][:rows, :] = inputs[...]
    for g in range(4):
        cols = []
        for c in range(3):
            cols.append(weight[:, c * width + g * part : c * width + (g + 1) * part])
            cols.append(jnp.zeros((weight.shape[0], 256 - part), BF16))
        piece = jnp.concatenate(cols, axis=1)

        @pl.when(place[0] == g)
        def _():
            outs[0][...] = piece

        half = piece.shape[0] // 2
        own = jnp.where(place[1] == 0, piece[:half], piece[half:])
        for k in range(1, 4):

            @pl.when((place[0] + k) % 4 == g)
            def _():
                outs[k][rows:, :] = own


def group_pieces(weight, inputs, place):
    rows, count = weight.shape[0], inputs.shape[0]
    outs = [shape(rows, 768, BF16)] + [shape(count + rows // 2, 768, BF16)] * 3
    whole = lambda a: pl.BlockSpec(a.shape, lambda i, s: (0, 0))
    return pl.pallas_call(
        group_kernel,
        grid_spec=pltpu.PrefetchScalarGridSpec(
            num_scalar_prefetch=1,
            grid=(1,),
            in_specs=[whole(weight), whole(inputs)],
            out_specs=[whole(a) for a in outs],
        ),
        out_shape=outs,
        compiler_params=room(10),
    )(place, weight, inputs)


def enc_in_kernel(place, *refs, vectors):
    own, piece, others, swapped, vec = refs[0], refs[1], refs[2:5], refs[5], refs[6]
    qkv_ref, low_ref, weight_ref = refs[7:]
    tokens, rows = own.shape[0], piece.shape[0]
    half = rows // 2
    weight_ref[pl.ds(pl.multiple_of(place[0] * rows, 16), rows), :] = piece[...]
    for k in range(1, 4):
        to = ((place[0] + 4 - k) % 4) * rows
        mine = pl.multiple_of(to + place[1] * half, 16)
        weight_ref[pl.ds(mine, half), :] = others[k - 1][tokens:, :]
        rest = pl.multiple_of(to + (1 - place[1]) * half, 16)
        weight_ref[pl.ds(rest, half), :] = swapped[(k - 1) * half : k * half, :]
    biases = []
    for first in (0, 768):
        groups = [vectors.of(vec, "enc_qv_bias", first + g * 192, 192) for g in range(4)]
        biases += [pick(groups, place[0]), jnp.zeros((1, 64), F32)]
    bias = jnp.concatenate(biases[:2] + [jnp.zeros((1, 256), F32)] + biases[2:], axis=1)
    scale = jnp.where(lax.broadcasted_iota(jnp.int32, (1, 768), 1) < 256, 0.125, 1.0)
    gain, offset = vectors.of(vec, "enc_norm1_gain"), vectors.of(vec, "enc_norm1_shift")
    for k in range(4):
        inputs = own[...] if k == 0 else others[k - 1][:tokens, :]
        normed, _ = norm_parts(inputs.astype(F32))
        low = (normed * gain + offset).astype(BF16)
        out = pl.ds(k * tokens, tokens)
        low_ref[out, :] = low
        qkv_ref[out, :] = ((dot_nn(low, weight_ref[...]) + bias) * scale).astype(BF16)


def enc_in(own, piece, others, swapped, vectors, place):
    tokens, width = own.shape
    rows = 4 * tokens
    whole = lambda a: pl.BlockSpec(a.shape, lambda i, s: (0, 0))
    outs = [shape(rows, 768, BF16), shape(rows, width, BF16), shape(width, 768, BF16)]
    return pl.pallas_call(
        functools.partial(enc_in_kernel, vectors=vectors),
        grid_spec=pltpu.PrefetchScalarGridSpec(
            num_scalar_prefetch=1,
            grid=(1,),
            in_specs=[whole(a) for a in (own, piece, *others, swapped, vectors.row)],
            out_specs=[whole(a) for a in outs],
        ),
        out_shape=outs,
        compiler_params=room(20),
        cost_estimate=cost(2 * rows * width * 768, rows * width * 8),
    )(place, own, piece, *others, swapped, vectors.row)


MATRIX_SPECS = [
    pl.BlockSpec((1, 768, 768), lambda j, s: (4, 0, 0)),
    pl.BlockSpec((1, 768, 768), lambda j, s: (5 + j, 0, 0)),
    pl.BlockSpec((4, 192, 768), lambda j, s: (0, j, 0)),
]


def enc_block_kernel(place, *refs, vectors):
    parts, (x, proj, fc1, fc2, to_dec, send_map, vec) = refs[:4], refs[4:11]
    att_ref, x1_ref, low_ref, act_ref, slope_ref, y_ref, *sends, total = refs[11:]
    step = pl.program_id(0)

    @pl.when(step == 0)
    def _():
        groups = [part[...] for part in parts]
        att = jnp.concatenate([pick(groups, (place[0] + 4 - g) % 4) for g in range(4)], axis=1)
        att_ref[...] = att
        x1 = x[...].astype(F32) + (dot_nn(att, proj[0]) + vectors.of(vec, "enc_proj_bias"))
        x1_ref[...] = x1
        normed, _ = norm_parts(x1)
        gain, offset = vectors.of(vec, "enc_norm2_gain"), vectors.of(vec, "enc_norm2_shift")
        low_ref[...] = (normed * gain + offset).astype(BF16)
        total[...] = x1 + vectors.of(vec, "enc_fc2_bias")

    bias = pick([vectors.of(vec, "enc_fc1_bias", j * 768, 768) for j in range(4)], step)
    pre = dot_nn(low_ref[...], fc1[0]) + bias
    act, slope = gelu_parts(pre)
    act = act.astype(BF16)
    act_ref[...] = act
    slope_ref[...] = slope.astype(BF16)
    total[...] += dot_nn(act, fc2[...].reshape(768, 768))

    @pl.when(step == 3)
    def _():
        y = total[...].astype(BF16)
        y_ref[...] = y
        reduced = dot_nn(y, to_dec[...]).astype(BF16)
        send = dot_nn(send_map[...], reduced).astype(BF16)
        for k in range(4):
            sends[k][...] = send[k * CAP : (k + 1) * CAP, :]


def enc_block(parts, x, matrices, to_dec, send_map, vectors, place):
    rows, width = x.shape
    whole = lambda a: pl.BlockSpec(a.shape, lambda j, s: (0,) * len(a.shape))
    chunk = pl.BlockSpec((rows, 768), lambda j, s: (0, j))
    outs = [
        shape(rows, width, BF16),
        shape(rows, width, F32),
        shape(rows, width, BF16),
        shape(rows, 4 * width, BF16),
        shape(rows, 4 * width, BF16),
        shape(rows, width, BF16),
        *[shape(CAP, DD, BF16)] * 4,
    ]
    return pl.pallas_call(
        functools.partial(enc_block_kernel, vectors=vectors),
        grid_spec=pltpu.PrefetchScalarGridSpec(
            num_scalar_prefetch=1,
            grid=(4,),
            in_specs=[whole(a) for a in (*parts, x)]
            + MATRIX_SPECS
            + [whole(a) for a in (to_dec, send_map, vectors.row)],
            out_specs=[
                chunk if a.shape[-1] == 4 * width else whole(a) for a in outs
            ],
            scratch_shapes=[pltpu.VMEM((rows, width), F32)],
        ),
        out_shape=outs,
        compiler_params=room(18),
        cost_estimate=cost(rows * width * width * 20, width * width * 20, rows * width * 8),
    )(place, *parts, x, *[matrices] * 3, to_dec, send_map, vectors.row)


def enc_block_back_kernel(place, *refs, vectors, first):
    parts, (send_map, to_dec, x1, y, low, att) = refs[:4], refs[4:10]
    act, slope, proj, fc1, fc2, vec = refs[10:16]
    refs = refs[16 + first :]
    fc1_g, fc2_g, fc1_b, gx1_ref, proj_g, to_dec_g = refs[:6]
    gatt_refs, (fc2_b, gain_g, shift_g, proj_b) = refs[6:10], refs[10:14]
    gz, gy, back, low_turned = refs[14:]
    step = pl.program_id(0)

    @pl.when(step == 0)
    def _():
        rows = jnp.concatenate([part[...] for part in parts], axis=0)
        reduced = dot_nn(send_map[...], rows).astype(BF16)
        to_dec_g[...] = dot_nn(y[...].T, reduced).astype(BF16)
        grad = dot_nt(reduced, to_dec[...])
        gy[...] = grad
        gz[...] = grad.astype(BF16)
        fc2_b[...] = column_sum(grad.astype(BF16).astype(F32))
        back[...] = jnp.zeros_like(back)
        low_turned[...] = low[...].T

    fc2_g[...] = dot_nn(act[...].T, gz[...]).astype(BF16)
    gpre = dot_nt(gz[...], fc2[...].reshape(768, 768)) * slope[...].astype(F32)
    gpre = gpre.astype(BF16)
    fc1_b[...] = column_sum(gpre.astype(F32))
    fc1_g[...] = dot_nn(low_turned[...], gpre).astype(BF16)
    back[...] += dot_nt(gpre, fc1[0])

    @pl.when(step == 3)
    def _():
        normed, inv_std = norm_parts(x1[...])
        total = back[...]
        gain_g[...] = column_sum(total * normed)
        shift_g[...] = column_sum(total)
        gx1 = gy[...] + norm_back(total, normed, inv_std, vectors.of(vec, "enc_norm2_gain"))
        gx1_ref[...] = gx1
        go = gx1.astype(BF16)
        proj_b[...] = column_sum(go.astype(F32))
        proj_g[...] = dot_nn(att[...].T, go).astype(BF16)
        gatt = dot_nt(go, proj[0]).astype(BF16)
        groups = [gatt[:, g * 192 : (g + 1) * 192] for g in range(4)]
        for k in range(4):
            gatt_refs[k][...] = pick(groups, (place[0] + k) % 4)


def enc_block_back(
    parts, send_map, to_dec, x1, y, low, att, act, slope, matrices, vectors, place, first
):
    rows, width = x1.shape
    whole = lambda a: pl.BlockSpec(a.shape, lambda j, s: (0,) * len(a.shape))
    columns = lambda count: pl.BlockSpec((count, 768), lambda j, s: (0, j))
    rest = [
        shape(rows, width, F32),
        shape(width, width, BF16),
        shape(width, DD, BF16),
        *[shape(rows, 192, BF16)] * 4,
        *[shape(1, width, F32)] * 4,
    ]
    return pl.pallas_call(
        functools.partial(enc_block_back_kernel, vectors=vectors, first=len(first)),
        grid_spec=pltpu.PrefetchScalarGridSpec(
            num_scalar_prefetch=1,
            grid=(4,),
            in_specs=[whole(a) for a in (*parts, send_map, to_dec, x1, y, low, att)]
            + [columns(rows), columns(rows), *MATRIX_SPECS, whole(vectors.row)]
            + [pl.BlockSpec(memory_space=pl.ANY)] * len(first),
            out_specs=[
                columns(width),
                pl.BlockSpec((768, width), lambda j, s: (j, 0)),
                columns(1),
            ]
            + [whole(a) for a in rest],
            scratch_shapes=[
                pltpu.VMEM((rows, width), BF16),
                pltpu.VMEM((rows, width), F32),
                pltpu.VMEM((rows, width), F32),
                pltpu.VMEM((width, rows), BF16),
            ],
        ),
        out_shape=[
            shape(width, 4 * width, BF16),
            shape(4 * width, width, BF16),
            shape(1, 4 * width, F32),
            *rest,
        ],
        compiler_params=room(32),
        cost_estimate=cost(rows * width * width * 40, width * width * 40),
    )(
        place,
        *parts,
        send_map,
        to_dec,
        x1,
        y,
        low,
        att,
        act,
        slope,
        *[matrices] * 3,
        vectors.row,
        *first,
    )


def enc_in_back_kernel(*refs, vectors):
    inputs, (grad, weight, vec) = refs[:4], refs[4:7]
    own_ref, others, (gain_g, shift_g, grad_sum) = refs[7], refs[8:11], refs[11:]
    tokens = inputs[0].shape[0]
    gains = shifts = 0.0
    for k in range(4):
        part = dot_nt(grad[pl.ds(k * tokens, tokens), :], weight[...])
        normed, _ = norm_parts(inputs[k][:tokens, :].astype(F32))
        gains = gains + column_sum(part * normed)
        shifts = shifts + column_sum(part)
        if k == 0:
            own_ref[...] = part
        else:
            others[k - 1][...] = part.astype(BF16)
    gain_g[...] = gains
    shift_g[...] = shifts
    grad_sum[...] = column_sum(grad[...].astype(F32))


def enc_in_back(inputs, grad, weight, vectors):
    tokens, width = inputs[0].shape
    outs = [shape(tokens, width, F32)] + [shape(tokens, width, BF16)] * 3
    outs += [shape(1, width, F32)] * 2 + [shape(1, 768, F32)]
    return pl.pallas_call(
        functools.partial(enc_in_back_kernel, vectors=vectors),
        out_shape=outs,
        compiler_params=room(14),
        cost_estimate=cost(8 * tokens * width * 768, tokens * width * 32),
    )(*inputs, grad, weight, vectors.row)


def enc_end_kernel(x, gx1, own, a, b, c, vec, out, *, vectors):
    normed, inv_std = norm_parts(x[...].astype(F32))
    back = own[...] + (a[...].astype(F32) + b[...].astype(F32) + c[...].astype(F32))
    out[...] = gx1[...] + norm_back(back, normed, inv_std, vectors.of(vec, "enc_norm1_gain"))


def enc_end(x, gx1, back, vectors):
    return pl.pallas_call(
        functools.partial(enc_end_kernel, vectors=vectors),
        out_shape=shape(*x.shape, F32),
        compiler_params=room(8),
    )(x, gx1, *back, vectors.row)


def dec_in_kernel(*refs, vectors):
    parts, (restore, slots, table, weight, vec) = refs[:4], refs[4:9]
    grid_ref, low_ref, qkv_ref = refs[9:]
    rows = jnp.concatenate([part[...] for part in parts], axis=0)
    order = restore[...]
    hot = jnp.where(order == slots[...], 1.0, 0.0).astype(BF16)
    placed = dot_nn(hot, rows)
    grid = placed + jnp.where(order >= VIS, vectors.of(vec, "mask_token"), 0.0) + table[...]
    grid_ref[...] = grid
    normed, _ = norm_parts(grid)
    low = normed * vectors.of(vec, "dec_norm1_gain") + vectors.of(vec, "dec_norm1_shift")
    low = low.astype(BF16)
    low_ref[...] = low
    packed = dot_nn(low, weight[...])
    queries = packed[:, :DD] + vectors.of(vec, "dec_qv_bias", 0, DD)
    qkv_ref[:, :DD] = (queries * 0.125).astype(BF16)
    qkv_ref[:, DD : 2 * DD] = packed[:, DD : 2 * DD].astype(BF16)
    values = packed[:, 2 * DD :] + vectors.of(vec, "dec_qv_bias", DD, DD)
    qkv_ref[:, 2 * DD :] = values.astype(BF16)


def dec_in(parts, restore, slots, table, weight, vectors, tile):
    rows = table.shape[0]
    row = lambda n: pl.BlockSpec((tile, n), lambda i: (i, 0))
    whole = lambda a: pl.BlockSpec(a.shape, lambda i: (0, 0))
    return pl.pallas_call(
        functools.partial(dec_in_kernel, vectors=vectors),
        grid=(rows // tile,),
        in_specs=[whole(a) for a in parts]
        + [row(1), whole(slots), row(DD), whole(weight), whole(vectors.row)],
        out_specs=[row(DD), row(DD), row(3 * DD)],
        out_shape=[shape(rows, DD, F32), shape(rows, DD, BF16), shape(rows, 3 * DD, BF16)],
        compiler_params=room(24),
        cost_estimate=cost(rows * DD * DD * 8, rows * DD * 16),
    )(*parts, restore, slots, table, weight, vectors.row)


def dec_in_back_kernel(grad, weight, grid, gx1, restore, column, slots, vec, *outs, vectors):
    slot_refs, (gain_g, shift_g, mask_g, grad_sum, total) = outs[:4], outs[4:]
    step = pl.program_id(0)

    @pl.when(step == 0)
    def _():
        for ref in (gain_g, shift_g, mask_g, grad_sum, total):
            ref[...] = jnp.zeros_like(ref)

    back = dot_nt(grad[...], weight[...])
    normed, inv_std = norm_parts(grid[...])
    gain_g[...] += column_sum(back * normed)
    shift_g[...] += column_sum(back)
    grad_sum[...] += column_sum(grad[...].astype(F32))
    gx = gx1[...] + norm_back(back, normed, inv_std, vectors.of(vec, "dec_norm1_gain"))
    order = restore[0]
    hot = jnp.where(slots[...] == order, 1.0, 0.0).astype(BF16)
    total[...] += dot_nn(hot, gx.astype(BF16))
    mask_g[...] += column_sum(jnp.where(column[...] >= VIS, gx, 0.0))

    @pl.when(step == pl.num_programs(0) - 1)
    def _():
        for k in range(4):
            slot_refs[k][...] = total[k * CAP : (k + 1) * CAP, :].astype(BF16)


def dec_in_back(grad, weight, grid, gx1, restore, column, slots, vectors, tile):
    rows = grid.shape[0]
    row = lambda n: pl.BlockSpec((tile, n), lambda i: (i, 0))
    whole = lambda shape: pl.BlockSpec(shape, lambda i: (0, 0))
    sums = [DD, DD, DD, 3 * DD]
    return pl.pallas_call(
        functools.partial(dec_in_back_kernel, vectors=vectors),
        grid=(rows // tile,),
        in_specs=[
            row(3 * DD),
            whole(weight.shape),
            row(DD),
            row(DD),
            pl.BlockSpec((1, 1, tile), lambda i: (i, 0, 0)),
            row(1),
            whole(slots.shape),
            whole(vectors.row.shape),
        ],
        out_specs=[whole((CAP, DD))] * 4 + [whole((1, n)) for n in sums],
        out_shape=[shape(CAP, DD, BF16)] * 4 + [shape(1, n, F32) for n in sums],
        scratch_shapes=[pltpu.VMEM((4 * CAP, DD), F32)],
        compiler_params=room(16),
        cost_estimate=cost(rows * DD * DD * 8, rows * DD * 16),
    )(grad, weight, grid, gx1, restore, column, slots, vectors.row)


def dec_mid_kernel(x, att, gy, proj, fc1, fc2, vec, *outs, vectors, chunk):
    y_ref, gx1_ref, go_ref, gatt_ref, fc1_g, fc2_g = outs[:6]
    (fc1_b, fc2_b, gain_g, shift_g, proj_b), (act_ref, slope, fc1_sum, fc2_sum) = (
        outs[6:11],
        outs[11:],
    )
    step = pl.program_id(0)

    @pl.when(step == 0)
    def _():
        for ref in (fc1_b, fc2_b, gain_g, shift_g, proj_b, fc1_sum, fc2_sum):
            ref[...] = jnp.zeros_like(ref)

    hidden = fc1.shape[1]
    gain = vectors.of(vec, "dec_norm2_gain")
    x1 = x[...] + (dot_nn(att[...], proj[...]) + vectors.of(vec, "dec_proj_bias"))
    normed, inv_std = norm_parts(x1)
    low = (normed * gain + vectors.of(vec, "dec_norm2_shift")).astype(BF16)
    total = x1 + vectors.of(vec, "dec_fc2_bias")

    def pre_of(c):
        return dot_nn(low, fc1[:, c : c + chunk]) + vectors.of(vec, "dec_fc1_bias", c, chunk)

    pre = pre_of(0)
    for c in range(0, hidden, chunk):
        later = pre_of(c + chunk) if c + chunk < hidden else None
        act, rise = gelu_parts(pre)
        act = act.astype(BF16)
        act_ref[:, c : c + chunk] = act
        slope[:, c : c + chunk] = rise.astype(BF16)
        total = total + dot_nn(act, fc2[c : c + chunk, :])
        pre = later
    y_ref[...] = total.astype(BF16)

    gz = gy[...]
    gz_turned = gz.T
    low_turned = low.T
    fc2_b[...] += column_sum(gz.astype(F32))
    grad = dot_nt(gz, fc2[:chunk, :])
    back = None
    for c in range(0, hidden, chunk):
        later = None
        if c + chunk < hidden:
            later = dot_nt(gz, fc2[c + chunk : c + 2 * chunk, :])
        fc2_sum[:, c : c + chunk] += dot_nn(gz_turned, act_ref[:, c : c + chunk])
        gpre = (grad * slope[:, c : c + chunk].astype(F32)).astype(BF16)
        fc1_b[:, c : c + chunk] += column_sum(gpre.astype(F32))
        fc1_sum[:, c : c + chunk] += dot_nn(low_turned, gpre)
        part = dot_nt(gpre, fc1[:, c : c + chunk])
        back = part if back is None else back + part
        grad = later
    gain_g[...] += column_sum(back * normed)
    shift_g[...] += column_sum(back)
    gx1 = gz.astype(F32) + norm_back(back, normed, inv_std, gain)
    gx1_ref[...] = gx1
    go = gx1.astype(BF16)
    go_ref[...] = go
    proj_b[...] += column_sum(go.astype(F32))
    gatt_ref[...] = dot_nt(go, proj[...]).astype(BF16)

    @pl.when(step == pl.num_programs(0) - 1)
    def _():
        fc1_g[...] = fc1_sum[...].astype(BF16)
        for c in range(0, hidden, chunk):
            fc2_g[c : c + chunk, :] = fc2_sum[:, c : c + chunk].T.astype(BF16)


def dec_mid(x, att, gy, proj, fc1, fc2, vectors, tile, chunk):
    rows, width = x.shape
    hidden = fc1.shape[1]
    row = lambda n: pl.BlockSpec((tile, n), lambda i: (i, 0))
    whole = lambda shape: pl.BlockSpec(shape, lambda i: (0, 0))
    consts = (proj, fc1, fc2, vectors.row)
    shapes = [(width, BF16), (width, F32), (width, BF16), (width, BF16)]
    fixed = [shape(width, hidden, BF16), shape(hidden, width, BF16)]
    fixed += [shape(1, n, F32) for n in (hidden, width, width, width, width)]
    return pl.pallas_call(
        functools.partial(dec_mid_kernel, vectors=vectors, chunk=chunk),
        grid=(rows // tile,),
        in_specs=[row(width)] * 3 + [whole(a.shape) for a in consts],
        out_specs=[row(n) for n, _ in shapes] + [whole(a.shape) for a in fixed],
        out_shape=[shape(rows, n, t) for n, t in shapes] + fixed,
        scratch_shapes=[pltpu.VMEM((tile, hidden), BF16)] * 2
        + [pltpu.VMEM((width, hidden), F32)] * 2,
        compiler_params=room(42),
        cost_estimate=cost(rows * hidden * width * 28, rows * width * 20, rows * hidden * 2),
    )(x, att, gy, *consts)


def widen_kernel(*refs):
    count = len(refs) // 2
    for k in range(count):
        refs[count + k][...] = refs[k][...].astype(F32)


def widen(arrays):
    piece = lambda a: pl.BlockSpec((a.shape[0] // 8, a.shape[1]), lambda i: (i, 0))
    return pl.pallas_call(
        widen_kernel,
        grid=(8,),
        in_specs=[piece(a) for a in arrays],
        out_specs=[piece(a) for a in arrays],
        out_shape=[shape(*a.shape, F32) for a in arrays],
        compiler_params=room(16),
        cost_estimate=cost(0, sum(a.shape[0] * a.shape[1] * 6 for a in arrays)),
    )(*arrays)


def body(
    encoder_input,
    seg_ids,
    vis_slot,
    restore_order,
    enc_norm1_gain,
    enc_norm1_shift,
    enc_qkv_weight,
    enc_qv_bias,
    enc_proj_weight,
    enc_proj_bias,
    enc_norm2_gain,
    enc_norm2_shift,
    enc_fc1_weight,
    enc_fc1_bias,
    enc_fc2_weight,
    enc_fc2_bias,
    to_dec_weight,
    mask_token,
    dec_norm1_gain,
    dec_norm1_shift,
    dec_qkv_weight,
    dec_qv_bias,
    dec_proj_weight,
    dec_proj_bias,
    dec_norm2_gain,
    dec_norm2_shift,
    dec_fc1_weight,
    dec_fc1_bias,
    dec_fc2_weight,
    dec_fc2_bias,
    out_grad,
):
    x_at = lax.axis_index("x")
    core = lax.axis_index("core")
    place = place_of(("x", "core"))
    tokens, width = encoder_input.shape[1:]
    hw = width // 4
    vectors = Vectors(
        {
            "enc_norm1_gain": enc_norm1_gain,
            "enc_norm1_shift": enc_norm1_shift,
            "enc_qv_bias": enc_qv_bias,
            "enc_proj_bias": enc_proj_bias,
            "enc_norm2_gain": enc_norm2_gain,
            "enc_norm2_shift": enc_norm2_shift,
            "enc_fc1_bias": enc_fc1_bias,
            "enc_fc2_bias": enc_fc2_bias,
            "mask_token": mask_token,
            "dec_norm1_gain": dec_norm1_gain,
            "dec_norm1_shift": dec_norm1_shift,
            "dec_qv_bias": dec_qv_bias,
            "dec_proj_bias": dec_proj_bias,
            "dec_norm2_gain": dec_norm2_gain,
            "dec_norm2_shift": dec_norm2_shift,
            "dec_fc1_bias": dec_fc1_bias,
            "dec_fc2_bias": dec_fc2_bias,
        }
    )

    own_input = encoder_input[0]
    piece, *others = exchange(group_pieces(enc_qkv_weight, own_input, place), "x")
    swapped = swap(jnp.concatenate([other[tokens:] for other in others], axis=0))
    inputs = [own_input, *others]

    eighth = hw // 8
    first_row = (core * 4 + lax.axis_index("y")) * eighth
    rows_of = lambda stack: lax.dynamic_slice_in_dim(stack, first_row, eighth, 1)
    strip = [
        rows_of(enc_fc2_weight.reshape(4, hw, width)),
        rows_of(enc_proj_weight[None]),
    ]
    fc1_rows = lax.dynamic_slice_in_dim(enc_fc1_weight, first_row, eighth, 0)
    strip += [fc1_rows[None, :, k * width : (k + 1) * width] for k in range(4)]
    matrices = lax.all_gather(
        jnp.concatenate(strip, axis=0), ("x", "core", "y"), axis=1, tiled=True
    )

    row_seg = seg_ids[0].reshape(4, tokens)
    row_slot = vis_slot[0].reshape(4, tokens)
    position = jnp.arange(tokens)
    earlier = position[None, :] < position[:, None]
    same_clip = row_seg[:, :, None] == row_seg[:, None, :]
    ranks = jnp.sum(jnp.logical_and(same_clip, earlier), axis=-1)
    turn = (x_at - jnp.arange(4)) % 4
    seg_turned = jnp.take(row_seg, turn, axis=0)
    segs = (seg_turned.reshape(4 * tokens, 1), seg_turned.reshape(1, 4 * tokens))
    own_seg = lax.dynamic_index_in_dim(row_seg, x_at, 0, keepdims=False)
    own_rank = lax.dynamic_index_in_dim(ranks, x_at, 0, keepdims=False)
    cap_index = jnp.arange(4 * CAP)
    clip_to = (x_at + cap_index // CAP) % 4
    send_map = jnp.logical_and(
        own_seg[None, :] == clip_to[:, None],
        own_rank[None, :] == (cap_index % CAP)[:, None],
    ).astype(BF16)
    send_back = jnp.logical_and(
        own_seg[:, None] == clip_to[None, :],
        own_rank[:, None] == (cap_index % CAP)[None, :],
    ).astype(BF16)
    chosen = jnp.logical_and(
        seg_turned[:, None, :] == x_at,
        jnp.take(ranks, turn, axis=0)[:, None, :] == jnp.arange(CAP)[None, :, None],
    )
    slot_turned = jnp.take(row_slot, turn, axis=0)
    slot_vis = jnp.sum(jnp.where(chosen, slot_turned[:, None, :] + 1, 0), axis=-1) - 1
    restore_row = restore_order[0, 0]
    restore_col = restore_row[:, None]
    restore_row = restore_row.reshape(2, 1, FULL // 2)
    table = jnp.asarray(sincos_table(FULL, DD))

    qkv, first_in, qkv_mine = enc_in(own_input, piece, others, swapped, vectors, place)
    att_mine, enc_lse = attend(qkv, segs, 128)
    blocks = att_mine.reshape(4, tokens, 256)
    parts = exchange([blocks[(4 - k) % 4, :, :hw] for k in range(4)], "x")
    attended, enc_x1, second_in, enc_act, enc_slope, enc_low, *sends = enc_block(
        parts, own_input, matrices, to_dec_weight, send_map, vectors, place
    )

    received = exchange(sends, "x")
    grid, dec_in_low, dec_qkv = dec_in(
        received,
        restore_col,
        slot_vis.reshape(1, 4 * CAP),
        table,
        dec_qkv_weight,
        vectors,
        FULL // 2,
    )
    dec_att, dec_lse = attend(dec_qkv, (), 224)

    dec_gz = out_grad[0, 0]
    dec_out, dec_gx1, dec_go, dec_gatt, dec_fc1_g, dec_fc2_g, *dec_sums = dec_mid(
        grid,
        dec_att,
        dec_gz,
        dec_proj_weight,
        dec_fc1_weight,
        dec_fc2_weight,
        vectors,
        FULL // 2,
        512,
    )
    dec_fc1_b, dec_fc2_b, dec_gain2_g, dec_shift2_g, dec_proj_b = dec_sums
    dec_gqkv = attend_back(dec_qkv, dec_att, dec_gatt, dec_lse, (), 112)
    *slot_grads, dec_gain1_g, dec_shift1_g, mask_g, dec_gqkv_sum = dec_in_back(
        dec_gqkv,
        dec_qkv_weight,
        grid,
        dec_gx1,
        restore_row,
        restore_col,
        slot_vis.reshape(4 * CAP, 1),
        vectors,
        FULL // 2,
    )
    slot_grads, dec_in_low, dec_att = lax.optimization_barrier((slot_grads, dec_in_low, dec_att))
    low_grad = lambda left, right: mm_grad(left, right).astype(BF16)
    dec_early = (low_grad(dec_in_low, dec_gqkv), low_grad(dec_att, dec_go), dec_fc1_g, dec_fc2_g)

    returned = exchange(slot_grads, "x", -1)
    enc_fc1_g, enc_fc2_g, enc_fc1_b, enc_gx1, enc_proj_g, to_dec_g, *rest = enc_block_back(
        returned,
        send_back,
        to_dec_weight,
        enc_x1,
        enc_low,
        second_in,
        attended,
        enc_act,
        enc_slope,
        matrices,
        vectors,
        place,
        dec_early[:2],
    )
    gatt_parts, (enc_fc2_b, enc_gain2_g, enc_shift2_g, enc_proj_b) = rest[:4], rest[4:]
    columns = lambda array, which: lax.dynamic_slice_in_dim(
        array, which * (array.shape[1] // 2), array.shape[1] // 2, 1
    )

    def halves(make):
        return make(core), make(1 - core)

    early = (*dec_early, enc_proj_g, enc_fc1_g, enc_fc2_g, to_dec_g)
    gatt_mine = jnp.concatenate(exchange(gatt_parts, "x"), axis=0)
    gatt_mine = jnp.pad(gatt_mine, ((0, 0), (0, 64)))
    def finish():
        gqkv = attend_back(qkv, att_mine, gatt_mine, enc_lse, segs, 128, early)
        own_back, *others, gain1_g, shift1_g, gqkv_sum = enc_in_back(
            inputs, gqkv, qkv_mine, vectors
        )

        qv = jnp.zeros((2, 4, hw), F32)
        qv = lax.dynamic_update_index_in_dim(
            qv, jnp.stack([gqkv_sum[0, :hw], gqkv_sum[0, 512 : 512 + hw]]), x_at, 1
        )
        small = [
            gain1_g,
            shift1_g,
            qv.reshape(1, 2 * width),
            enc_proj_b,
            enc_gain2_g,
            enc_shift2_g,
            enc_fc1_b,
            enc_fc2_b,
            mask_g,
            dec_gain1_g,
            dec_shift1_g,
            dec_gqkv_sum[:, :DD],
            dec_gqkv_sum[:, 2 * DD :],
            dec_proj_b,
            dec_gain2_g,
            dec_shift2_g,
            dec_fc1_b,
            dec_fc2_b,
        ]
        sizes = [v.shape[1] for v in small]
        vector = jnp.concatenate([*small, jnp.zeros((1, 14336 - sum(sizes)), F32)], axis=1)
        terms = spread(vector.reshape(112, 128), "x")
        vector = ((terms[0] + terms[1]) + (terms[2] + terms[3])).reshape(4, 56, 64)
        extra = lax.dynamic_index_in_dim(vector, x_at, 0, keepdims=False).astype(BF16)
        extra = jnp.pad(extra, ((0, width - 56), (0, 0)))

        def qkv_half(which):
            grad = low_grad(columns(first_in, which), gqkv)
            grad = [grad[:, c * 256 : c * 256 + hw] for c in range(3)]
            more = lax.dynamic_slice_in_dim(extra, which * (width // 2), width // 2, 0)
            return jnp.concatenate([*grad, more], axis=1)


        qkv_sum, vec_sum = tail_sum(*halves(qkv_half))
        back = exchange([None, *others], "x", -1)
        gx = enc_end(own_input, enc_gx1, (own_back, *back[1:]), vectors)
        return qkv_sum, vec_sum, gx

    def nothing():
        return tuple(
            jnp.zeros(dims, F32)
            for dims in ((width, 3 * width), (width, 256), (tokens, width))
        )

    rest_grads = lax.psum(early, ALL)
    qkv_grad, vector, input_grad = lax.cond(seg_ids[0, 0] >= 0, finish, nothing)
    vector = vector[:56].reshape(56, 4, 64).transpose(1, 0, 2).reshape(14336)
    sizes = [width, width, 2 * width, width, width, width, 4 * width, width, DD]
    sizes += [DD, DD, 2 * DD, DD, DD, DD, 4 * DD, DD]
    cuts = [int(c) for c in np.cumsum(sizes)]
    v = jnp.split(vector, cuts)

    dec_qkv_g, dec_proj_g, dec_fc1_g, dec_fc2_g, *rest_grads = widen(rest_grads)
    enc_proj_g, enc_fc1_g, enc_fc2_g, to_dec_g = rest_grads
    return (
        dec_out[None, None],
        input_grad[None],
        v[0],
        v[1],
        qkv_grad,
        v[2],
        enc_proj_g,
        v[3],
        v[4],
        v[5],
        enc_fc1_g,
        v[6],
        enc_fc2_g,
        v[7],
        to_dec_g,
        v[8],
        v[9],
        v[10],
        dec_qkv_g,
        v[11],
        dec_proj_g,
        v[12],
        v[13],
        v[14],
        dec_fc1_g,
        v[15],
        dec_fc2_g,
        v[16],
    )


def solution(mesh):
    fine = Mesh(mesh.devices.reshape(4, 4, 2, 4), ALL)
    row, shared, split = P(WIDE, None), P(), P("x", None)
    return jax.shard_map(
        body,
        mesh=fine,
        in_specs=(
            P(WIDE, "x", None),
            row,
            row,
            P(WIDE, "x", None),
            shared,
            shared,
            split,
            shared,
            split,
            shared,
            shared,
            shared,
            split,
            shared,
            split,
        )
        + (shared,) * 15
        + (P(WIDE, "x", None, None),),
        out_specs=(P(WIDE, "x", None, None), P(WIDE, "x", None)) + (shared,) * 26,
        check_vma=False,
    )
```

```python
import functools

import jax
import jax.numpy as jnp
import numpy as np
from jax import lax
from jax.experimental import pallas as pl
from jax.experimental.pallas import tpu as pltpu
from jax.sharding import Mesh
from jax.sharding import PartitionSpec as P

HEADS = 12
DD = 384
DHEADS = 6
VIS = 157
FULL = 1568
CAP = 64
NORM_EPS = 1e-06
NEG_LARGE = -1e30
ALL = ("z", "y", "core", "x")
WIDE = ("z", "y", "core")
F32 = jnp.float32
BF16 = jnp.bfloat16


def room(mebibytes):
    return pltpu.CompilerParams(vmem_limit_bytes=mebibytes << 20)


def shift(value, axis, step):
    return lax.ppermute(value, axis, [(i, (i + step) % 4) for i in range(4)])


def swap(value):
    return lax.ppermute(value, "core", [(0, 1), (1, 0)])


def spread(piece, axis):
    across = shift(piece, axis, 2)
    return [piece, shift(piece, axis, 1), across, shift(piece, axis, 3)]


def exchange(pieces, axis, sign=1):
    far = shift(pieces[2], axis, 2)
    return [pieces[0], shift(pieces[1], axis, sign), far, shift(pieces[3], axis, -sign)]


def reduce_phase(current, axis):
    rows = current.shape[0] // 4
    index = lax.axis_index(axis)
    got = []
    for step in (2, 1, 3):
        piece = lax.dynamic_slice_in_dim(current, ((index + step) % 4) * rows, rows, 0)
        got.append(shift(piece.astype(BF16), axis, step).astype(F32))
    own = lax.dynamic_slice_in_dim(current, index * rows, rows, 0).astype(F32)
    return own + (got[0] + got[1] + got[2])


def sum_vector(vector):
    vector = vector + swap(vector)
    for axis in ("x", "y", "z"):
        parts = spread(vector, axis)
        vector = (parts[0] + parts[1]) + (parts[2] + parts[3])
    return vector


def pick(values, index):
    low = jnp.where(index == 0, values[0], values[1])
    high = jnp.where(index == 2, values[2], values[3])
    return jnp.where(index < 2, low, high)


def place_of(axes):
    return jnp.stack([lax.axis_index(a) for a in axes]).astype(jnp.int32)


def tail_kernel(place, *refs):
    ins, out, extra = refs[:8], refs[8], refs[9]
    half = pl.program_id(0)
    low = out.shape[0] // 4
    for b in range(4):
        rows = pl.ds(b * low, low)
        parts = [jnp.where(half == 0, ins[k][rows, :], ins[4 + k][rows, :]) for k in range(4)]
        parts = [pick(parts, (place[0] + 4 - g) % 4).astype(F32) for g in range(4)]
        to = pl.multiple_of(((place[2] + 4 - b) % 4) * low, 8)
        for c in range(3):
            out[pl.ds(to, low), c * 768 : (c + 1) * 768] = jnp.concatenate(
                [part[:, c * 192 : (c + 1) * 192] for part in parts], axis=1
            )
        extra[pl.ds(to, low), :] = jnp.concatenate([part[:, 576:] for part in parts], axis=1)


def tail_sum(own_half, other_half):
    current = own_half.astype(F32) + swap(other_half).astype(F32)
    current = reduce_phase(current, "y")
    current = reduce_phase(current, "z")
    parts = spread(current.astype(BF16), "z")
    parts = spread(jnp.concatenate(parts, 0), "y")
    mine = spread(jnp.concatenate(parts, 0), "x")
    theirs = [swap(part) for part in mine]
    rows, cols = mine[0].shape
    piece = pl.BlockSpec((rows // 4, cols), lambda h, a, s: (a, 0))
    return pl.pallas_call(
        tail_kernel,
        grid_spec=pltpu.PrefetchScalarGridSpec(
            num_scalar_prefetch=1,
            grid=(2, 4),
            in_specs=[piece] * 8,
            out_specs=[
                pl.BlockSpec(
                    (rows // 4, 4 * count),
                    lambda h, a, s: (((s[3] + h) % 2) * 4 + (s[1] + 4 - a) % 4, 0),
                )
                for count in (576, 64)
            ],
        ),
        out_shape=[jax.ShapeDtypeStruct((2 * rows, 4 * count), F32) for count in (576, 64)],
        compiler_params=room(16),
    )(place_of(("x", "y", "z", "core")), *mine, *theirs)


def dot_nt(left, right):
    return lax.dot_general(left, right, (((1,), (1,)), ((), ())), preferred_element_type=F32)


def dot_nn(left, right):
    return lax.dot_general(left, right, (((1,), (0,)), ((), ())), preferred_element_type=F32)


def low_lanes(rows):
    return lax.broadcasted_iota(jnp.int32, (rows, 128), 1) < 64


def two_heads(ref, at, count):
    pair = ref[pl.ds(at, count), :]
    low, zero = low_lanes(count), jnp.zeros_like(pair)
    return jnp.concatenate([jnp.where(low, pair, zero), jnp.where(low, zero, pair)], axis=0)


def mask_scores(scores, seg_q, seg_k, at, count):
    if seg_q is None:
        return scores
    mine = seg_q[pl.ds(at, count), :]
    allowed = jnp.concatenate([mine, mine], axis=0) == seg_k[...]
    return jnp.where(allowed, scores, NEG_LARGE)


def forward_kernel(*refs, block, masked):
    if masked:
        seg_q, seg_k, q_ref, k_ref, v_ref, out_ref, lse_ref = refs
    else:
        seg_q = seg_k = None
        q_ref, k_ref, v_ref, out_ref, lse_ref = refs
    count = q_ref.shape[0] // block
    low = low_lanes(block)

    def scores_of(i):
        scores = dot_nt(two_heads(q_ref, i * block, block), k_ref[...])
        return mask_scores(scores, seg_q, seg_k, i * block, block)

    scores = scores_of(0)
    for i in range(count):
        later = scores_of(i + 1) if i + 1 < count else None
        peak = jnp.max(scores, axis=1, keepdims=True)
        probs = jnp.exp(scores - peak)
        total = jnp.sum(probs, axis=1, keepdims=True)
        out = dot_nn(probs.astype(BF16), v_ref[...]) * (1.0 / total)
        rows = pl.ds(i * block, block)
        out_ref[rows, :] = jnp.where(low, out[:block], out[block:]).astype(BF16)
        lse = peak + jnp.log(total)
        lse_ref[0, rows, :] = jnp.concatenate([lse[:block], lse[block:]], axis=1)
        scores = later


def backward_kernel(*refs, block, masked, first):
    if masked:
        seg_q, seg_k = refs[:2]
        refs = refs[2:]
    else:
        seg_q = seg_k = None
    q_ref, k_ref, v_ref, out_ref, grad_ref, lse_ref = refs[:6]
    res_ref, k_sum, v_sum = refs[6 + first :]
    length = q_ref.shape[0]
    count = length // block
    low = low_lanes(block)
    pair = pl.program_id(0)
    width = res_ref.shape[1] // 3
    at_q = pl.multiple_of(pair * 128, 128)
    at_k = pl.multiple_of(width + pair * 128, 128)
    at_v = pl.multiple_of(2 * width + pair * 128, 128)

    def front(i):
        queries = two_heads(q_ref, i * block, block)
        grads = two_heads(grad_ref, i * block, block)
        scores = mask_scores(dot_nt(queries, k_ref[...]), seg_q, seg_k, i * block, block)
        return queries, grads, scores, dot_nt(grads, v_ref[...])

    current = front(0)
    for i in range(count):
        later = front(i + 1) if i + 1 < count else None
        queries, grads, scores, probs_grad = current
        rows = pl.ds(i * block, block)
        lse = lse_ref[0, rows, :]
        lse = jnp.concatenate([lse[:, 0:1], lse[:, 1:2]], axis=0)
        inner = grad_ref[rows, :].astype(F32) * out_ref[rows, :].astype(F32)
        zero = jnp.zeros_like(inner)
        inner = jnp.concatenate(
            [
                jnp.sum(jnp.where(low, inner, zero), axis=1, keepdims=True),
                jnp.sum(jnp.where(low, zero, inner), axis=1, keepdims=True),
            ],
            axis=0,
        )
        probs = jnp.exp(scores - lse)
        score_grad = (probs * (probs_grad - inner)).astype(BF16)
        q_grad = dot_nn(score_grad, k_ref[...])
        q_grad = jnp.where(low, q_grad[:block], q_grad[block:]).astype(BF16).astype(F32)
        res_ref[rows, pl.ds(at_q, 128)] = (q_grad * 0.125).astype(BF16)
        v_part = dot_nn(grads.T, probs.astype(BF16))
        k_part = dot_nn(queries.T, score_grad)
        if i == 0:
            k_sum[...] = k_part
            v_sum[...] = v_part
        else:
            k_sum[...] += k_part
            v_sum[...] += v_part
        current = later
    res_ref[:, pl.ds(at_k, 128)] = k_sum[...].T.astype(BF16)
    res_ref[:, pl.ds(at_v, 128)] = v_sum[...].T.astype(BF16)


def attention_specs(length, width, masked):
    pairs = width // 128
    column = lambda first: pl.BlockSpec((length, 128), lambda p: (0, first + p))
    segs = [
        pl.BlockSpec((length, 1), lambda p: (0, 0)),
        pl.BlockSpec((1, length), lambda p: (0, 0)),
    ]
    qkv = [column(0), column(pairs), column(2 * pairs)]
    stat = pl.BlockSpec((1, length, 2), lambda p: (p, 0, 0))
    return pairs, column, (segs if masked else []) + qkv, stat


def attend(qkv, segs, block):
    length, width = qkv.shape[0], qkv.shape[1] // 3
    masked = len(segs) > 0
    pairs, column, ins, stat = attention_specs(length, width, masked)
    work = 2 * pairs * length * length
    return pl.pallas_call(
        functools.partial(forward_kernel, block=block, masked=masked),
        grid=(pairs,),
        in_specs=ins,
        out_specs=[column(0), stat],
        out_shape=[
            jax.ShapeDtypeStruct((length, width), BF16),
            jax.ShapeDtypeStruct((pairs, length, 2), F32),
        ],
        compiler_params=room(26),
        cost_estimate=pl.CostEstimate(
            flops=work * 64 * 16, bytes_accessed=length * width * 8, transcendentals=work
        ),
    )(*segs, qkv, qkv, qkv)


def attend_back(qkv, out, grad, lse, segs, block, first=()):
    length, width = qkv.shape[0], qkv.shape[1] // 3
    masked = len(segs) > 0
    pairs, column, ins, stat = attention_specs(length, width, masked)
    work = 2 * pairs * length * length
    return pl.pallas_call(
        functools.partial(backward_kernel, block=block, masked=masked, first=len(first)),
        grid=(pairs,),
        in_specs=ins
        + [column(0), column(0), stat]
        + [pl.BlockSpec(memory_space=pl.ANY)] * len(first),
        out_specs=pl.BlockSpec((length, 3 * width), lambda p: (0, 0)),
        out_shape=jax.ShapeDtypeStruct((length, 3 * width), BF16),
        scratch_shapes=[pltpu.VMEM((128, length), F32)] * 2,
        compiler_params=room(27),
        cost_estimate=pl.CostEstimate(
            flops=work * 64 * 40, bytes_accessed=length * width * 16, transcendentals=work
        ),
    )(*segs, qkv, qkv, qkv, out, grad, lse, *first)


def sincos_table(count_pos, count_col):
    position = np.arange(count_pos).astype(np.float32)[:, None]
    column = np.arange(count_col)
    exponent = (2 * (column // 2)).astype(np.float32) / np.float32(count_col)
    angles = position / np.power(np.float32(10000.0), exponent)[None, :]
    table = np.where(column[None, :] % 2 == 0, np.sin(angles), np.cos(angles))
    return table.astype(np.float32)


def shape(rows, cols, dtype):
    return jax.ShapeDtypeStruct((rows, cols), dtype)


def cost(flops, moved, special=0):
    return pl.CostEstimate(flops=flops, bytes_accessed=moved, transcendentals=special)


def norm_parts(values):
    average = jnp.mean(values, axis=-1, keepdims=True)
    centred = values - average
    variance = jnp.mean(centred * centred, axis=-1, keepdims=True)
    inv_std = lax.rsqrt(variance + NORM_EPS)
    return centred * inv_std, inv_std


def norm_back(gradient, normed, inv_std, gain):
    scaled = gradient * gain
    return inv_std * (
        scaled
        - jnp.mean(scaled, axis=-1, keepdims=True)
        - normed * jnp.mean(scaled * normed, axis=-1, keepdims=True)
    )


def column_sum(values):
    return jnp.sum(values, axis=0, keepdims=True)


def mm_grad(left, right):
    return jnp.einsum("sk,sn->kn", left, right, preferred_element_type=F32)


def gelu_parts(u):
    cdf = 0.5 + 0.5 * lax.erf(u * 0.7071067811865476)
    bell = jnp.exp(u * u * -0.5)
    return u * cdf, cdf + u * (bell * 0.3989422804014327)


class Vectors:
    def __init__(self, arrays):
        self.at, self.size, total = {}, {}, 0
        for name, array in arrays.items():
            self.at[name], self.size[name] = total, array.shape[0]
            total += array.shape[0]
        self.total = total
        self.row = jnp.concatenate(list(arrays.values())).astype(F32).reshape(1, total)

    def of(self, ref, name, first=0, count=None):
        at = self.at[name] + first
        return ref[:, at : at + (self.size[name] - first if count is None else count)]


def start_kernel(place, weight, inputs, fc2, proj, fc1, *outs):
    strip = outs[4]
    eighth = strip.shape[1]
    for v in range(8):

        @pl.when(place[2] == v)
        def _():
            rows = slice(v * eighth, (v + 1) * eighth)
            for b in range(4):
                strip[b] = fc2[b * 192 + rows.start : b * 192 + rows.stop, :]
                strip[5 + b] = fc1[rows, b * 768 : (b + 1) * 768]
            strip[4] = proj[rows, :]

    width = weight.shape[1] // 3
    part = width // 4
    rows = inputs.shape[0]
    for k in range(3):
        outs[1 + k][:rows, :] = inputs[...]
    for g in range(4):
        cols = []
        for c in range(3):
            cols.append(weight[:, c * width + g * part : c * width + (g + 1) * part])
            cols.append(jnp.zeros((weight.shape[0], 256 - part), BF16))
        piece = jnp.concatenate(cols, axis=1)

        @pl.when(place[0] == g)
        def _():
            outs[0][...] = piece

        half = piece.shape[0] // 2
        own = jnp.where(place[1] == 0, piece[:half], piece[half:])
        for k in range(1, 4):

            @pl.when((place[0] + k) % 4 == g)
            def _():
                outs[k][rows:, :] = own


def start(weight, inputs, fc2, proj, fc1, place):
    rows, count = weight.shape[0], inputs.shape[0]
    outs = [shape(rows, 768, BF16)] + [shape(count + rows // 2, 768, BF16)] * 3
    outs.append(jax.ShapeDtypeStruct((9, rows // 8, 768), BF16))
    whole = lambda a: pl.BlockSpec(a.shape, lambda i, s: (0,) * len(a.shape))
    return pl.pallas_call(
        start_kernel,
        grid_spec=pltpu.PrefetchScalarGridSpec(
            num_scalar_prefetch=1,
            grid=(1,),
            in_specs=[whole(a) for a in (weight, inputs, fc2, proj, fc1)],
            out_specs=[whole(a) for a in outs],
        ),
        out_shape=outs,
        compiler_params=room(24),
    )(place, weight, inputs, fc2, proj, fc1)


def enc_in_kernel(place, *refs, vectors):
    own, piece, others, swapped, vec = refs[0], refs[1], refs[2:5], refs[5], refs[6]
    qkv_ref, low_ref, weight_ref = refs[7:]
    tokens, rows = own.shape[0], piece.shape[0]
    half = rows // 2
    weight_ref[pl.ds(pl.multiple_of(place[0] * rows, 16), rows), :] = piece[...]
    for k in range(1, 4):
        to = ((place[0] + 4 - k) % 4) * rows
        mine = pl.multiple_of(to + place[1] * half, 16)
        weight_ref[pl.ds(mine, half), :] = others[k - 1][tokens:, :]
        rest = pl.multiple_of(to + (1 - place[1]) * half, 16)
        weight_ref[pl.ds(rest, half), :] = swapped[(k - 1) * half : k * half, :]
    biases = []
    for first in (0, 768):
        groups = [vectors.of(vec, "enc_qv_bias", first + g * 192, 192) for g in range(4)]
        biases += [pick(groups, place[0]), jnp.zeros((1, 64), F32)]
    bias = jnp.concatenate(biases[:2] + [jnp.zeros((1, 256), F32)] + biases[2:], axis=1)
    scale = jnp.where(lax.broadcasted_iota(jnp.int32, (1, 768), 1) < 256, 0.125, 1.0)
    gain, offset = vectors.of(vec, "enc_norm1_gain"), vectors.of(vec, "enc_norm1_shift")
    for k in range(4):
        inputs = own[...] if k == 0 else others[k - 1][:tokens, :]
        normed, _ = norm_parts(inputs.astype(F32))
        low = (normed * gain + offset).astype(BF16)
        out = pl.ds(k * tokens, tokens)
        low_ref[out, :] = low
        qkv_ref[out, :] = ((dot_nn(low, weight_ref[...]) + bias) * scale).astype(BF16)


def enc_in(own, piece, others, swapped, vectors, place):
    tokens, width = own.shape
    rows = 4 * tokens
    whole = lambda a: pl.BlockSpec(a.shape, lambda i, s: (0, 0))
    outs = [shape(rows, 768, BF16), shape(rows, width, BF16), shape(width, 768, BF16)]
    return pl.pallas_call(
        functools.partial(enc_in_kernel, vectors=vectors),
        grid_spec=pltpu.PrefetchScalarGridSpec(
            num_scalar_prefetch=1,
            grid=(1,),
            in_specs=[whole(a) for a in (own, piece, *others, swapped, vectors.row)],
            out_specs=[whole(a) for a in outs],
        ),
        out_shape=outs,
        compiler_params=room(20),
        cost_estimate=cost(2 * rows * width * 768, rows * width * 8),
    )(place, own, piece, *others, swapped, vectors.row)


MATRIX_SPECS = [
    pl.BlockSpec((1, 768, 768), lambda j, s: (4, 0, 0)),
    pl.BlockSpec((1, 768, 768), lambda j, s: (5 + j, 0, 0)),
    pl.BlockSpec((4, 192, 768), lambda j, s: (0, j, 0)),
]


def enc_block_kernel(place, *refs, vectors):
    parts, (x, proj, fc1, fc2, to_dec, send_map, vec) = refs[:4], refs[4:11]
    att_ref, x1_ref, low_ref, act_ref, slope_ref, y_ref, *sends, total = refs[11:]
    step = pl.program_id(0)

    @pl.when(step == 0)
    def _():
        groups = [part[...] for part in parts]
        att = jnp.concatenate([pick(groups, (place[0] + 4 - g) % 4) for g in range(4)], axis=1)
        att_ref[...] = att
        x1 = x[...].astype(F32) + (dot_nn(att, proj[0]) + vectors.of(vec, "enc_proj_bias"))
        x1_ref[...] = x1
        normed, _ = norm_parts(x1)
        gain, offset = vectors.of(vec, "enc_norm2_gain"), vectors.of(vec, "enc_norm2_shift")
        low_ref[...] = (normed * gain + offset).astype(BF16)
        total[...] = x1 + vectors.of(vec, "enc_fc2_bias")

    bias = pick([vectors.of(vec, "enc_fc1_bias", j * 768, 768) for j in range(4)], step)
    pre = dot_nn(low_ref[...], fc1[0]) + bias
    act, slope = gelu_parts(pre)
    act = act.astype(BF16)
    act_ref[...] = act
    slope_ref[...] = slope.astype(BF16)
    total[...] += dot_nn(act, fc2[...].reshape(768, 768))

    @pl.when(step == 3)
    def _():
        y = total[...].astype(BF16)
        y_ref[...] = y
        reduced = dot_nn(y, to_dec[...]).astype(BF16)
        send = dot_nn(send_map[...], reduced).astype(BF16)
        for k in range(4):
            sends[k][...] = send[k * CAP : (k + 1) * CAP, :]


def enc_block(parts, x, matrices, to_dec, send_map, vectors, place):
    rows, width = x.shape
    whole = lambda a: pl.BlockSpec(a.shape, lambda j, s: (0,) * len(a.shape))
    chunk = pl.BlockSpec((rows, 768), lambda j, s: (0, j))
    outs = [
        shape(rows, width, BF16),
        shape(rows, width, F32),
        shape(rows, width, BF16),
        shape(rows, 4 * width, BF16),
        shape(rows, 4 * width, BF16),
        shape(rows, width, BF16),
        *[shape(CAP, DD, BF16)] * 4,
    ]
    return pl.pallas_call(
        functools.partial(enc_block_kernel, vectors=vectors),
        grid_spec=pltpu.PrefetchScalarGridSpec(
            num_scalar_prefetch=1,
            grid=(4,),
            in_specs=[whole(a) for a in (*parts, x)]
            + MATRIX_SPECS
            + [whole(a) for a in (to_dec, send_map, vectors.row)],
            out_specs=[
                chunk if a.shape[-1] == 4 * width else whole(a) for a in outs
            ],
            scratch_shapes=[pltpu.VMEM((rows, width), F32)],
        ),
        out_shape=outs,
        compiler_params=room(18),
        cost_estimate=cost(rows * width * width * 20, width * width * 20, rows * width * 8),
    )(place, *parts, x, *[matrices] * 3, to_dec, send_map, vectors.row)


def enc_block_back_kernel(place, *refs, vectors, first):
    parts, (send_map, to_dec, x1, y, low, att) = refs[:4], refs[4:10]
    act, slope, proj, fc1, fc2, vec = refs[10:16]
    refs = refs[16 + first :]
    fc1_g, fc2_g, fc1_b, gx1_ref, proj_g, to_dec_g = refs[:6]
    gatt_refs, (fc2_b, gain_g, shift_g, proj_b) = refs[6:10], refs[10:14]
    gz, gy, back, low_turned = refs[14:]
    step = pl.program_id(0)

    @pl.when(step == 0)
    def _():
        rows = jnp.concatenate([part[...] for part in parts], axis=0)
        reduced = dot_nn(send_map[...], rows).astype(BF16)
        to_dec_g[...] = dot_nn(y[...].T, reduced).astype(BF16)
        grad = dot_nt(reduced, to_dec[...])
        gy[...] = grad
        gz[...] = grad.astype(BF16)
        fc2_b[...] = column_sum(grad.astype(BF16).astype(F32))
        back[...] = jnp.zeros_like(back)
        low_turned[...] = low[...].T

    fc2_g[...] = dot_nn(act[...].T, gz[...]).astype(BF16)
    gpre = dot_nt(gz[...], fc2[...].reshape(768, 768)) * slope[...].astype(F32)
    gpre = gpre.astype(BF16)
    fc1_b[...] = column_sum(gpre.astype(F32))
    fc1_g[...] = dot_nn(low_turned[...], gpre).astype(BF16)
    back[...] += dot_nt(gpre, fc1[0])

    @pl.when(step == 3)
    def _():
        normed, inv_std = norm_parts(x1[...])
        total = back[...]
        gain_g[...] = column_sum(total * normed)
        shift_g[...] = column_sum(total)
        gx1 = gy[...] + norm_back(total, normed, inv_std, vectors.of(vec, "enc_norm2_gain"))
        gx1_ref[...] = gx1
        go = gx1.astype(BF16)
        proj_b[...] = column_sum(go.astype(F32))
        proj_g[...] = dot_nn(att[...].T, go).astype(BF16)
        gatt = dot_nt(go, proj[0]).astype(BF16)
        groups = [gatt[:, g * 192 : (g + 1) * 192] for g in range(4)]
        for k in range(4):
            gatt_refs[k][...] = pick(groups, (place[0] + k) % 4)


def enc_block_back(
    parts, send_map, to_dec, x1, y, low, att, act, slope, matrices, vectors, place, first
):
    rows, width = x1.shape
    whole = lambda a: pl.BlockSpec(a.shape, lambda j, s: (0,) * len(a.shape))
    columns = lambda count: pl.BlockSpec((count, 768), lambda j, s: (0, j))
    rest = [
        shape(rows, width, F32),
        shape(width, width, BF16),
        shape(width, DD, BF16),
        *[shape(rows, 192, BF16)] * 4,
        *[shape(1, width, F32)] * 4,
    ]
    return pl.pallas_call(
        functools.partial(enc_block_back_kernel, vectors=vectors, first=len(first)),
        grid_spec=pltpu.PrefetchScalarGridSpec(
            num_scalar_prefetch=1,
            grid=(4,),
            in_specs=[whole(a) for a in (*parts, send_map, to_dec, x1, y, low, att)]
            + [columns(rows), columns(rows), *MATRIX_SPECS, whole(vectors.row)]
            + [pl.BlockSpec(memory_space=pl.ANY)] * len(first),
            out_specs=[
                columns(width),
                pl.BlockSpec((768, width), lambda j, s: (j, 0)),
                columns(1),
            ]
            + [whole(a) for a in rest],
            scratch_shapes=[
                pltpu.VMEM((rows, width), BF16),
                pltpu.VMEM((rows, width), F32),
                pltpu.VMEM((rows, width), F32),
                pltpu.VMEM((width, rows), BF16),
            ],
        ),
        out_shape=[
            shape(width, 4 * width, BF16),
            shape(4 * width, width, BF16),
            shape(1, 4 * width, F32),
            *rest,
        ],
        compiler_params=room(32),
        cost_estimate=cost(rows * width * width * 40, width * width * 40),
    )(
        place,
        *parts,
        send_map,
        to_dec,
        x1,
        y,
        low,
        att,
        act,
        slope,
        *[matrices] * 3,
        vectors.row,
        *first,
    )


def enc_in_back_kernel(*refs, vectors):
    inputs, (grad, weight, vec) = refs[:4], refs[4:7]
    own_ref, others, (gain_g, shift_g, grad_sum) = refs[7], refs[8:11], refs[11:]
    tokens = inputs[0].shape[0]
    gains = shifts = 0.0
    for k in range(4):
        part = dot_nt(grad[pl.ds(k * tokens, tokens), :], weight[...])
        normed, _ = norm_parts(inputs[k][:tokens, :].astype(F32))
        gains = gains + column_sum(part * normed)
        shifts = shifts + column_sum(part)
        if k == 0:
            own_ref[...] = part
        else:
            others[k - 1][...] = part.astype(BF16)
    gain_g[...] = gains
    shift_g[...] = shifts
    grad_sum[...] = column_sum(grad[...].astype(F32))


def enc_in_back(inputs, grad, weight, vectors):
    tokens, width = inputs[0].shape
    outs = [shape(tokens, width, F32)] + [shape(tokens, width, BF16)] * 3
    outs += [shape(1, width, F32)] * 2 + [shape(1, 768, F32)]
    return pl.pallas_call(
        functools.partial(enc_in_back_kernel, vectors=vectors),
        out_shape=outs,
        compiler_params=room(14),
        cost_estimate=cost(8 * tokens * width * 768, tokens * width * 32),
    )(*inputs, grad, weight, vectors.row)


def enc_end_kernel(x, gx1, own, a, b, c, vec, out, *, vectors):
    normed, inv_std = norm_parts(x[...].astype(F32))
    back = own[...] + (a[...].astype(F32) + b[...].astype(F32) + c[...].astype(F32))
    out[...] = gx1[...] + norm_back(back, normed, inv_std, vectors.of(vec, "enc_norm1_gain"))


def enc_end(x, gx1, back, vectors):
    return pl.pallas_call(
        functools.partial(enc_end_kernel, vectors=vectors),
        out_shape=shape(*x.shape, F32),
        compiler_params=room(8),
    )(x, gx1, *back, vectors.row)


def dec_in_kernel(*refs, vectors):
    parts, (restore, slots, table, weight, vec) = refs[:4], refs[4:9]
    grid_ref, low_ref, qkv_ref = refs[9:]
    rows = jnp.concatenate([part[...] for part in parts], axis=0)
    order = restore[...]
    hot = jnp.where(order == slots[...], 1.0, 0.0).astype(BF16)
    placed = dot_nn(hot, rows)
    grid = placed + jnp.where(order >= VIS, vectors.of(vec, "mask_token"), 0.0) + table[...]
    grid_ref[...] = grid
    normed, _ = norm_parts(grid)
    low = normed * vectors.of(vec, "dec_norm1_gain") + vectors.of(vec, "dec_norm1_shift")
    low = low.astype(BF16)
    low_ref[...] = low
    packed = dot_nn(low, weight[...])
    queries = packed[:, :DD] + vectors.of(vec, "dec_qv_bias", 0, DD)
    qkv_ref[:, :DD] = (queries * 0.125).astype(BF16)
    qkv_ref[:, DD : 2 * DD] = packed[:, DD : 2 * DD].astype(BF16)
    values = packed[:, 2 * DD :] + vectors.of(vec, "dec_qv_bias", DD, DD)
    qkv_ref[:, 2 * DD :] = values.astype(BF16)


def dec_in(parts, restore, slots, table, weight, vectors, tile):
    rows = table.shape[0]
    row = lambda n: pl.BlockSpec((tile, n), lambda i: (i, 0))
    whole = lambda a: pl.BlockSpec(a.shape, lambda i: (0, 0))
    return pl.pallas_call(
        functools.partial(dec_in_kernel, vectors=vectors),
        grid=(rows // tile,),
        in_specs=[whole(a) for a in parts]
        + [row(1), whole(slots), row(DD), whole(weight), whole(vectors.row)],
        out_specs=[row(DD), row(DD), row(3 * DD)],
        out_shape=[shape(rows, DD, F32), shape(rows, DD, BF16), shape(rows, 3 * DD, BF16)],
        compiler_params=room(24),
        cost_estimate=cost(rows * DD * DD * 8, rows * DD * 16),
    )(*parts, restore, slots, table, weight, vectors.row)


def dec_in_back_kernel(grad, weight, grid, gx1, restore, column, slots, vec, *outs, vectors):
    slot_refs, (gain_g, shift_g, mask_g, grad_sum, total) = outs[:4], outs[4:]
    step = pl.program_id(0)

    @pl.when(step == 0)
    def _():
        for ref in (gain_g, shift_g, mask_g, grad_sum, total):
            ref[...] = jnp.zeros_like(ref)

    back = dot_nt(grad[...], weight[...])
    normed, inv_std = norm_parts(grid[...])
    gain_g[...] += column_sum(back * normed)
    shift_g[...] += column_sum(back)
    grad_sum[...] += column_sum(grad[...].astype(F32))
    gx = gx1[...] + norm_back(back, normed, inv_std, vectors.of(vec, "dec_norm1_gain"))
    order = restore[0]
    hot = jnp.where(slots[...] == order, 1.0, 0.0).astype(BF16)
    total[...] += dot_nn(hot, gx.astype(BF16))
    mask_g[...] += column_sum(jnp.where(column[...] >= VIS, gx, 0.0))

    @pl.when(step == pl.num_programs(0) - 1)
    def _():
        for k in range(4):
            slot_refs[k][...] = total[k * CAP : (k + 1) * CAP, :].astype(BF16)


def dec_in_back(grad, weight, grid, gx1, restore, column, slots, vectors, tile):
    rows = grid.shape[0]
    row = lambda n: pl.BlockSpec((tile, n), lambda i: (i, 0))
    whole = lambda shape: pl.BlockSpec(shape, lambda i: (0, 0))
    sums = [DD, DD, DD, 3 * DD]
    return pl.pallas_call(
        functools.partial(dec_in_back_kernel, vectors=vectors),
        grid=(rows // tile,),
        in_specs=[
            row(3 * DD),
            whole(weight.shape),
            row(DD),
            row(DD),
            pl.BlockSpec((1, 1, tile), lambda i: (i, 0, 0)),
            row(1),
            whole(slots.shape),
            whole(vectors.row.shape),
        ],
        out_specs=[whole((CAP, DD))] * 4 + [whole((1, n)) for n in sums],
        out_shape=[shape(CAP, DD, BF16)] * 4 + [shape(1, n, F32) for n in sums],
        scratch_shapes=[pltpu.VMEM((4 * CAP, DD), F32)],
        compiler_params=room(16),
        cost_estimate=cost(rows * DD * DD * 8, rows * DD * 16),
    )(grad, weight, grid, gx1, restore, column, slots, vectors.row)


def dec_mid_kernel(x, att, gy, proj, fc1, fc2, vec, *outs, vectors, chunk):
    y_ref, gx1_ref, go_ref, gatt_ref, fc1_g, fc2_g = outs[:6]
    (fc1_b, fc2_b, gain_g, shift_g, proj_b), (act_ref, slope, fc1_sum, fc2_sum) = (
        outs[6:11],
        outs[11:],
    )
    step = pl.program_id(0)

    @pl.when(step == 0)
    def _():
        for ref in (fc1_b, fc2_b, gain_g, shift_g, proj_b, fc1_sum, fc2_sum):
            ref[...] = jnp.zeros_like(ref)

    hidden = fc1.shape[1]
    gain = vectors.of(vec, "dec_norm2_gain")
    x1 = x[...] + (dot_nn(att[...], proj[...]) + vectors.of(vec, "dec_proj_bias"))
    normed, inv_std = norm_parts(x1)
    low = (normed * gain + vectors.of(vec, "dec_norm2_shift")).astype(BF16)
    total = x1 + vectors.of(vec, "dec_fc2_bias")

    def pre_of(c):
        return dot_nn(low, fc1[:, c : c + chunk]) + vectors.of(vec, "dec_fc1_bias", c, chunk)

    pre = pre_of(0)
    for c in range(0, hidden, chunk):
        later = pre_of(c + chunk) if c + chunk < hidden else None
        act, rise = gelu_parts(pre)
        act = act.astype(BF16)
        act_ref[:, c : c + chunk] = act
        slope[:, c : c + chunk] = rise.astype(BF16)
        total = total + dot_nn(act, fc2[c : c + chunk, :])
        pre = later
    y_ref[...] = total.astype(BF16)

    gz = gy[...]
    gz_turned = gz.T
    low_turned = low.T
    fc2_b[...] += column_sum(gz.astype(F32))
    grad = dot_nt(gz, fc2[:chunk, :])
    back = None
    for c in range(0, hidden, chunk):
        later = None
        if c + chunk < hidden:
            later = dot_nt(gz, fc2[c + chunk : c + 2 * chunk, :])
        fc2_sum[:, c : c + chunk] += dot_nn(gz_turned, act_ref[:, c : c + chunk])
        gpre = (grad * slope[:, c : c + chunk].astype(F32)).astype(BF16)
        fc1_b[:, c : c + chunk] += column_sum(gpre.astype(F32))
        fc1_sum[:, c : c + chunk] += dot_nn(low_turned, gpre)
        part = dot_nt(gpre, fc1[:, c : c + chunk])
        back = part if back is None else back + part
        grad = later
    gain_g[...] += column_sum(back * normed)
    shift_g[...] += column_sum(back)
    gx1 = gz.astype(F32) + norm_back(back, normed, inv_std, gain)
    gx1_ref[...] = gx1
    go = gx1.astype(BF16)
    go_ref[...] = go
    proj_b[...] += column_sum(go.astype(F32))
    gatt_ref[...] = dot_nt(go, proj[...]).astype(BF16)

    @pl.when(step == pl.num_programs(0) - 1)
    def _():
        fc1_g[...] = fc1_sum[...].astype(BF16)
        for c in range(0, hidden, chunk):
            fc2_g[c : c + chunk, :] = fc2_sum[:, c : c + chunk].T.astype(BF16)


def dec_mid(x, att, gy, proj, fc1, fc2, vectors, tile, chunk):
    rows, width = x.shape
    hidden = fc1.shape[1]
    row = lambda n: pl.BlockSpec((tile, n), lambda i: (i, 0))
    whole = lambda shape: pl.BlockSpec(shape, lambda i: (0, 0))
    consts = (proj, fc1, fc2, vectors.row)
    shapes = [(width, BF16), (width, F32), (width, BF16), (width, BF16)]
    fixed = [shape(width, hidden, BF16), shape(hidden, width, BF16)]
    fixed += [shape(1, n, F32) for n in (hidden, width, width, width, width)]
    return pl.pallas_call(
        functools.partial(dec_mid_kernel, vectors=vectors, chunk=chunk),
        grid=(rows // tile,),
        in_specs=[row(width)] * 3 + [whole(a.shape) for a in consts],
        out_specs=[row(n) for n, _ in shapes] + [whole(a.shape) for a in fixed],
        out_shape=[shape(rows, n, t) for n, t in shapes] + fixed,
        scratch_shapes=[pltpu.VMEM((tile, hidden), BF16)] * 2
        + [pltpu.VMEM((width, hidden), F32)] * 2,
        compiler_params=room(42),
        cost_estimate=cost(rows * hidden * width * 28, rows * width * 20, rows * hidden * 2),
    )(x, att, gy, *consts)


def widen_kernel(*refs):
    count = len(refs) // 2
    for k in range(count):
        refs[count + k][...] = refs[k][...].astype(F32)


def widen(arrays):
    piece = lambda a: pl.BlockSpec((a.shape[0] // 8, a.shape[1]), lambda i: (i, 0))
    return pl.pallas_call(
        widen_kernel,
        grid=(8,),
        in_specs=[piece(a) for a in arrays],
        out_specs=[piece(a) for a in arrays],
        out_shape=[shape(*a.shape, F32) for a in arrays],
        compiler_params=room(56),
        cost_estimate=cost(0, sum(a.shape[0] * a.shape[1] * 6 for a in arrays)),
    )(*arrays)


def body(
    encoder_input,
    seg_ids,
    vis_slot,
    restore_order,
    enc_norm1_gain,
    enc_norm1_shift,
    enc_qkv_weight,
    enc_qv_bias,
    enc_proj_weight,
    enc_proj_bias,
    enc_norm2_gain,
    enc_norm2_shift,
    enc_fc1_weight,
    enc_fc1_bias,
    enc_fc2_weight,
    enc_fc2_bias,
    to_dec_weight,
    mask_token,
    dec_norm1_gain,
    dec_norm1_shift,
    dec_qkv_weight,
    dec_qv_bias,
    dec_proj_weight,
    dec_proj_bias,
    dec_norm2_gain,
    dec_norm2_shift,
    dec_fc1_weight,
    dec_fc1_bias,
    dec_fc2_weight,
    dec_fc2_bias,
    out_grad,
):
    x_at = lax.axis_index("x")
    core = lax.axis_index("core")
    place = jnp.stack([x_at, core, core * 4 + lax.axis_index("y")]).astype(jnp.int32)
    tokens, width = encoder_input.shape[1:]
    hw = width // 4
    vectors = Vectors(
        {
            "enc_norm1_gain": enc_norm1_gain,
            "enc_norm1_shift": enc_norm1_shift,
            "enc_qv_bias": enc_qv_bias,
            "enc_proj_bias": enc_proj_bias,
            "enc_norm2_gain": enc_norm2_gain,
            "enc_norm2_shift": enc_norm2_shift,
            "enc_fc1_bias": enc_fc1_bias,
            "enc_fc2_bias": enc_fc2_bias,
            "mask_token": mask_token,
            "dec_norm1_gain": dec_norm1_gain,
            "dec_norm1_shift": dec_norm1_shift,
            "dec_qv_bias": dec_qv_bias,
            "dec_proj_bias": dec_proj_bias,
            "dec_norm2_gain": dec_norm2_gain,
            "dec_norm2_shift": dec_norm2_shift,
            "dec_fc1_bias": dec_fc1_bias,
            "dec_fc2_bias": dec_fc2_bias,
        }
    )

    own_input = encoder_input[0]
    *pieces, strip = start(
        enc_qkv_weight, own_input, enc_fc2_weight, enc_proj_weight, enc_fc1_weight, place
    )
    piece, *others = exchange(pieces, "x")
    swapped = swap(jnp.concatenate([other[tokens:] for other in others], axis=0))
    inputs = [own_input, *others]

    matrices = lax.all_gather(strip, ("x", "core", "y"), axis=1, tiled=True)

    row_seg = seg_ids[0].reshape(4, tokens)
    row_slot = vis_slot[0].reshape(4, tokens)
    position = jnp.arange(tokens)
    earlier = position[None, :] < position[:, None]
    same_clip = row_seg[:, :, None] == row_seg[:, None, :]
    ranks = jnp.sum(jnp.logical_and(same_clip, earlier), axis=-1)
    turn = (x_at - jnp.arange(4)) % 4
    seg_turned = jnp.take(row_seg, turn, axis=0)
    segs = (seg_turned.reshape(4 * tokens, 1), seg_turned.reshape(1, 4 * tokens))
    own_seg = lax.dynamic_index_in_dim(row_seg, x_at, 0, keepdims=False)
    own_rank = lax.dynamic_index_in_dim(ranks, x_at, 0, keepdims=False)
    cap_index = jnp.arange(4 * CAP)
    clip_to = (x_at + cap_index // CAP) % 4
    send_map = jnp.logical_and(
        own_seg[None, :] == clip_to[:, None],
        own_rank[None, :] == (cap_index % CAP)[:, None],
    ).astype(BF16)
    send_back = jnp.logical_and(
        own_seg[:, None] == clip_to[None, :],
        own_rank[:, None] == (cap_index % CAP)[None, :],
    ).astype(BF16)
    chosen = jnp.logical_and(
        seg_turned[:, None, :] == x_at,
        jnp.take(ranks, turn, axis=0)[:, None, :] == jnp.arange(CAP)[None, :, None],
    )
    slot_turned = jnp.take(row_slot, turn, axis=0)
    slot_vis = jnp.sum(jnp.where(chosen, slot_turned[:, None, :] + 1, 0), axis=-1) - 1
    restore_row = restore_order[0, 0]
    restore_col = restore_row[:, None]
    restore_row = restore_row.reshape(2, 1, FULL // 2)
    table = jnp.asarray(sincos_table(FULL, DD))

    qkv, first_in, qkv_mine = enc_in(own_input, piece, others, swapped, vectors, place)
    att_mine, enc_lse = attend(qkv, segs, 128)
    blocks = att_mine.reshape(4, tokens, 256)
    parts = exchange([blocks[(4 - k) % 4, :, :hw] for k in range(4)], "x")
    attended, enc_x1, second_in, enc_act, enc_slope, enc_low, *sends = enc_block(
        parts, own_input, matrices, to_dec_weight, send_map, vectors, place
    )

    received = exchange(sends, "x")
    grid, dec_in_low, dec_qkv = dec_in(
        received,
        restore_col,
        slot_vis.reshape(1, 4 * CAP),
        table,
        dec_qkv_weight,
        vectors,
        FULL // 2,
    )
    dec_att, dec_lse = attend(dec_qkv, (), 224)

    dec_gz = out_grad[0, 0]
    dec_out, dec_gx1, dec_go, dec_gatt, dec_fc1_g, dec_fc2_g, *dec_sums = dec_mid(
        grid,
        dec_att,
        dec_gz,
        dec_proj_weight,
        dec_fc1_weight,
        dec_fc2_weight,
        vectors,
        FULL // 2,
        512,
    )
    dec_fc1_b, dec_fc2_b, dec_gain2_g, dec_shift2_g, dec_proj_b = dec_sums
    dec_gqkv = attend_back(dec_qkv, dec_att, dec_gatt, dec_lse, (), 112)
    *slot_grads, dec_gain1_g, dec_shift1_g, mask_g, dec_gqkv_sum = dec_in_back(
        dec_gqkv,
        dec_qkv_weight,
        grid,
        dec_gx1,
        restore_row,
        restore_col,
        slot_vis.reshape(4 * CAP, 1),
        vectors,
        FULL // 2,
    )
    slot_grads, dec_in_low, dec_att = lax.optimization_barrier((slot_grads, dec_in_low, dec_att))
    low_grad = lambda left, right: mm_grad(left, right).astype(BF16)
    dec_early = (low_grad(dec_in_low, dec_gqkv), low_grad(dec_att, dec_go), dec_fc1_g, dec_fc2_g)

    returned = exchange(slot_grads, "x", -1)
    enc_fc1_g, enc_fc2_g, enc_fc1_b, enc_gx1, enc_proj_g, to_dec_g, *rest = enc_block_back(
        returned,
        send_back,
        to_dec_weight,
        enc_x1,
        enc_low,
        second_in,
        attended,
        enc_act,
        enc_slope,
        matrices,
        vectors,
        place,
        dec_early[:2],
    )
    gatt_parts, (enc_fc2_b, enc_gain2_g, enc_shift2_g, enc_proj_b) = rest[:4], rest[4:]
    columns = lambda array, which: lax.dynamic_slice_in_dim(
        array, which * (array.shape[1] // 2), array.shape[1] // 2, 1
    )

    def halves(make):
        return make(core), make(1 - core)

    early = (*dec_early, enc_proj_g, enc_fc1_g, enc_fc2_g, to_dec_g)
    gatt_mine = jnp.concatenate(exchange(gatt_parts, "x"), axis=0)
    gatt_mine = jnp.pad(gatt_mine, ((0, 0), (0, 64)))
    def finish():
        gqkv = attend_back(qkv, att_mine, gatt_mine, enc_lse, segs, 128, early)
        own_back, *others, gain1_g, shift1_g, gqkv_sum = enc_in_back(
            inputs, gqkv, qkv_mine, vectors
        )

        qv = jnp.zeros((2, 4, hw), F32)
        qv = lax.dynamic_update_index_in_dim(
            qv, jnp.stack([gqkv_sum[0, :hw], gqkv_sum[0, 512 : 512 + hw]]), x_at, 1
        )
        small = [
            gain1_g,
            shift1_g,
            qv.reshape(1, 2 * width),
            enc_proj_b,
            enc_gain2_g,
            enc_shift2_g,
            enc_fc1_b,
            enc_fc2_b,
            mask_g,
            dec_gain1_g,
            dec_shift1_g,
            dec_gqkv_sum[:, :DD],
            dec_gqkv_sum[:, 2 * DD :],
            dec_proj_b,
            dec_gain2_g,
            dec_shift2_g,
            dec_fc1_b,
            dec_fc2_b,
        ]
        sizes = [v.shape[1] for v in small]
        vector = jnp.concatenate([*small, jnp.zeros((1, 14336 - sum(sizes)), F32)], axis=1)
        terms = spread(vector.reshape(112, 128), "x")
        vector = ((terms[0] + terms[1]) + (terms[2] + terms[3])).reshape(4, 56, 64)
        extra = lax.dynamic_index_in_dim(vector, x_at, 0, keepdims=False).astype(BF16)
        extra = jnp.pad(extra, ((0, width - 56), (0, 0)))

        def qkv_half(which):
            grad = low_grad(columns(first_in, which), gqkv)
            grad = [grad[:, c * 256 : c * 256 + hw] for c in range(3)]
            more = lax.dynamic_slice_in_dim(extra, which * (width // 2), width // 2, 0)
            return jnp.concatenate([*grad, more], axis=1)


        qkv_sum, vec_sum = tail_sum(*halves(qkv_half))
        back = exchange([None, *others], "x", -1)
        gx = enc_end(own_input, enc_gx1, (own_back, *back[1:]), vectors)
        return qkv_sum, vec_sum, gx

    def nothing():
        return tuple(
            jnp.zeros(dims, F32)
            for dims in ((width, 3 * width), (width, 256), (tokens, width))
        )

    rest_grads = lax.psum(early, ALL)
    qkv_grad, vector, input_grad = lax.cond(seg_ids[0, 0] >= 0, finish, nothing)
    vector = vector[:56].reshape(56, 4, 64).transpose(1, 0, 2).reshape(14336)
    sizes = [width, width, 2 * width, width, width, width, 4 * width, width, DD]
    sizes += [DD, DD, 2 * DD, DD, DD, DD, 4 * DD, DD]
    cuts = [int(c) for c in np.cumsum(sizes)]
    v = jnp.split(vector, cuts)

    dec_qkv_g, dec_proj_g, dec_fc1_g, dec_fc2_g, *rest_grads = widen(rest_grads)
    enc_proj_g, enc_fc1_g, enc_fc2_g, to_dec_g = rest_grads
    return (
        dec_out[None, None],
        input_grad[None],
        v[0],
        v[1],
        qkv_grad,
        v[2],
        enc_proj_g,
        v[3],
        v[4],
        v[5],
        enc_fc1_g,
        v[6],
        enc_fc2_g,
        v[7],
        to_dec_g,
        v[8],
        v[9],
        v[10],
        dec_qkv_g,
        v[11],
        dec_proj_g,
        v[12],
        v[13],
        v[14],
        dec_fc1_g,
        v[15],
        dec_fc2_g,
        v[16],
    )


def solution(mesh):
    fine = Mesh(mesh.devices.reshape(4, 4, 2, 4), ALL)
    row, shared, split = P(WIDE, None), P(), P("x", None)
    return jax.shard_map(
        body,
        mesh=fine,
        in_specs=(
            P(WIDE, "x", None),
            row,
            row,
            P(WIDE, "x", None),
            shared,
            shared,
            split,
            shared,
            split,
            shared,
            shared,
            shared,
            split,
            shared,
            split,
        )
        + (shared,) * 15
        + (P(WIDE, "x", None, None),),
        out_specs=(P(WIDE, "x", None, None), P(WIDE, "x", None)) + (shared,) * 26,
        check_vma=False,
    )
```

```python
import functools

import jax
import jax.numpy as jnp
import numpy as np
from jax import lax
from jax.experimental import pallas as pl
from jax.experimental.pallas import tpu as pltpu
from jax.sharding import Mesh
from jax.sharding import PartitionSpec as P

HEADS = 12
DD = 384
DHEADS = 6
VIS = 157
FULL = 1568
CAP = 64
NORM_EPS = 1e-06
NEG_LARGE = -1e30
ALL = ("z", "y", "core", "x")
WIDE = ("z", "y", "core")
F32 = jnp.float32
BF16 = jnp.bfloat16


def room(mebibytes):
    return pltpu.CompilerParams(vmem_limit_bytes=mebibytes << 20)


def shift(value, axis, step):
    return lax.ppermute(value, axis, [(i, (i + step) % 4) for i in range(4)])


def swap(value):
    return lax.ppermute(value, "core", [(0, 1), (1, 0)])


def spread(piece, axis):
    across = shift(piece, axis, 2)
    return [piece, shift(piece, axis, 1), across, shift(piece, axis, 3)]


def exchange(pieces, axis, sign=1):
    far = shift(pieces[2], axis, 2)
    return [pieces[0], shift(pieces[1], axis, sign), far, shift(pieces[3], axis, -sign)]


def reduce_phase(current, axis):
    rows = current.shape[0] // 4
    index = lax.axis_index(axis)
    got = []
    for step in (2, 1, 3):
        piece = lax.dynamic_slice_in_dim(current, ((index + step) % 4) * rows, rows, 0)
        got.append(shift(piece.astype(BF16), axis, step).astype(F32))
    own = lax.dynamic_slice_in_dim(current, index * rows, rows, 0).astype(F32)
    return own + (got[0] + got[1] + got[2])


def sum_vector(vector):
    vector = vector + swap(vector)
    for axis in ("x", "y", "z"):
        parts = spread(vector, axis)
        vector = (parts[0] + parts[1]) + (parts[2] + parts[3])
    return vector


def pick(values, index):
    low = jnp.where(index == 0, values[0], values[1])
    high = jnp.where(index == 2, values[2], values[3])
    return jnp.where(index < 2, low, high)


def place_of(axes):
    return jnp.stack([lax.axis_index(a) for a in axes]).astype(jnp.int32)


def tail_kernel(place, *refs):
    ins, out, extra = refs[:8], refs[8], refs[9]
    half = pl.program_id(0)
    low = out.shape[0] // 4
    for b in range(4):
        rows = pl.ds(b * low, low)
        parts = [jnp.where(half == 0, ins[k][rows, :], ins[4 + k][rows, :]) for k in range(4)]
        parts = [pick(parts, (place[0] + 4 - g) % 4).astype(F32) for g in range(4)]
        to = pl.multiple_of(((place[2] + 4 - b) % 4) * low, 8)
        for c in range(3):
            out[pl.ds(to, low), c * 768 : (c + 1) * 768] = jnp.concatenate(
                [part[:, c * 192 : (c + 1) * 192] for part in parts], axis=1
            )
        extra[pl.ds(to, low), :] = jnp.concatenate([part[:, 576:] for part in parts], axis=1)


def tail_sum(own_half, other_half):
    current = own_half.astype(F32) + swap(other_half).astype(F32)
    current = reduce_phase(current, "y")
    current = reduce_phase(current, "z")
    parts = spread(current.astype(BF16), "z")
    parts = spread(jnp.concatenate(parts, 0), "y")
    mine = spread(jnp.concatenate(parts, 0), "x")
    theirs = [swap(part) for part in mine]
    rows, cols = mine[0].shape
    piece = pl.BlockSpec((rows // 4, cols), lambda h, a, s: (a, 0))
    return pl.pallas_call(
        tail_kernel,
        grid_spec=pltpu.PrefetchScalarGridSpec(
            num_scalar_prefetch=1,
            grid=(2, 4),
            in_specs=[piece] * 8,
            out_specs=[
                pl.BlockSpec(
                    (rows // 4, 4 * count),
                    lambda h, a, s: (((s[3] + h) % 2) * 4 + (s[1] + 4 - a) % 4, 0),
                )
                for count in (576, 64)
            ],
        ),
        out_shape=[jax.ShapeDtypeStruct((2 * rows, 4 * count), F32) for count in (576, 64)],
        compiler_params=room(16),
    )(place_of(("x", "y", "z", "core")), *mine, *theirs)


def dot_nt(left, right):
    return lax.dot_general(left, right, (((1,), (1,)), ((), ())), preferred_element_type=F32)


def dot_nn(left, right):
    return lax.dot_general(left, right, (((1,), (0,)), ((), ())), preferred_element_type=F32)


def low_lanes(rows):
    return lax.broadcasted_iota(jnp.int32, (rows, 128), 1) < 64


def two_heads(ref, at, count):
    pair = ref[pl.ds(at, count), :]
    low, zero = low_lanes(count), jnp.zeros_like(pair)
    return jnp.concatenate([jnp.where(low, pair, zero), jnp.where(low, zero, pair)], axis=0)


def mask_scores(scores, seg_q, seg_k, at, count):
    if seg_q is None:
        return scores
    mine = seg_q[pl.ds(at, count), :]
    allowed = jnp.concatenate([mine, mine], axis=0) == seg_k[...]
    return jnp.where(allowed, scores, NEG_LARGE)


def forward_kernel(*refs, block, masked):
    if masked:
        seg_q, seg_k, q_ref, k_ref, v_ref, out_ref, lse_ref = refs
    else:
        seg_q = seg_k = None
        q_ref, k_ref, v_ref, out_ref, lse_ref = refs
    count = q_ref.shape[0] // block
    low = low_lanes(block)

    def scores_of(i):
        scores = dot_nt(two_heads(q_ref, i * block, block), k_ref[...])
        return mask_scores(scores, seg_q, seg_k, i * block, block)

    scores = scores_of(0)
    for i in range(count):
        later = scores_of(i + 1) if i + 1 < count else None
        peak = jnp.max(scores, axis=1, keepdims=True)
        probs = jnp.exp(scores - peak)
        total = jnp.sum(probs, axis=1, keepdims=True)
        out = dot_nn(probs.astype(BF16), v_ref[...]) * (1.0 / total)
        rows = pl.ds(i * block, block)
        out_ref[rows, :] = jnp.where(low, out[:block], out[block:]).astype(BF16)
        lse = peak + jnp.log(total)
        lse_ref[0, rows, :] = jnp.concatenate([lse[:block], lse[block:]], axis=1)
        scores = later


def backward_kernel(*refs, block, masked, first):
    if masked:
        seg_q, seg_k = refs[:2]
        refs = refs[2:]
    else:
        seg_q = seg_k = None
    q_ref, k_ref, v_ref, out_ref, grad_ref, lse_ref = refs[:6]
    res_ref, k_sum, v_sum = refs[6 + first :]
    length = q_ref.shape[0]
    count = length // block
    low = low_lanes(block)
    pair = pl.program_id(0)
    width = res_ref.shape[1] // 3
    at_q = pl.multiple_of(pair * 128, 128)
    at_k = pl.multiple_of(width + pair * 128, 128)
    at_v = pl.multiple_of(2 * width + pair * 128, 128)

    def front(i):
        queries = two_heads(q_ref, i * block, block)
        grads = two_heads(grad_ref, i * block, block)
        scores = mask_scores(dot_nt(queries, k_ref[...]), seg_q, seg_k, i * block, block)
        return queries, grads, scores, dot_nt(grads, v_ref[...])

    current = front(0)
    for i in range(count):
        later = front(i + 1) if i + 1 < count else None
        queries, grads, scores, probs_grad = current
        rows = pl.ds(i * block, block)
        lse = lse_ref[0, rows, :]
        lse = jnp.concatenate([lse[:, 0:1], lse[:, 1:2]], axis=0)
        inner = grad_ref[rows, :].astype(F32) * out_ref[rows, :].astype(F32)
        zero = jnp.zeros_like(inner)
        inner = jnp.concatenate(
            [
                jnp.sum(jnp.where(low, inner, zero), axis=1, keepdims=True),
                jnp.sum(jnp.where(low, zero, inner), axis=1, keepdims=True),
            ],
            axis=0,
        )
        probs = jnp.exp(scores - lse)
        score_grad = (probs * (probs_grad - inner)).astype(BF16)
        q_grad = dot_nn(score_grad, k_ref[...])
        q_grad = jnp.where(low, q_grad[:block], q_grad[block:]).astype(BF16).astype(F32)
        res_ref[rows, pl.ds(at_q, 128)] = (q_grad * 0.125).astype(BF16)
        v_part = dot_nn(grads.T, probs.astype(BF16))
        k_part = dot_nn(queries.T, score_grad)
        if i == 0:
            k_sum[...] = k_part
            v_sum[...] = v_part
        else:
            k_sum[...] += k_part
            v_sum[...] += v_part
        current = later
    res_ref[:, pl.ds(at_k, 128)] = k_sum[...].T.astype(BF16)
    res_ref[:, pl.ds(at_v, 128)] = v_sum[...].T.astype(BF16)


def attention_specs(length, width, masked):
    pairs = width // 128
    column = lambda first: pl.BlockSpec((length, 128), lambda p: (0, first + p))
    segs = [
        pl.BlockSpec((length, 1), lambda p: (0, 0)),
        pl.BlockSpec((1, length), lambda p: (0, 0)),
    ]
    qkv = [column(0), column(pairs), column(2 * pairs)]
    stat = pl.BlockSpec((1, length, 2), lambda p: (p, 0, 0))
    return pairs, column, (segs if masked else []) + qkv, stat


def attend(qkv, segs, block):
    length, width = qkv.shape[0], qkv.shape[1] // 3
    masked = len(segs) > 0
    pairs, column, ins, stat = attention_specs(length, width, masked)
    work = 2 * pairs * length * length
    return pl.pallas_call(
        functools.partial(forward_kernel, block=block, masked=masked),
        grid=(pairs,),
        in_specs=ins,
        out_specs=[column(0), stat],
        out_shape=[
            jax.ShapeDtypeStruct((length, width), BF16),
            jax.ShapeDtypeStruct((pairs, length, 2), F32),
        ],
        compiler_params=room(26),
        cost_estimate=pl.CostEstimate(
            flops=work * 64 * 16, bytes_accessed=length * width * 8, transcendentals=work
        ),
    )(*segs, qkv, qkv, qkv)


def attend_back(qkv, out, grad, lse, segs, block, first=()):
    length, width = qkv.shape[0], qkv.shape[1] // 3
    masked = len(segs) > 0
    pairs, column, ins, stat = attention_specs(length, width, masked)
    work = 2 * pairs * length * length
    return pl.pallas_call(
        functools.partial(backward_kernel, block=block, masked=masked, first=len(first)),
        grid=(pairs,),
        in_specs=ins
        + [column(0), column(0), stat]
        + [pl.BlockSpec(memory_space=pl.ANY)] * len(first),
        out_specs=pl.BlockSpec((length, 3 * width), lambda p: (0, 0)),
        out_shape=jax.ShapeDtypeStruct((length, 3 * width), BF16),
        scratch_shapes=[pltpu.VMEM((128, length), F32)] * 2,
        compiler_params=room(27),
        cost_estimate=pl.CostEstimate(
            flops=work * 64 * 40, bytes_accessed=length * width * 16, transcendentals=work
        ),
    )(*segs, qkv, qkv, qkv, out, grad, lse, *first)


def sincos_table(count_pos, count_col):
    position = np.arange(count_pos).astype(np.float32)[:, None]
    column = np.arange(count_col)
    exponent = (2 * (column // 2)).astype(np.float32) / np.float32(count_col)
    angles = position / np.power(np.float32(10000.0), exponent)[None, :]
    table = np.where(column[None, :] % 2 == 0, np.sin(angles), np.cos(angles))
    return table.astype(np.float32)


def shape(rows, cols, dtype):
    return jax.ShapeDtypeStruct((rows, cols), dtype)


def cost(flops, moved, special=0):
    return pl.CostEstimate(flops=flops, bytes_accessed=moved, transcendentals=special)


def norm_parts(values):
    average = jnp.mean(values, axis=-1, keepdims=True)
    centred = values - average
    variance = jnp.mean(centred * centred, axis=-1, keepdims=True)
    inv_std = lax.rsqrt(variance + NORM_EPS)
    return centred * inv_std, inv_std


def norm_back(gradient, normed, inv_std, gain):
    scaled = gradient * gain
    return inv_std * (
        scaled
        - jnp.mean(scaled, axis=-1, keepdims=True)
        - normed * jnp.mean(scaled * normed, axis=-1, keepdims=True)
    )


def column_sum(values):
    return jnp.sum(values, axis=0, keepdims=True)


def mm_grad(left, right):
    return jnp.einsum("sk,sn->kn", left, right, preferred_element_type=F32)


def gelu_parts(u):
    cdf = 0.5 + 0.5 * lax.erf(u * 0.7071067811865476)
    bell = jnp.exp(u * u * -0.5)
    return u * cdf, cdf + u * (bell * 0.3989422804014327)


class Vectors:
    def __init__(self, arrays):
        self.at, self.size, total = {}, {}, 0
        for name, array in arrays.items():
            self.at[name], self.size[name] = total, array.shape[0]
            total += array.shape[0]
        self.total = total
        self.row = jnp.concatenate(list(arrays.values())).astype(F32).reshape(1, total)

    def of(self, ref, name, first=0, count=None):
        at = self.at[name] + first
        return ref[:, at : at + (self.size[name] - first if count is None else count)]


def start_kernel(place, weight, inputs, fc2, proj, fc1, *outs):
    strip = outs[4]
    eighth = strip.shape[1]
    for v in range(8):

        @pl.when(place[2] == v)
        def _():
            rows = slice(v * eighth, (v + 1) * eighth)
            for b in range(4):
                strip[b] = fc2[b * 192 + rows.start : b * 192 + rows.stop, :]
                strip[5 + b] = fc1[rows, b * 768 : (b + 1) * 768]
            strip[4] = proj[rows, :]

    width = weight.shape[1] // 3
    part = width // 4
    rows = inputs.shape[0]
    for k in range(3):
        outs[1 + k][:rows, :] = inputs[...]
    for g in range(4):
        cols = []
        for c in range(3):
            cols.append(weight[:, c * width + g * part : c * width + (g + 1) * part])
            cols.append(jnp.zeros((weight.shape[0], 256 - part), BF16))
        piece = jnp.concatenate(cols, axis=1)

        @pl.when(place[0] == g)
        def _():
            outs[0][...] = piece

        half = piece.shape[0] // 2
        own = jnp.where(place[1] == 0, piece[:half], piece[half:])
        for k in range(1, 4):

            @pl.when((place[0] + k) % 4 == g)
            def _():
                outs[k][rows:, :] = own


def start(weight, inputs, fc2, proj, fc1, place):
    rows, count = weight.shape[0], inputs.shape[0]
    outs = [shape(rows, 768, BF16)] + [shape(count + rows // 2, 768, BF16)] * 3
    outs.append(jax.ShapeDtypeStruct((9, rows // 8, 768), BF16))
    whole = lambda a: pl.BlockSpec(a.shape, lambda i, s: (0,) * len(a.shape))
    return pl.pallas_call(
        start_kernel,
        grid_spec=pltpu.PrefetchScalarGridSpec(
            num_scalar_prefetch=1,
            grid=(1,),
            in_specs=[whole(a) for a in (weight, inputs, fc2, proj, fc1)],
            out_specs=[whole(a) for a in outs],
        ),
        out_shape=outs,
        compiler_params=room(56),
    )(place, weight, inputs, fc2, proj, fc1)


def enc_in_kernel(place, *refs, vectors):
    own, piece, others, swapped, vec = refs[0], refs[1], refs[2:5], refs[5], refs[6]
    qkv_ref, low_ref, weight_ref = refs[7:]
    tokens, rows = own.shape[0], piece.shape[0]
    half = rows // 2
    weight_ref[pl.ds(pl.multiple_of(place[0] * rows, 16), rows), :] = piece[...]
    for k in range(1, 4):
        to = ((place[0] + 4 - k) % 4) * rows
        mine = pl.multiple_of(to + place[1] * half, 16)
        weight_ref[pl.ds(mine, half), :] = others[k - 1][tokens:, :]
        rest = pl.multiple_of(to + (1 - place[1]) * half, 16)
        weight_ref[pl.ds(rest, half), :] = swapped[(k - 1) * half : k * half, :]
    biases = []
    for first in (0, 768):
        groups = [vectors.of(vec, "enc_qv_bias", first + g * 192, 192) for g in range(4)]
        biases += [pick(groups, place[0]), jnp.zeros((1, 64), F32)]
    bias = jnp.concatenate(biases[:2] + [jnp.zeros((1, 256), F32)] + biases[2:], axis=1)
    scale = jnp.where(lax.broadcasted_iota(jnp.int32, (1, 768), 1) < 256, 0.125, 1.0)
    gain, offset = vectors.of(vec, "enc_norm1_gain"), vectors.of(vec, "enc_norm1_shift")
    for k in range(4):
        inputs = own[...] if k == 0 else others[k - 1][:tokens, :]
        normed, _ = norm_parts(inputs.astype(F32))
        low = (normed * gain + offset).astype(BF16)
        out = pl.ds(k * tokens, tokens)
        low_ref[out, :] = low
        qkv_ref[out, :] = ((dot_nn(low, weight_ref[...]) + bias) * scale).astype(BF16)


def enc_in(own, piece, others, swapped, vectors, place):
    tokens, width = own.shape
    rows = 4 * tokens
    whole = lambda a: pl.BlockSpec(a.shape, lambda i, s: (0, 0))
    outs = [shape(rows, 768, BF16), shape(rows, width, BF16), shape(width, 768, BF16)]
    return pl.pallas_call(
        functools.partial(enc_in_kernel, vectors=vectors),
        grid_spec=pltpu.PrefetchScalarGridSpec(
            num_scalar_prefetch=1,
            grid=(1,),
            in_specs=[whole(a) for a in (own, piece, *others, swapped, vectors.row)],
            out_specs=[whole(a) for a in outs],
        ),
        out_shape=outs,
        compiler_params=room(20),
        cost_estimate=cost(2 * rows * width * 768, rows * width * 8),
    )(place, own, piece, *others, swapped, vectors.row)


MATRIX_SPECS = [
    pl.BlockSpec((1, 768, 768), lambda j, s: (4, 0, 0)),
    pl.BlockSpec((1, 768, 768), lambda j, s: (5 + j, 0, 0)),
    pl.BlockSpec((4, 192, 768), lambda j, s: (0, j, 0)),
]


def enc_block_kernel(place, *refs, vectors):
    parts, (x, proj, fc1, fc2, to_dec, send_map, vec) = refs[:4], refs[4:11]
    att_ref, x1_ref, low_ref, act_ref, slope_ref, y_ref, *sends, total = refs[11:]
    step = pl.program_id(0)

    @pl.when(step == 0)
    def _():
        groups = [part[...] for part in parts]
        att = jnp.concatenate([pick(groups, (place[0] + 4 - g) % 4) for g in range(4)], axis=1)
        att_ref[...] = att
        x1 = x[...].astype(F32) + (dot_nn(att, proj[0]) + vectors.of(vec, "enc_proj_bias"))
        x1_ref[...] = x1
        normed, _ = norm_parts(x1)
        gain, offset = vectors.of(vec, "enc_norm2_gain"), vectors.of(vec, "enc_norm2_shift")
        low_ref[...] = (normed * gain + offset).astype(BF16)
        total[...] = x1 + vectors.of(vec, "enc_fc2_bias")

    bias = pick([vectors.of(vec, "enc_fc1_bias", j * 768, 768) for j in range(4)], step)
    pre = dot_nn(low_ref[...], fc1[0]) + bias
    act, slope = gelu_parts(pre)
    act = act.astype(BF16)
    act_ref[...] = act
    slope_ref[...] = slope.astype(BF16)
    total[...] += dot_nn(act, fc2[...].reshape(768, 768))

    @pl.when(step == 3)
    def _():
        y = total[...].astype(BF16)
        y_ref[...] = y
        reduced = dot_nn(y, to_dec[...]).astype(BF16)
        send = dot_nn(send_map[...], reduced).astype(BF16)
        for k in range(4):
            sends[k][...] = send[k * CAP : (k + 1) * CAP, :]


def enc_block(parts, x, matrices, to_dec, send_map, vectors, place):
    rows, width = x.shape
    whole = lambda a: pl.BlockSpec(a.shape, lambda j, s: (0,) * len(a.shape))
    chunk = pl.BlockSpec((rows, 768), lambda j, s: (0, j))
    outs = [
        shape(rows, width, BF16),
        shape(rows, width, F32),
        shape(rows, width, BF16),
        shape(rows, 4 * width, BF16),
        shape(rows, 4 * width, BF16),
        shape(rows, width, BF16),
        *[shape(CAP, DD, BF16)] * 4,
    ]
    return pl.pallas_call(
        functools.partial(enc_block_kernel, vectors=vectors),
        grid_spec=pltpu.PrefetchScalarGridSpec(
            num_scalar_prefetch=1,
            grid=(4,),
            in_specs=[whole(a) for a in (*parts, x)]
            + MATRIX_SPECS
            + [whole(a) for a in (to_dec, send_map, vectors.row)],
            out_specs=[
                chunk if a.shape[-1] == 4 * width else whole(a) for a in outs
            ],
            scratch_shapes=[pltpu.VMEM((rows, width), F32)],
        ),
        out_shape=outs,
        compiler_params=room(18),
        cost_estimate=cost(rows * width * width * 20, width * width * 20, rows * width * 8),
    )(place, *parts, x, *[matrices] * 3, to_dec, send_map, vectors.row)


def enc_block_back_kernel(place, *refs, vectors, first):
    parts, (send_map, to_dec, x1, y, low, att) = refs[:4], refs[4:10]
    act, slope, proj, fc1, fc2, vec = refs[10:16]
    refs = refs[16 + first :]
    fc1_g, fc2_g, fc1_b, gx1_ref, proj_g, to_dec_g = refs[:6]
    gatt_refs, (fc2_b, gain_g, shift_g, proj_b) = refs[6:10], refs[10:14]
    gz, gy, back, low_turned = refs[14:]
    step = pl.program_id(0)

    @pl.when(step == 0)
    def _():
        rows = jnp.concatenate([part[...] for part in parts], axis=0)
        reduced = dot_nn(send_map[...], rows).astype(BF16)
        to_dec_g[...] = dot_nn(y[...].T, reduced).astype(BF16)
        grad = dot_nt(reduced, to_dec[...])
        gy[...] = grad
        gz[...] = grad.astype(BF16)
        fc2_b[...] = column_sum(grad.astype(BF16).astype(F32))
        back[...] = jnp.zeros_like(back)
        low_turned[...] = low[...].T

    fc2_g[...] = dot_nn(act[...].T, gz[...]).astype(BF16)
    gpre = dot_nt(gz[...], fc2[...].reshape(768, 768)) * slope[...].astype(F32)
    gpre = gpre.astype(BF16)
    fc1_b[...] = column_sum(gpre.astype(F32))
    fc1_g[...] = dot_nn(low_turned[...], gpre).astype(BF16)
    back[...] += dot_nt(gpre, fc1[0])

    @pl.when(step == 3)
    def _():
        normed, inv_std = norm_parts(x1[...])
        total = back[...]
        gain_g[...] = column_sum(total * normed)
        shift_g[...] = column_sum(total)
        gx1 = gy[...] + norm_back(total, normed, inv_std, vectors.of(vec, "enc_norm2_gain"))
        gx1_ref[...] = gx1
        go = gx1.astype(BF16)
        proj_b[...] = column_sum(go.astype(F32))
        proj_g[...] = dot_nn(att[...].T, go).astype(BF16)
        gatt = dot_nt(go, proj[0]).astype(BF16)
        groups = [gatt[:, g * 192 : (g + 1) * 192] for g in range(4)]
        for k in range(4):
            gatt_refs[k][...] = pick(groups, (place[0] + k) % 4)


def enc_block_back(
    parts, send_map, to_dec, x1, y, low, att, act, slope, matrices, vectors, place, first
):
    rows, width = x1.shape
    whole = lambda a: pl.BlockSpec(a.shape, lambda j, s: (0,) * len(a.shape))
    columns = lambda count: pl.BlockSpec((count, 768), lambda j, s: (0, j))
    rest = [
        shape(rows, width, F32),
        shape(width, width, BF16),
        shape(width, DD, BF16),
        *[shape(rows, 192, BF16)] * 4,
        *[shape(1, width, F32)] * 4,
    ]
    return pl.pallas_call(
        functools.partial(enc_block_back_kernel, vectors=vectors, first=len(first)),
        grid_spec=pltpu.PrefetchScalarGridSpec(
            num_scalar_prefetch=1,
            grid=(4,),
            in_specs=[whole(a) for a in (*parts, send_map, to_dec, x1, y, low, att)]
            + [columns(rows), columns(rows), *MATRIX_SPECS, whole(vectors.row)]
            + [pl.BlockSpec(memory_space=pl.ANY)] * len(first),
            out_specs=[
                columns(width),
                pl.BlockSpec((768, width), lambda j, s: (j, 0)),
                columns(1),
            ]
            + [whole(a) for a in rest],
            scratch_shapes=[
                pltpu.VMEM((rows, width), BF16),
                pltpu.VMEM((rows, width), F32),
                pltpu.VMEM((rows, width), F32),
                pltpu.VMEM((width, rows), BF16),
            ],
        ),
        out_shape=[
            shape(width, 4 * width, BF16),
            shape(4 * width, width, BF16),
            shape(1, 4 * width, F32),
            *rest,
        ],
        compiler_params=room(32),
        cost_estimate=cost(rows * width * width * 40, width * width * 40),
    )(
        place,
        *parts,
        send_map,
        to_dec,
        x1,
        y,
        low,
        att,
        act,
        slope,
        *[matrices] * 3,
        vectors.row,
        *first,
    )


def enc_in_back_kernel(*refs, vectors):
    inputs, (grad, weight, vec) = refs[:4], refs[4:7]
    own_ref, others, (gain_g, shift_g, grad_sum) = refs[7], refs[8:11], refs[11:]
    tokens = inputs[0].shape[0]
    gains = shifts = 0.0
    for k in range(4):
        part = dot_nt(grad[pl.ds(k * tokens, tokens), :], weight[...])
        normed, _ = norm_parts(inputs[k][:tokens, :].astype(F32))
        gains = gains + column_sum(part * normed)
        shifts = shifts + column_sum(part)
        if k == 0:
            own_ref[...] = part
        else:
            others[k - 1][...] = part.astype(BF16)
    gain_g[...] = gains
    shift_g[...] = shifts
    grad_sum[...] = column_sum(grad[...].astype(F32))


def enc_in_back(inputs, grad, weight, vectors):
    tokens, width = inputs[0].shape
    outs = [shape(tokens, width, F32)] + [shape(tokens, width, BF16)] * 3
    outs += [shape(1, width, F32)] * 2 + [shape(1, 768, F32)]
    return pl.pallas_call(
        functools.partial(enc_in_back_kernel, vectors=vectors),
        out_shape=outs,
        compiler_params=room(14),
        cost_estimate=cost(8 * tokens * width * 768, tokens * width * 32),
    )(*inputs, grad, weight, vectors.row)


def enc_end_kernel(x, gx1, own, a, b, c, vec, out, *, vectors):
    normed, inv_std = norm_parts(x[...].astype(F32))
    back = own[...] + (a[...].astype(F32) + b[...].astype(F32) + c[...].astype(F32))
    out[...] = gx1[...] + norm_back(back, normed, inv_std, vectors.of(vec, "enc_norm1_gain"))


def enc_end(x, gx1, back, vectors):
    return pl.pallas_call(
        functools.partial(enc_end_kernel, vectors=vectors),
        out_shape=shape(*x.shape, F32),
        compiler_params=room(8),
    )(x, gx1, *back, vectors.row)


def dec_in_kernel(*refs, vectors):
    parts, (restore, slots, table, weight, vec) = refs[:4], refs[4:9]
    grid_ref, low_ref, qkv_ref = refs[9:]
    rows = jnp.concatenate([part[...] for part in parts], axis=0)
    order = restore[...]
    hot = jnp.where(order == slots[...], 1.0, 0.0).astype(BF16)
    placed = dot_nn(hot, rows)
    grid = placed + jnp.where(order >= VIS, vectors.of(vec, "mask_token"), 0.0) + table[...]
    grid_ref[...] = grid
    normed, _ = norm_parts(grid)
    low = normed * vectors.of(vec, "dec_norm1_gain") + vectors.of(vec, "dec_norm1_shift")
    low = low.astype(BF16)
    low_ref[...] = low
    packed = dot_nn(low, weight[...])
    queries = packed[:, :DD] + vectors.of(vec, "dec_qv_bias", 0, DD)
    qkv_ref[:, :DD] = (queries * 0.125).astype(BF16)
    qkv_ref[:, DD : 2 * DD] = packed[:, DD : 2 * DD].astype(BF16)
    values = packed[:, 2 * DD :] + vectors.of(vec, "dec_qv_bias", DD, DD)
    qkv_ref[:, 2 * DD :] = values.astype(BF16)


def dec_in(parts, restore, slots, table, weight, vectors, tile):
    rows = table.shape[0]
    row = lambda n: pl.BlockSpec((tile, n), lambda i: (i, 0))
    whole = lambda a: pl.BlockSpec(a.shape, lambda i: (0, 0))
    return pl.pallas_call(
        functools.partial(dec_in_kernel, vectors=vectors),
        grid=(rows // tile,),
        in_specs=[whole(a) for a in parts]
        + [row(1), whole(slots), row(DD), whole(weight), whole(vectors.row)],
        out_specs=[row(DD), row(DD), row(3 * DD)],
        out_shape=[shape(rows, DD, F32), shape(rows, DD, BF16), shape(rows, 3 * DD, BF16)],
        compiler_params=room(24),
        cost_estimate=cost(rows * DD * DD * 8, rows * DD * 16),
    )(*parts, restore, slots, table, weight, vectors.row)


def dec_in_back_kernel(grad, weight, grid, gx1, restore, column, slots, vec, *outs, vectors):
    slot_refs, (gain_g, shift_g, mask_g, grad_sum, total) = outs[:4], outs[4:]
    step = pl.program_id(0)

    @pl.when(step == 0)
    def _():
        for ref in (gain_g, shift_g, mask_g, grad_sum, total):
            ref[...] = jnp.zeros_like(ref)

    back = dot_nt(grad[...], weight[...])
    normed, inv_std = norm_parts(grid[...])
    gain_g[...] += column_sum(back * normed)
    shift_g[...] += column_sum(back)
    grad_sum[...] += column_sum(grad[...].astype(F32))
    gx = gx1[...] + norm_back(back, normed, inv_std, vectors.of(vec, "dec_norm1_gain"))
    order = restore[0]
    hot = jnp.where(slots[...] == order, 1.0, 0.0).astype(BF16)
    total[...] += dot_nn(hot, gx.astype(BF16))
    mask_g[...] += column_sum(jnp.where(column[...] >= VIS, gx, 0.0))

    @pl.when(step == pl.num_programs(0) - 1)
    def _():
        for k in range(4):
            slot_refs[k][...] = total[k * CAP : (k + 1) * CAP, :].astype(BF16)


def dec_in_back(grad, weight, grid, gx1, restore, column, slots, vectors, tile):
    rows = grid.shape[0]
    row = lambda n: pl.BlockSpec((tile, n), lambda i: (i, 0))
    whole = lambda shape: pl.BlockSpec(shape, lambda i: (0, 0))
    sums = [DD, DD, DD, 3 * DD]
    return pl.pallas_call(
        functools.partial(dec_in_back_kernel, vectors=vectors),
        grid=(rows // tile,),
        in_specs=[
            row(3 * DD),
            whole(weight.shape),
            row(DD),
            row(DD),
            pl.BlockSpec((1, 1, tile), lambda i: (i, 0, 0)),
            row(1),
            whole(slots.shape),
            whole(vectors.row.shape),
        ],
        out_specs=[whole((CAP, DD))] * 4 + [whole((1, n)) for n in sums],
        out_shape=[shape(CAP, DD, BF16)] * 4 + [shape(1, n, F32) for n in sums],
        scratch_shapes=[pltpu.VMEM((4 * CAP, DD), F32)],
        compiler_params=room(16),
        cost_estimate=cost(rows * DD * DD * 8, rows * DD * 16),
    )(grad, weight, grid, gx1, restore, column, slots, vectors.row)


def dec_mid_kernel(x, att, gy, proj, fc1, fc2, vec, *outs, vectors, chunk):
    y_ref, gx1_ref, go_ref, gatt_ref, fc1_g, fc2_g = outs[:6]
    (fc1_b, fc2_b, gain_g, shift_g, proj_b), (act_ref, slope, fc1_sum, fc2_sum) = (
        outs[6:11],
        outs[11:],
    )
    step = pl.program_id(0)

    @pl.when(step == 0)
    def _():
        for ref in (fc1_b, fc2_b, gain_g, shift_g, proj_b, fc1_sum, fc2_sum):
            ref[...] = jnp.zeros_like(ref)

    hidden = fc1.shape[1]
    gain = vectors.of(vec, "dec_norm2_gain")
    x1 = x[...] + (dot_nn(att[...], proj[...]) + vectors.of(vec, "dec_proj_bias"))
    normed, inv_std = norm_parts(x1)
    low = (normed * gain + vectors.of(vec, "dec_norm2_shift")).astype(BF16)
    total = x1 + vectors.of(vec, "dec_fc2_bias")

    def pre_of(c):
        return dot_nn(low, fc1[:, c : c + chunk]) + vectors.of(vec, "dec_fc1_bias", c, chunk)

    pre = pre_of(0)
    for c in range(0, hidden, chunk):
        later = pre_of(c + chunk) if c + chunk < hidden else None
        act, rise = gelu_parts(pre)
        act = act.astype(BF16)
        act_ref[:, c : c + chunk] = act
        slope[:, c : c + chunk] = rise.astype(BF16)
        total = total + dot_nn(act, fc2[c : c + chunk, :])
        pre = later
    y_ref[...] = total.astype(BF16)

    gz = gy[...]
    gz_turned = gz.T
    low_turned = low.T
    fc2_b[...] += column_sum(gz.astype(F32))
    grad = dot_nt(gz, fc2[:chunk, :])
    back = None
    for c in range(0, hidden, chunk):
        later = None
        if c + chunk < hidden:
            later = dot_nt(gz, fc2[c + chunk : c + 2 * chunk, :])
        fc2_sum[:, c : c + chunk] += dot_nn(gz_turned, act_ref[:, c : c + chunk])
        gpre = (grad * slope[:, c : c + chunk].astype(F32)).astype(BF16)
        fc1_b[:, c : c + chunk] += column_sum(gpre.astype(F32))
        fc1_sum[:, c : c + chunk] += dot_nn(low_turned, gpre)
        part = dot_nt(gpre, fc1[:, c : c + chunk])
        back = part if back is None else back + part
        grad = later
    gain_g[...] += column_sum(back * normed)
    shift_g[...] += column_sum(back)
    gx1 = gz.astype(F32) + norm_back(back, normed, inv_std, gain)
    gx1_ref[...] = gx1
    go = gx1.astype(BF16)
    go_ref[...] = go
    proj_b[...] += column_sum(go.astype(F32))
    gatt_ref[...] = dot_nt(go, proj[...]).astype(BF16)

    @pl.when(step == pl.num_programs(0) - 1)
    def _():
        fc1_g[...] = fc1_sum[...].astype(BF16)
        for c in range(0, hidden, chunk):
            fc2_g[c : c + chunk, :] = fc2_sum[:, c : c + chunk].T.astype(BF16)


def dec_mid(x, att, gy, proj, fc1, fc2, vectors, tile, chunk):
    rows, width = x.shape
    hidden = fc1.shape[1]
    row = lambda n: pl.BlockSpec((tile, n), lambda i: (i, 0))
    whole = lambda shape: pl.BlockSpec(shape, lambda i: (0, 0))
    consts = (proj, fc1, fc2, vectors.row)
    shapes = [(width, BF16), (width, F32), (width, BF16), (width, BF16)]
    fixed = [shape(width, hidden, BF16), shape(hidden, width, BF16)]
    fixed += [shape(1, n, F32) for n in (hidden, width, width, width, width)]
    return pl.pallas_call(
        functools.partial(dec_mid_kernel, vectors=vectors, chunk=chunk),
        grid=(rows // tile,),
        in_specs=[row(width)] * 3 + [whole(a.shape) for a in consts],
        out_specs=[row(n) for n, _ in shapes] + [whole(a.shape) for a in fixed],
        out_shape=[shape(rows, n, t) for n, t in shapes] + fixed,
        scratch_shapes=[pltpu.VMEM((tile, hidden), BF16)] * 2
        + [pltpu.VMEM((width, hidden), F32)] * 2,
        compiler_params=room(42),
        cost_estimate=cost(rows * hidden * width * 28, rows * width * 20, rows * hidden * 2),
    )(x, att, gy, *consts)


def widen_kernel(*refs):
    count = len(refs) // 2
    for k in range(count):
        refs[count + k][...] = refs[k][...].astype(F32)


def widen(arrays):
    piece = lambda a: pl.BlockSpec((a.shape[0] // 8, a.shape[1]), lambda i: (i, 0))
    return pl.pallas_call(
        widen_kernel,
        grid=(8,),
        in_specs=[piece(a) for a in arrays],
        out_specs=[piece(a) for a in arrays],
        out_shape=[shape(*a.shape, F32) for a in arrays],
        compiler_params=room(56),
        cost_estimate=cost(0, sum(a.shape[0] * a.shape[1] * 6 for a in arrays)),
    )(*arrays)


def body(
    encoder_input,
    seg_ids,
    vis_slot,
    restore_order,
    enc_norm1_gain,
    enc_norm1_shift,
    enc_qkv_weight,
    enc_qv_bias,
    enc_proj_weight,
    enc_proj_bias,
    enc_norm2_gain,
    enc_norm2_shift,
    enc_fc1_weight,
    enc_fc1_bias,
    enc_fc2_weight,
    enc_fc2_bias,
    to_dec_weight,
    mask_token,
    dec_norm1_gain,
    dec_norm1_shift,
    dec_qkv_weight,
    dec_qv_bias,
    dec_proj_weight,
    dec_proj_bias,
    dec_norm2_gain,
    dec_norm2_shift,
    dec_fc1_weight,
    dec_fc1_bias,
    dec_fc2_weight,
    dec_fc2_bias,
    out_grad,
):
    x_at = lax.axis_index("x")
    core = lax.axis_index("core")
    place = jnp.stack([x_at, core, core * 4 + lax.axis_index("y")]).astype(jnp.int32)
    tokens, width = encoder_input.shape[1:]
    hw = width // 4
    vectors = Vectors(
        {
            "enc_norm1_gain": enc_norm1_gain,
            "enc_norm1_shift": enc_norm1_shift,
            "enc_qv_bias": enc_qv_bias,
            "enc_proj_bias": enc_proj_bias,
            "enc_norm2_gain": enc_norm2_gain,
            "enc_norm2_shift": enc_norm2_shift,
            "enc_fc1_bias": enc_fc1_bias,
            "enc_fc2_bias": enc_fc2_bias,
            "mask_token": mask_token,
            "dec_norm1_gain": dec_norm1_gain,
            "dec_norm1_shift": dec_norm1_shift,
            "dec_qv_bias": dec_qv_bias,
            "dec_proj_bias": dec_proj_bias,
            "dec_norm2_gain": dec_norm2_gain,
            "dec_norm2_shift": dec_norm2_shift,
            "dec_fc1_bias": dec_fc1_bias,
            "dec_fc2_bias": dec_fc2_bias,
        }
    )

    own_input = encoder_input[0]
    *pieces, strip = start(
        enc_qkv_weight, own_input, enc_fc2_weight, enc_proj_weight, enc_fc1_weight, place
    )
    piece, *others = exchange(pieces, "x")
    swapped = swap(jnp.concatenate([other[tokens:] for other in others], axis=0))
    inputs = [own_input, *others]

    matrices = lax.all_gather(strip, ("x", "core", "y"), axis=1, tiled=True)

    row_seg = seg_ids[0].reshape(4, tokens)
    row_slot = vis_slot[0].reshape(4, tokens)
    position = jnp.arange(tokens)
    earlier = position[None, :] < position[:, None]
    same_clip = row_seg[:, :, None] == row_seg[:, None, :]
    ranks = jnp.sum(jnp.logical_and(same_clip, earlier), axis=-1)
    turn = (x_at - jnp.arange(4)) % 4
    seg_turned = jnp.take(row_seg, turn, axis=0)
    segs = (seg_turned.reshape(4 * tokens, 1), seg_turned.reshape(1, 4 * tokens))
    own_seg = lax.dynamic_index_in_dim(row_seg, x_at, 0, keepdims=False)
    own_rank = lax.dynamic_index_in_dim(ranks, x_at, 0, keepdims=False)
    cap_index = jnp.arange(4 * CAP)
    clip_to = (x_at + cap_index // CAP) % 4
    send_map = jnp.logical_and(
        own_seg[None, :] == clip_to[:, None],
        own_rank[None, :] == (cap_index % CAP)[:, None],
    ).astype(BF16)
    send_back = jnp.logical_and(
        own_seg[:, None] == clip_to[None, :],
        own_rank[:, None] == (cap_index % CAP)[None, :],
    ).astype(BF16)
    chosen = jnp.logical_and(
        seg_turned[:, None, :] == x_at,
        jnp.take(ranks, turn, axis=0)[:, None, :] == jnp.arange(CAP)[None, :, None],
    )
    slot_turned = jnp.take(row_slot, turn, axis=0)
    slot_vis = jnp.sum(jnp.where(chosen, slot_turned[:, None, :] + 1, 0), axis=-1) - 1
    restore_row = restore_order[0, 0]
    restore_col = restore_row[:, None]
    restore_row = restore_row.reshape(2, 1, FULL // 2)
    table = jnp.asarray(sincos_table(FULL, DD))

    qkv, first_in, qkv_mine = enc_in(own_input, piece, others, swapped, vectors, place)
    att_mine, enc_lse = attend(qkv, segs, 128)
    blocks = att_mine.reshape(4, tokens, 256)
    parts = exchange([blocks[(4 - k) % 4, :, :hw] for k in range(4)], "x")
    attended, enc_x1, second_in, enc_act, enc_slope, enc_low, *sends = enc_block(
        parts, own_input, matrices, to_dec_weight, send_map, vectors, place
    )

    received = exchange(sends, "x")
    grid, dec_in_low, dec_qkv = dec_in(
        received,
        restore_col,
        slot_vis.reshape(1, 4 * CAP),
        table,
        dec_qkv_weight,
        vectors,
        FULL // 2,
    )
    dec_att, dec_lse = attend(dec_qkv, (), 224)

    dec_gz = out_grad[0, 0]
    dec_out, dec_gx1, dec_go, dec_gatt, dec_fc1_g, dec_fc2_g, *dec_sums = dec_mid(
        grid,
        dec_att,
        dec_gz,
        dec_proj_weight,
        dec_fc1_weight,
        dec_fc2_weight,
        vectors,
        FULL // 2,
        512,
    )
    dec_fc1_b, dec_fc2_b, dec_gain2_g, dec_shift2_g, dec_proj_b = dec_sums
    dec_gqkv = attend_back(dec_qkv, dec_att, dec_gatt, dec_lse, (), 112)
    *slot_grads, dec_gain1_g, dec_shift1_g, mask_g, dec_gqkv_sum = dec_in_back(
        dec_gqkv,
        dec_qkv_weight,
        grid,
        dec_gx1,
        restore_row,
        restore_col,
        slot_vis.reshape(4 * CAP, 1),
        vectors,
        FULL // 2,
    )
    slot_grads, dec_in_low, dec_att = lax.optimization_barrier((slot_grads, dec_in_low, dec_att))
    low_grad = lambda left, right: mm_grad(left, right).astype(BF16)
    dec_early = (low_grad(dec_in_low, dec_gqkv), low_grad(dec_att, dec_go), dec_fc1_g, dec_fc2_g)

    returned = exchange(slot_grads, "x", -1)
    enc_fc1_g, enc_fc2_g, enc_fc1_b, enc_gx1, enc_proj_g, to_dec_g, *rest = enc_block_back(
        returned,
        send_back,
        to_dec_weight,
        enc_x1,
        enc_low,
        second_in,
        attended,
        enc_act,
        enc_slope,
        matrices,
        vectors,
        place,
        dec_early[:2],
    )
    gatt_parts, (enc_fc2_b, enc_gain2_g, enc_shift2_g, enc_proj_b) = rest[:4], rest[4:]
    columns = lambda array, which: lax.dynamic_slice_in_dim(
        array, which * (array.shape[1] // 2), array.shape[1] // 2, 1
    )

    def halves(make):
        return make(core), make(1 - core)

    early = (*dec_early, enc_proj_g, enc_fc1_g, enc_fc2_g, to_dec_g)
    gatt_mine = jnp.concatenate(exchange(gatt_parts, "x"), axis=0)
    gatt_mine = jnp.pad(gatt_mine, ((0, 0), (0, 64)))
    def finish():
        gqkv = attend_back(qkv, att_mine, gatt_mine, enc_lse, segs, 128, early)
        own_back, *others, gain1_g, shift1_g, gqkv_sum = enc_in_back(
            inputs, gqkv, qkv_mine, vectors
        )

        qv = jnp.zeros((2, 4, hw), F32)
        qv = lax.dynamic_update_index_in_dim(
            qv, jnp.stack([gqkv_sum[0, :hw], gqkv_sum[0, 512 : 512 + hw]]), x_at, 1
        )
        small = [
            gain1_g,
            shift1_g,
            qv.reshape(1, 2 * width),
            enc_proj_b,
            enc_gain2_g,
            enc_shift2_g,
            enc_fc1_b,
            enc_fc2_b,
            mask_g,
            dec_gain1_g,
            dec_shift1_g,
            dec_gqkv_sum[:, :DD],
            dec_gqkv_sum[:, 2 * DD :],
            dec_proj_b,
            dec_gain2_g,
            dec_shift2_g,
            dec_fc1_b,
            dec_fc2_b,
        ]
        sizes = [v.shape[1] for v in small]
        vector = jnp.concatenate([*small, jnp.zeros((1, 14336 - sum(sizes)), F32)], axis=1)
        terms = spread(vector.reshape(112, 128), "x")
        vector = ((terms[0] + terms[1]) + (terms[2] + terms[3])).reshape(4, 56, 64)
        extra = lax.dynamic_index_in_dim(vector, x_at, 0, keepdims=False).astype(BF16)
        extra = jnp.pad(extra, ((0, width - 56), (0, 0)))

        def qkv_half(which):
            grad = low_grad(columns(first_in, which), gqkv)
            grad = [grad[:, c * 256 : c * 256 + hw] for c in range(3)]
            more = lax.dynamic_slice_in_dim(extra, which * (width // 2), width // 2, 0)
            return jnp.concatenate([*grad, more], axis=1)


        qkv_sum, vec_sum = tail_sum(*halves(qkv_half))
        back = exchange([None, *others], "x", -1)
        gx = enc_end(own_input, enc_gx1, (own_back, *back[1:]), vectors)
        return qkv_sum, vec_sum, gx

    def nothing():
        return tuple(
            jnp.zeros(dims, F32)
            for dims in ((width, 3 * width), (width, 256), (tokens, width))
        )

    rest_grads = lax.psum(early, ALL)
    qkv_grad, vector, input_grad = lax.cond(seg_ids[0, 0] >= 0, finish, nothing)
    vector = vector[:56].reshape(56, 4, 64).transpose(1, 0, 2).reshape(14336)
    sizes = [width, width, 2 * width, width, width, width, 4 * width, width, DD]
    sizes += [DD, DD, 2 * DD, DD, DD, DD, 4 * DD, DD]
    cuts = [int(c) for c in np.cumsum(sizes)]
    v = jnp.split(vector, cuts)

    dec_qkv_g, dec_proj_g, dec_fc1_g, dec_fc2_g, *rest_grads = widen(rest_grads)
    enc_proj_g, enc_fc1_g, enc_fc2_g, to_dec_g = rest_grads
    return (
        dec_out[None, None],
        input_grad[None],
        v[0],
        v[1],
        qkv_grad,
        v[2],
        enc_proj_g,
        v[3],
        v[4],
        v[5],
        enc_fc1_g,
        v[6],
        enc_fc2_g,
        v[7],
        to_dec_g,
        v[8],
        v[9],
        v[10],
        dec_qkv_g,
        v[11],
        dec_proj_g,
        v[12],
        v[13],
        v[14],
        dec_fc1_g,
        v[15],
        dec_fc2_g,
        v[16],
    )


def solution(mesh):
    fine = Mesh(mesh.devices.reshape(4, 4, 2, 4), ALL)
    row, shared, split = P(WIDE, None), P(), P("x", None)
    return jax.shard_map(
        body,
        mesh=fine,
        in_specs=(
            P(WIDE, "x", None),
            row,
            row,
            P(WIDE, "x", None),
            shared,
            shared,
            split,
            shared,
            split,
            shared,
            shared,
            shared,
            split,
            shared,
            split,
        )
        + (shared,) * 15
        + (P(WIDE, "x", None, None),),
        out_specs=(P(WIDE, "x", None, None), P(WIDE, "x", None)) + (shared,) * 26,
        check_vma=False,
    )
```
